512 devices in a mesh: ctx: 8 (over x, core), tab: 64 (over z, y).
Axes of the slice: x: 4, y: 4, z: 16, core: 2. Of those that a mesh axis runs over, the one named last changes fastest.
Arguments:
- item_owner: int32 [64, 1024, 1], P('tab', 'ctx'), may hold values from 0 to 63; in each aligned block of 128 rows (0 to 127, 128 to 255, ..., all dimensions but the last counted through in order) at most 4 rows name the same one
- item_row: int32 [64, 1024], P('tab', 'ctx'), may hold values from 0 to 63
- action_id: int32 [64, 1024], P('tab', 'ctx'), may hold values from 0 to 7
- history_len: int32 [64, 4], P('tab'), may hold values from 1 to 512, 1024 in all within a row
- masters: float32 [4096, 1024], P('tab'), may hold values from -6 to 6
- row_accum: float32 [4096], P('tab'), may hold values from 0.05 to 1
- action_table: float32 [8, 1024], replicated, may hold values from -3 to 3
- norm_gain: float32 [1024], replicated, may hold values from 0.1 to 1.9
- w_qkv: bfloat16 [1024, 1536], replicated, may hold values from -0.1875 to 0.1875
- d_attended: bfloat16 [64, 1024, 512], P('tab', 'ctx'), may hold values from -6 to 6
Outputs:
- attended: bfloat16 [64, 1024, 512], P('tab', 'ctx')
- row_grads: float32 [4096, 1024], P('tab')
- new_masters: float32 [4096, 1024], P('tab')
- new_accum: float32 [4096], P('tab')
The draws below stay inside these ranges and needn't reach their ends.
Inputs may be any that keep to these rules, and one draw needn't show every extreme that they name: `item_owner`: among the 128 events of one device (aligned blocks of 128 events of a pack) at most 4 name the same shard, a bound that some block reaches. `history_len`: the 4 lengths of a pack sum to 1024; the longest is 512.
All inputs are finite; a program needn't handle non-finite values.
Results may differ from the reference program's by a relative error of at most 0.018.
Values may be sent and summed in bfloat16 or wider, within the bound.
A program may use at most 64 MiB of HBM per device.

```python
import math
import jax
import jax.numpy as jnp
import numpy as np
from jax import lax

D = 1024
HEADS = 4
HEAD = 128
ACTIONS = 8
USERS = 4
E_DEV = 128
R_DEV = 64
ATTN = 512
EVENTS = 1024
TABLE_ROWS = 4096
OWNERS = 64
CAP = 4
N_TAB = 64


def set_ends(values, own_key, smallest, largest):
    longest = values.shape.index(max(values.shape))
    spots = []
    for shift in (0, 1):
        where = [jax.random.randint(jax.random.fold_in(own_key, axis), (), 0, length) for axis, length in enumerate(values.shape)]
        where[longest] = (where[longest] + shift) % values.shape[longest]
        spots.append(tuple(where))
    return values.at[spots[0]].set(smallest).at[spots[1]].set(largest)


def levels(rng, shape, cuts, least, top_value):
    factor_of, own = 1.0, jax.random.fold_in(rng, 6)
    for axis_at, shards_of in cuts:
        draws = jnp.exp(jax.random.uniform(jax.random.fold_in(own, axis_at), (shards_of,), jnp.float32, least / len(cuts), top_value / len(cuts)))
        factor_of = factor_of * jnp.repeat(draws, shape[axis_at] // shards_of).reshape([-1 if axis == axis_at else 1 for axis in range(len(shape))])
    return factor_of


def rank_table(amount, lean):
    portions = [(1 << 20) // math.isqrt(standing ** lean) + 1 for standing in range(1, amount + 1)]
    spread = 1 + sum(portions) // (1 << 30)
    return np.cumsum(np.array([max(1, weight // spread) for weight in portions]))


def skewed_ids(rng, extent, count, skew):
    grid = rank_table(count, skew)
    pick = jax.random.randint(jax.random.fold_in(rng, 1), extent, 0, int(grid[count - 1]))
    grade = jnp.searchsorted(jnp.asarray(grid, jnp.int32), pick, side="right")
    return jax.random.permutation(jax.random.fold_in(rng, 2), count)[grade].astype(jnp.int32)


def split_up(amount, total, most, skew):
    weights = [(1 << 20) // math.isqrt(standing ** skew) + 1 for standing in range(2, amount + 1)]
    rest, holding = total - most - (amount - 1), [1] * (amount - 1)
    while rest > 0:
        free = [i for i in range(amount - 1) if holding[i] < most]
        mass, left = sum([weights[i] for i in free]), rest
        for i in free:
            more = min(most - holding[i], max(1, left * weights[i] // mass), rest)
            holding[i] = holding[i] + more
            rest = rest - more
    return np.array([most] + holding)


def uneven_parts(key, amount, total, limit, skew):
    if amount == 2:
        one = jax.random.randint(key, (), max(1, total - limit), min(limit, total - 1) + 1)
        return jnp.stack([one, total - one])
    sizes = jnp.asarray(split_up(amount, total, limit, skew), jnp.int32)
    twos = (amount - 1) // 2
    giver, receiver = sizes[1:1 + 2 * twos:2], sizes[2:2 + 2 * twos:2]
    room = jnp.minimum(giver - 1, limit - receiver)
    moved = jax.random.randint(jax.random.fold_in(key, 1), (twos,), 0, 1 << 20) % (room + 1)
    sizes = sizes.at[1:1 + 2 * twos:2].set(giver - moved).at[2:2 + 2 * twos:2].set(receiver + moved)
    return sizes[jax.random.permutation(jax.random.fold_in(key, 2), amount)]


def routed_block(stream_key, own, number, rows, amount, top, most, slope):
    order = jax.random.permutation(stream_key, amount)
    crowded, ordinary = shares(amount, rows * top, most, slope, True), shares(amount, rows * top, most, slope, False)
    places = jnp.arange(amount)

    def named(tallies, offset_by):
        used = int((tallies > 0).sum())
        fixed = max(1, used // 4)
        shifted = fixed + (places - fixed + offset_by * (used - fixed)) % max(1, amount - fixed)
        return jnp.zeros((amount,), jnp.int32).at[order[jnp.where(places < fixed, places, shifted)]].set(jnp.asarray(tallies, jnp.int32))

    tallies = jnp.where(number % 4 == 0, named(crowded, number // 4), named(ordinary, number - number // 4 - 1))
    mixed = jax.random.permutation(jax.random.fold_in(own, 3), amount)
    donor, sink = mixed[0:amount // 2 * 2:2], mixed[1:amount // 2 * 2:2]
    margin = jnp.minimum(tallies[donor] - 1, most - tallies[sink]) // 2
    margin = jnp.where((donor == order[0]) | (sink == order[0]) | (tallies[sink] == 0), 0, jnp.maximum(margin, 0))
    shifted = jax.random.randint(jax.random.fold_in(own, 4), (amount // 2,), 0, 1 << 20) % (margin + 1)
    tallies = tallies.at[donor].add(-shifted).at[sink].add(shifted)
    labels = jnp.searchsorted(jnp.cumsum(tallies), jnp.arange(rows * top), side="right").astype(jnp.int32)
    table = labels.reshape(top, rows).T
    table = table[jax.random.permutation(jax.random.fold_in(own, 1), rows)]
    offset_by = jax.random.randint(jax.random.fold_in(own, 2), (rows, 1), 0, top)
    return jnp.take_along_axis(table, (jnp.arange(top)[None, :] + offset_by) % top, axis=1)


def shares(count, total, reach, lean, full):
    weights = [(1 << 20) // math.isqrt(standing ** lean) + 1 for standing in range(1, count + 1)]
    largest = reach if full else min(reach, max(-(-total // count), total * weights[0] // sum(weights)))
    least = 1 if total - largest >= count - 1 else 0
    holding, surplus = [largest] + [least] * (count - 1), total - largest - least * (count - 1)
    while surplus > 0:
        candidates = [i for i in range(1, count) if holding[i] < largest] or [i for i in range(1, count) if holding[i] < reach]
        whole, remaining = sum([weights[i] for i in candidates]), surplus
        for i in candidates:
            extra = min(reach - holding[i], max(1, remaining * weights[i] // whole), surplus)
            holding[i] = holding[i] + extra
            surplus = surplus - extra
    return np.array(holding)


def scatter_about(own_key, dims, spread, limit, shards=(), kind=jnp.bfloat16):
    result = spread * jax.random.normal(own_key, dims, jnp.float32)
    if shards:
        result = result * levels(own_key, dims, shards, -0.22, 0.18)
    return jnp.clip(result, -limit, limit).astype(kind)


def setup_inputs(seed: int = 0) -> dict:
    key_list = jax.random.split(jax.random.key(seed), 11)
    item_owner_keys = jax.random.split(jax.random.fold_in(key_list[0], 1), N_TAB * EVENTS // E_DEV)
    item_owner_turns = jax.random.permutation(jax.random.fold_in(key_list[0], 3), N_TAB * EVENTS // E_DEV)
    item_owner = jax.vmap(lambda own, number: routed_block(jax.random.fold_in(key_list[0], 2), own, number, E_DEV, OWNERS, 1, CAP, 2))(item_owner_keys, item_owner_turns).reshape((N_TAB, EVENTS, 1))
    item_row = set_ends(skewed_ids(key_list[1], (N_TAB, EVENTS), R_DEV, 2), jax.random.fold_in(key_list[1], 3), 0, R_DEV - 1).astype(jnp.int32)
    action_id = set_ends(jax.random.randint(key_list[2], (N_TAB, EVENTS), 0, ACTIONS), jax.random.fold_in(key_list[2], 1), 0, ACTIONS - 1).astype(jnp.int32)
    history_len = jax.vmap(lambda own: uneven_parts(own, USERS, EVENTS, EVENTS // 2, 2))(jax.random.split(key_list[3], N_TAB)).reshape((N_TAB, USERS)).astype(jnp.int32)
    masters = scatter_about(key_list[4], (TABLE_ROWS, D), 1.0, 6.0, ((0, 64),), jnp.float32)
    row_accum = jnp.clip(jnp.exp(math.log(1.0) - 2.9957323 * jax.random.uniform(key_list[5], (TABLE_ROWS,), jnp.float32) ** levels(key_list[5], (TABLE_ROWS,), ((0, 64),), -0.2, 0.2)), 0.05, 1.0)
    action_table = scatter_about(key_list[6], (ACTIONS, D), 0.5, 3.0, (), jnp.float32)
    norm_gain = jnp.clip(1.0 + 0.18 * jax.random.normal(key_list[7], (D,), jnp.float32), 0.1, 1.9)
    w_qkv = scatter_about(key_list[8], (D, 3 * ATTN), D ** -0.5, 0.1875)
    d_attended = scatter_about(key_list[9], (N_TAB, EVENTS, ATTN), 1.0, 6.0, ((0, 64), (1, 8)))
    return dict(item_owner=item_owner, item_row=item_row, action_id=action_id, history_len=history_len, masters=masters, row_accum=row_accum, action_table=action_table, norm_gain=norm_gain, w_qkv=w_qkv, d_attended=d_attended)


NORM_EPS = 1e-05
LEARN_RATE = 0.1

def silu_grad(argument):
    sigmoid_value = jax.nn.sigmoid(argument)
    return sigmoid_value * (1.0 + argument * (1.0 - sigmoid_value))

def segments_of(positions, user_ends):
    return lax.optimization_barrier(jnp.sum((positions[:, None] >= user_ends[None, :]).astype(jnp.int32), axis=1)).astype(jnp.int32)

def length_of(segment, lengths):
    choose = segment[:, None] == jnp.arange(lengths.shape[0], dtype=jnp.int32)[None, :]
    return lax.optimization_barrier(jnp.sum(jnp.where(choose, lengths[None, :], 0), axis=1)).astype(jnp.float32)

def reference(item_owner, item_row, action_id, history_len, masters, row_accum, action_table, norm_gain, w_qkv, d_attended):
    item = (item_owner[..., 0] * R_DEV + item_row).astype(jnp.int32)
    fetched = masters[item].astype(jnp.bfloat16)
    fetched = lax.optimization_barrier(fetched).astype(jnp.float32)
    inputs_all = fetched + action_table[action_id]
    score_scale = 1.0 / math.sqrt(HEAD)

    def one_pack(pack_inputs):
        inputs, lengths, grad_low = pack_inputs
        centre = inputs - lax.optimization_barrier(jnp.mean(inputs, axis=1, keepdims=True))
        inv_std = lax.rsqrt(lax.optimization_barrier(jnp.mean(centre * centre, axis=1, keepdims=True)) + NORM_EPS)
        normed = centre * inv_std
        hnorm = (normed * norm_gain[None, :]).astype(jnp.bfloat16)
        project = jnp.dot(hnorm, w_qkv, preferred_element_type=jnp.float32)
        activated = jax.nn.silu(project).astype(jnp.bfloat16)
        activated = lax.optimization_barrier(activated).astype(jnp.float32)
        queries = activated[:, :ATTN].reshape(EVENTS, HEADS, HEAD)
        key_part = activated[:, ATTN:2 * ATTN].reshape(EVENTS, HEADS, HEAD)
        values = activated[:, 2 * ATTN:].reshape(EVENTS, HEADS, HEAD)
        positions = jnp.arange(EVENTS, dtype=jnp.int32)
        user_ends = jnp.cumsum(lengths).astype(jnp.int32)
        segment = segments_of(positions, user_ends)
        query_len = length_of(segment, lengths)
        allowed = (segment[:, None] == segment[None, :]) & (positions[None, :] <= positions[:, None])
        raw_scores = jnp.einsum('qhd,khd->hqk', queries, key_part) * score_scale
        weights = jnp.where(allowed[None], jax.nn.silu(raw_scores) / query_len[None, :, None], 0.0).astype(jnp.bfloat16)
        weights = lax.optimization_barrier(weights).astype(jnp.float32)
        attended = jnp.einsum('hqk,khd->qhd', weights, values).reshape(EVENTS, ATTN).astype(jnp.bfloat16)
        grad_out = grad_low.astype(jnp.float32).reshape(EVENTS, HEADS, HEAD)
        grad_weights = jnp.einsum('qhd,khd->hqk', grad_out, values)
        grad_raw = jnp.where(allowed[None], grad_weights * silu_grad(raw_scores) * score_scale / query_len[None, :, None], 0.0).astype(jnp.bfloat16)
        grad_raw = lax.optimization_barrier(grad_raw).astype(jnp.float32)
        grad_query = jnp.einsum('hqk,khd->qhd', grad_raw, key_part).reshape(EVENTS, ATTN)
        grad_key = jnp.einsum('hqk,qhd->khd', grad_raw, queries).reshape(EVENTS, ATTN)
        grad_value = jnp.einsum('hqk,qhd->khd', weights, grad_out).reshape(EVENTS, ATTN)
        grad_qkv = jnp.concatenate([grad_query, grad_key, grad_value], axis=1)
        grad_project = (grad_qkv * silu_grad(project)).astype(jnp.bfloat16)
        grad_hnorm = lax.dot_general(grad_project, w_qkv, (((1,), (1,)), ((), ())), preferred_element_type=jnp.float32)
        grad_hat = grad_hnorm * norm_gain[None, :]
        event_grad = inv_std * (grad_hat - lax.optimization_barrier(jnp.mean(grad_hat, axis=1, keepdims=True)) - normed * lax.optimization_barrier(jnp.mean(grad_hat * normed, axis=1, keepdims=True)))
        return (attended, event_grad)
    attended, event_grad = lax.map(one_pack, (inputs_all, history_len, d_attended))
    row_grads = jnp.zeros((TABLE_ROWS, D), jnp.float32).at[item.reshape(-1)].add(event_grad.reshape(-1, D))
    new_accum = row_accum + lax.optimization_barrier(jnp.mean(row_grads * row_grads, axis=1))
    new_masters = masters - LEARN_RATE * row_grads * lax.rsqrt(new_accum)[:, None]
    return (attended, row_grads, new_masters, new_accum)
```

```python
import functools
import math

import jax
import jax.numpy as jnp
from jax import lax
from jax.experimental import pallas as pl
from jax.experimental.pallas import tpu as pltpu
from jax.sharding import PartitionSpec as P

MESH = pl.DeviceIdType.MESH
F32 = jnp.float32
BF16 = jnp.bfloat16
I32 = jnp.int32

NORM_EPS = 1e-05
LEARN_RATE = 0.1

CTX = 8
Y = 4
B = 128
ROWS = 64
PLANE = Y * ROWS
MODEL = 1024
HEADS = 4
CHUNKS = 2
PIECE = PLANE // CHUNKS
SPLIT = 3
REACH = 5
SCALE = 1.0 / math.sqrt(B)
FAR_FIRST = (4, 3, 5, 2, 6, 1, 7)

NT = (((1,), (1,)), ((), ()))
TN = (((0,), (0,)), ((), ()))


def dot(a, b, dims=(((1,), (0,)), ((), ()))):
    return lax.dot_general(a, b, dims, preferred_element_type=F32)


def kernel(
    planes,
    item_ref, act_ref, hist_ref, masters_ref, accum_ref, atab_ref, gain_ref, w_ref, dout_ref,
    att_out, rg_out, nm_out, na_out,
    mslice, mfull, w_v, tbl, ids, itemb, gacc, g1, x1, xin, hn, startb, invb,
    pd, stq, stkv, qb, kvb, dob, attacc, dqacc, dqs, dkvs, atts, rdq, rdkv, ratt, dqf, gh,
    g2, gin, sb, rb, own, yb, fin,
    loc_s, y_s, y_r, z_s, z_r, id_s, id_r, a1_s, a1_r, q_s, q_r, kv_s, kv_r, do_s, do_r,
    dq_s, dq_r, dkv_s, dkv_r, at_s, at_r, a2_s, a2_r, rs_s, rs_r, ry_s, ry_r, f_s, f_r,
):
    half = planes // 2
    c = lax.axis_index("ctx")
    t = lax.axis_index("tab")
    x, core = lax.div(c, 2), lax.rem(c, 2)
    z, y = lax.div(t, Y), lax.rem(t, Y)

    def ctx_at(d):
        return lax.rem(c + d, CTX)

    def tab_y(d):
        return z * Y + lax.rem(y + d + Y, Y)

    def z_at(d):
        return lax.rem(z + d + 2 * planes, planes)

    def tab_z(d):
        return z_at(d) * Y + y

    def remote(src, dst, ssem, rsem, to_ctx, to_tab):
        return pltpu.make_async_remote_copy(
            src_ref=src, dst_ref=dst, send_sem=ssem, recv_sem=rsem,
            device_id=(to_ctx, to_tab), device_id_type=MESH,
        )

    def got(dst, rsem, ssem):
        remote(dst, dst, ssem, rsem, c, t).wait_recv()

    def sent(src, ssem, rsem):
        remote(src, src, ssem, rsem, c, t).wait_send()

    cp_slice = pltpu.make_async_copy(
        masters_ref.at[:, pl.ds(pl.multiple_of(c * B, B), B)], mslice, loc_s.at[0]
    )
    cp_slice.start()
    cp_full = pltpu.make_async_copy(masters_ref, mfull, loc_s.at[1])
    cp_w = []
    for h in range(HEADS):
        for part in range(3):
            cp_w.append(
                pltpu.make_async_copy(
                    w_ref.at[:, pl.ds(part * HEADS * B + h * B, B)],
                    w_v.at[h, :, pl.ds(part * B, B)],
                    loc_s.at[2 + 3 * h + part],
                )
            )

    barrier = pltpu.get_barrier_semaphore()
    for d in (1, -1):
        pl.semaphore_signal(barrier, inc=1, device_id=(c, tab_z(d)), device_id_type=MESH)
    for d in range(1, Y):
        pl.semaphore_signal(barrier, inc=1, device_id=(c, tab_y(d)), device_id_type=MESH)
    for d in range(1, CTX):
        pl.semaphore_signal(barrier, inc=1, device_id=(ctx_at(d), t), device_id_type=MESH)

    item = item_ref[...]
    owner, row = lax.shift_right_logical(item, 6), item & 63
    place = (
        lax.shift_right_logical(owner, 2) * PLANE + ((y + Y - (owner & 3)) & 3) * ROWS + row
    )
    ids[c] = jnp.broadcast_to(place, (8, B))

    cp_slice.wait()
    tbl[z, 0:ROWS, :] = mslice[...].astype(BF16)
    pl.semaphore_wait(barrier, CTX - 1 + Y - 1 + 2)

    for d in (2, 1, 3):
        remote(
            tbl.at[z, pl.ds(0, ROWS)], tbl.at[z, pl.ds(d * ROWS, ROWS)],
            y_s.at[d - 1], y_r.at[d - 1], c, tab_y(d),
        ).start()
    for d in FAR_FIRST:
        remote(ids.at[c], ids.at[c], id_s.at[d - 1], id_r.at[d - 1], ctx_at(d), t).start()

    def ring_send(side, k, n):
        plane = z_at(-k) if side == 0 else z_at(k)
        block = tbl.at[plane, pl.ds(n * PIECE, PIECE)]
        return remote(
            block, block, z_s.at[side, k, n], z_r.at[side, k, n], c, tab_z(1 if side == 0 else -1)
        )

    def ring_got(side, k, n):
        plane = z_at(-1 - k) if side == 0 else z_at(1 + k)
        got(tbl.at[plane, pl.ds(n * PIECE, PIECE)], z_r.at[side, k, n], z_s.at[side, k, n])

    def far_side(n):
        return 0 if n < CHUNKS // 2 else 1

    per_piece = Y // CHUNKS
    for n in range(CHUNKS):
        for d in range(n * per_piece, (n + 1) * per_piece):
            if d:
                got(tbl.at[z, pl.ds(d * ROWS, ROWS)], y_r.at[d - 1], y_s.at[d - 1])
        for side in range(2):
            ring_send(side, 0, n).start()

    def to_heads(src_of, dst, ssem, rsem, local):
        for r in (2, 1, 3, 0):
            h = lax.rem(x + r, HEADS)
            for s in range(2):
                need = (c <= SPLIT + REACH - 2) if s == 0 else (c >= SPLIT)
                dev = 2 * h + s

                @pl.when(need & (dev != c))
                def _():
                    remote(src_of(h), dst.at[c], ssem.at[h, s], rsem.at[c], dev, t).start()

                @pl.when(need & (dev == c))
                def _():
                    local(h)

    def dout_of(h):
        return dout_ref.at[:, pl.ds(pl.multiple_of(h * B, B), B)]

    def dout_here(h):
        dob[c] = dout_ref[:, pl.ds(pl.multiple_of(h * B, B), B)]

    to_heads(dout_of, dob, do_s, do_r, dout_here)
    for copy in cp_w:
        copy.start()
    cp_full.start()

    actb = jnp.broadcast_to(act_ref[...], (B, B)).T
    for j in range(8):
        block = pl.ds(j * B, B)
        emb = jnp.broadcast_to(atab_ref[0:1, block], (B, B))
        for a in range(1, 8):
            emb = jnp.where(actb == a, atab_ref[a : a + 1, block], emb)
        xin[j] = emb
    h0, h1, h2, h3 = hist_ref[0, 0], hist_ref[0, 1], hist_ref[0, 2], hist_ref[0, 3]
    e0, e1, e2 = h0, h0 + h1, h0 + h1 + h2

    def spans(i, carry):
        p = lax.broadcasted_iota(I32, (B, B), 0) + i * B
        in0, in1, in2 = p < e0, p < e1, p < e2
        startb[i] = jnp.where(in0, 0, jnp.where(in1, e0, jnp.where(in2, e1, e2)))
        length = jnp.where(in0, h0, jnp.where(in1, h1, jnp.where(in2, h2, h3)))
        invb[i] = 1.0 / length.astype(F32)
        return carry

    lax.fori_loop(0, 8, spans, 0)
    for d in range(1, CTX):
        src = ctx_at(CTX - d)
        got(ids.at[src], id_r.at[d - 1], id_s.at[d - 1])

    def spread(j, carry):
        itemb[j] = jnp.broadcast_to(ids[j, 0:1, :], (B, B)).T
        gacc[j] = jnp.zeros((B, B), F32)
        return carry

    lax.fori_loop(0, 8, spread, 0)

    lane = lax.broadcasted_iota(I32, (2 * B, B), 1)

    def gather_plane(plane):
        rows = tbl[plane]
        base = plane * PLANE

        def some(i, carry):
            at = pl.ds(2 * i, 2)
            wanted = itemb[at].reshape(2 * B, B) - base
            hot = jnp.concatenate(
                [jnp.where(wanted == lane + k * B, 1.0, 0.0).astype(BF16) for k in range(2)], axis=1
            )
            gacc[at] = gacc[at] + dot(hot, rows).reshape(2, B, B)
            return carry

        lax.fori_loop(0, 4, some, 0)

    gather_plane(z)

    def ring_step(k, last):
        for n in range(CHUNKS):
            for side in range(2):
                ring_got(side, k - 1, n)
                if not last or far_side(n) == side:
                    ring_send(side, k, n).start()
        gather_plane(z_at(-k))
        gather_plane(z_at(k))

    def ring_body(k, carry):
        ring_step(k, False)
        return carry

    lax.fori_loop(1, half - 1, ring_body, 0)
    ring_step(half - 1, True)
    for n in range(CHUNKS):
        ring_got(far_side(n), half - 1, n)
    gather_plane(z_at(half))

    for j in range(8):
        g1[j] = gacc[j].astype(BF16)
    for d in FAR_FIRST:
        dst = ctx_at(d)
        remote(g1.at[dst], x1.at[c], a1_s.at[d - 1], a1_r.at[d - 1], dst, t).start()
    x1[c] = g1[c]
    for d in range(1, CTX):
        src = ctx_at(CTX - d)
        got(x1.at[src], a1_r.at[d - 1], a1_s.at[d - 1])

    total = jnp.zeros((B, B), F32)
    for j in range(8):
        value = xin[j] + x1[j].astype(F32)
        xin[j] = value
        total = total + value
    mean = jnp.sum(total, axis=1, keepdims=True) * (1.0 / MODEL)
    total = jnp.zeros((B, B), F32)
    for j in range(8):
        centre = xin[j] - mean
        total = total + centre * centre
    inv_std = lax.rsqrt(jnp.sum(total, axis=1, keepdims=True) * (1.0 / MODEL) + NORM_EPS)
    for j in range(8):
        normed = (xin[j] - mean) * inv_std
        xin[j] = normed
        hn[:, j * B : (j + 1) * B] = (normed * gain_ref[:, j * B : (j + 1) * B]).astype(BF16)
    for copy in cp_w:
        copy.wait()

    def q_of(h):
        return stq.at[h]

    def q_here(h):
        qb[c] = stq[h]

    holder = jnp.where(c >= SPLIT, 1, 0)
    for r in (2, 1, 3, 0):
        h = lax.rem(x + r, HEADS)
        project = dot(hn[...], w_v[h])
        sig = jax.nn.sigmoid(project)
        pd[h] = sig * (1.0 + project * (1.0 - sig))
        active = (project * sig).astype(BF16)
        stq[h] = active[:, 0:B]
        stkv[h] = active[:, B : 3 * B]
        dev = 2 * h + holder

        @pl.when(dev != c)
        def _():
            remote(stkv.at[h], kvb.at[c], kv_s.at[h], kv_r.at[c], dev, t).start()

        @pl.when(dev == c)
        def _():
            kvb[c] = stkv[h]

        for s in (1, 0):
            need = (c <= SPLIT + REACH - 2) if s == 0 else (c >= SPLIT)
            to = 2 * h + s

            @pl.when(need & (to != c))
            def _():
                remote(stq.at[h], qb.at[c], q_s.at[h, s], q_r.at[c], to, t).start()

            @pl.when(need & (to == c))
            def _():
                q_here(h)

    def send_back(stage, ssem, rsem, dst, block):
        @pl.when(c != block)
        def _():
            remote(stage.at[block], dst, ssem.at[block], rsem, block, t).start()

        @pl.when(c == block)
        def _():
            dst[...] = stage[block]

    def attend(s):
        key_blocks = range(0, SPLIT) if s == 0 else range(SPLIT, 8)
        lowest = key_blocks[0]
        query_blocks = range(0, SPLIT + REACH - 1) if s == 0 else range(SPLIT, 8)
        waited = set()
        for kb in key_blocks:
            end = min(kb + REACH, 8)
            n = (end - kb) * B

            @pl.when(c != kb)
            def _():
                got(kvb.at[kb], kv_r.at[kb], kv_s.at[0])

            for b in range(kb, end):
                if b not in waited:
                    waited.add(b)

                    @pl.when(c != b)
                    def _():
                        got(qb.at[b], q_r.at[b], q_s.at[0, 0])
                        got(dob.at[b], do_r.at[b], do_s.at[0, 0])

            queries = qb[kb:end].reshape(n, B)
            grad_out = dob[kb:end].reshape(n, B)
            keys = kvb[kb, :, 0:B]
            values = kvb[kb, :, B : 2 * B]
            raw = dot(queries, keys, NT) * SCALE
            sig = jax.nn.sigmoid(raw)
            inv = invb[kb:end].reshape(n, B)
            k_pos = lax.broadcasted_iota(I32, (n, B), 1) + kb * B
            q_pos = lax.broadcasted_iota(I32, (n, B), 0) + kb * B
            allowed = (k_pos >= startb[kb:end].reshape(n, B)) & (k_pos <= q_pos)
            weights = jnp.where(allowed, raw * sig * inv, 0.0).astype(BF16)
            grad_w = dot(grad_out, values, NT)
            slope = sig * (1.0 + raw * (1.0 - sig))
            grad_raw = jnp.where(allowed, grad_w * slope * (inv * SCALE), 0.0).astype(BF16)
            dkvs[kb, :, 0:B] = dot(grad_raw, queries, TN).astype(BF16)
            dkvs[kb, :, B : 2 * B] = dot(weights, grad_out, TN).astype(BF16)
            send_back(dkvs, dkv_s, dkv_r.at[x], rdkv.at[x], kb)
            dq = dot(grad_raw, keys)
            at = dot(weights, values)
            for b in range(kb, end):
                rows = slice((b - kb) * B, (b - kb + 1) * B)
                first = kb == max(b - REACH + 1, lowest)
                last = kb == min(b, key_blocks[-1])
                dq_b = dq[rows] if first else dqacc[b] + dq[rows]
                at_b = at[rows] if first else attacc[b] + at[rows]
                if last:
                    dqs[b] = dq_b.astype(BF16)
                    send_back(dqs, dq_s, dq_r.at[s, x], rdq.at[s, x], b)
                    atts[b] = at_b.astype(BF16)
                else:
                    dqacc[b] = dq_b
                    attacc[b] = at_b
        for b in query_blocks:
            send_back(atts, at_s, at_r.at[s, x], ratt.at[s, x], b)

    for s in range(2):
        @pl.when(core == s)
        def _():
            attend(s)

    both = (c >= SPLIT) & (c <= SPLIT + REACH - 2)
    for r in (0, 1, 3, 2):
        h = lax.rem(x + r, HEADS)

        @pl.when(2 * h + holder != c)
        def _():
            got(rdkv.at[h], dkv_r.at[h], dkv_s.at[0])
            got(rdq.at[holder, h], dq_r.at[holder, h], dq_s.at[0])

        @pl.when(both & (2 * h != c))
        def _():
            got(rdq.at[0, h], dq_r.at[0, h], dq_s.at[0])

        dqf[...] = rdq[holder, h].astype(F32)

        @pl.when(both)
        def _():
            dqf[...] = dqf[...] + rdq[0, h].astype(F32)

        slope = pd[h]
        grad_project = jnp.concatenate(
            [
                (dqf[...] * slope[:, 0:B]).astype(BF16),
                (rdkv[h].astype(F32) * slope[:, B : 3 * B]).astype(BF16),
            ],
            axis=1,
        )
        part = dot(grad_project, w_v[h], NT)
        gh[...] = part if r == 0 else gh[...] + part

    total = jnp.zeros((B, B), F32)
    cross = jnp.zeros((B, B), F32)
    for j in range(8):
        cols = slice(j * B, (j + 1) * B)
        g = gh[:, cols] * gain_ref[:, cols]
        gh[:, cols] = g
        total = total + g
        cross = cross + g * xin[j]
    mean_g = jnp.sum(total, axis=1, keepdims=True) * (1.0 / MODEL)
    mean_c = jnp.sum(cross, axis=1, keepdims=True) * (1.0 / MODEL)
    for j in range(8):
        g = gh[:, j * B : (j + 1) * B]
        g2[j] = (inv_std * (g - mean_g - xin[j] * mean_c)).astype(BF16)

    for d in FAR_FIRST:
        dst = ctx_at(d)
        remote(g2.at[dst], gin.at[c], a2_s.at[d - 1], a2_r.at[d - 1], dst, t).start()
    gin[c] = g2[c]
    for d in range(1, CTX):
        src = ctx_at(CTX - d)
        got(gin.at[src], a2_r.at[d - 1], a2_s.at[d - 1])

    sub = lax.broadcasted_iota(I32, (PLANE, B), 0)

    def plane_sum(plane):
        base = plane * PLANE
        hot = jnp.concatenate(
            [jnp.where(ids[j, 0:1, :] - base == sub, 1.0, 0.0).astype(BF16) for j in range(8)],
            axis=1,
        )
        return dot(hot, gin[...].reshape(8 * B, B))

    def reduce_send(side, k, n):
        at = pl.ds(n * PIECE, PIECE)
        return remote(
            sb.at[side, k, at], rb.at[side, k, at], rs_s.at[side, k, n], rs_r.at[side, k, n],
            c, tab_z(1 if side == 0 else -1),
        )

    def reduce_got(side, k, n):
        got(rb.at[side, k, pl.ds(n * PIECE, PIECE)], rs_r.at[side, k, n], rs_s.at[side, k, n])

    first_sum = plane_sum(z_at(half))
    for n in range(CHUNKS):
        rows = slice(n * PIECE, (n + 1) * PIECE)
        sb[far_side(n), 0, rows, :] = first_sum[rows].astype(BF16)
        reduce_send(far_side(n), 0, n).start()

    def reduce_step(k, first):
        for side in range(2):
            own[side] = plane_sum(z_at(half - k) if side == 0 else z_at(k - half))
        for n in range(CHUNKS):
            rows = slice(n * PIECE, (n + 1) * PIECE)
            for side in range(2):
                value = own[side, rows, :]
                if not first or far_side(n) == side:
                    reduce_got(side, k - 1, n)
                    value = value + rb[side, k - 1, rows, :].astype(F32)
                sb[side, k, rows, :] = value.astype(BF16)
                reduce_send(side, k, n).start()

    def reduce_body(k, carry):
        reduce_step(k, False)
        return carry

    reduce_step(1, True)
    lax.fori_loop(2, half, reduce_body, 0)
    own[0] = plane_sum(z)

    for h in range(HEADS):
        @pl.when(2 * h + holder != c)
        def _():
            got(ratt.at[holder, h], at_r.at[holder, h], at_s.at[0])

        @pl.when(both & (2 * h != c))
        def _():
            got(ratt.at[0, h], at_r.at[0, h], at_s.at[0])

        dqf[...] = ratt[holder, h].astype(F32)

        @pl.when(both)
        def _():
            dqf[...] = dqf[...] + ratt[0, h].astype(F32)

        att_out[:, h * B : (h + 1) * B] = dqf[...].astype(BF16)

    for n in range(CHUNKS):
        rows = slice(n * PIECE, (n + 1) * PIECE)
        value = own[0, rows, :]
        for side in range(2):
            reduce_got(side, half - 1, n)
            value = value + rb[side, half - 1, rows, :].astype(F32)
        own[0, rows, :] = value

    for d in (2, 1, 3):
        yb[0, d - 1] = own[0, d * ROWS : (d + 1) * ROWS, :].astype(BF16)
        remote(
            yb.at[0, d - 1], yb.at[1, d - 1], ry_s.at[d - 1], ry_r.at[d - 1], c, tab_y(-d)
        ).start()
    value = own[0, 0:ROWS, :]
    for d in (1, 3, 2):
        got(yb.at[1, d - 1], ry_r.at[d - 1], ry_s.at[d - 1])
        value = value + yb[1, d - 1].astype(F32)

    fin[c] = value.astype(BF16)
    for d in FAR_FIRST:
        remote(fin.at[c], fin.at[c], f_s.at[d - 1], f_r.at[d - 1], ctx_at(d), t).start()
    cp_full.wait()
    for d in range(1, CTX):
        src = ctx_at(CTX - d)
        got(fin.at[src], f_r.at[d - 1], f_s.at[d - 1])

    total = jnp.zeros((ROWS, B), F32)
    for j in range(8):
        g = fin[j].astype(F32)
        rg_out[:, j * B : (j + 1) * B] = g
        total = total + g * g
    diagonal = lax.broadcasted_iota(I32, (ROWS, ROWS), 0) == lax.broadcasted_iota(
        I32, (ROWS, ROWS), 1
    )
    before = jnp.sum(jnp.where(diagonal, accum_ref[...], 0.0), axis=1, keepdims=True)
    after = before + jnp.sum(total, axis=1, keepdims=True) * (1.0 / MODEL)
    na_out[...] = jnp.sum(jnp.where(diagonal, after, 0.0), axis=0, keepdims=True)
    rate = LEARN_RATE * lax.rsqrt(after)
    for j in range(8):
        cols = slice(j * B, (j + 1) * B)
        nm_out[:, cols] = mfull[:, cols] - fin[j].astype(F32) * rate

    for d in range(1, Y):
        sent(tbl.at[z, pl.ds(0, ROWS)], y_s.at[d - 1], y_r.at[d - 1])
        sent(yb.at[0, d - 1], ry_s.at[d - 1], ry_r.at[d - 1])
    for d in range(1, CTX):
        sent(ids.at[c], id_s.at[d - 1], id_r.at[d - 1])
        sent(g1.at[0], a1_s.at[d - 1], a1_r.at[d - 1])
        sent(g2.at[0], a2_s.at[d - 1], a2_r.at[d - 1])
        sent(fin.at[c], f_s.at[d - 1], f_r.at[d - 1])
    for side in range(2):
        for n in range(CHUNKS):
            for k in range(half):
                if k < half - 1 or far_side(n) == side:
                    ring_send(side, k, n).wait_send()
                if k > 0 or far_side(n) == side:
                    reduce_send(side, k, n).wait_send()
    for h in range(HEADS):
        @pl.when(2 * h + holder != c)
        def _():
            sent(stkv.at[h], kv_s.at[h], kv_r.at[0])

        for s in range(2):
            need = (c <= SPLIT + REACH - 2) if s == 0 else (c >= SPLIT)

            @pl.when(need & (2 * h + s != c))
            def _():
                sent(stq.at[h], q_s.at[h, s], q_r.at[0])
                sent(dob.at[0], do_s.at[h, s], do_r.at[0])

    for b in range(8):
        @pl.when((c != b) & (core == (0 if b < SPLIT else 1)))
        def _():
            sent(dkvs.at[b], dkv_s.at[b], dkv_r.at[0])

        for s in range(2):
            need = b <= SPLIT + REACH - 2 if s == 0 else b >= SPLIT
            if need:
                @pl.when((c != b) & (core == s))
                def _():
                    sent(dqs.at[b], dq_s.at[b], dq_r.at[0, 0])
                    sent(atts.at[b], at_s.at[b], at_r.at[0, 0])


def per_device(
    item_owner, item_row, action_id, history_len, masters, row_accum, action_table, norm_gain,
    w_qkv, d_attended,
):
    planes = lax.axis_size("tab") // Y
    half = planes // 2
    item = item_owner[0, :, 0][None, :] * ROWS + item_row
    vmem = pl.BlockSpec(memory_space=pltpu.VMEM)
    smem = pl.BlockSpec(memory_space=pltpu.SMEM)
    hbm = pl.BlockSpec(memory_space=pl.ANY)
    dma = pltpu.SemaphoreType.DMA

    def block(*lead, rows=B, cols=B, dtype=BF16):
        return pltpu.VMEM((*lead, rows, cols), dtype)

    scratch = [
        pltpu.VMEM((ROWS, B), F32),
        pltpu.VMEM((ROWS, MODEL), F32),
        pltpu.VMEM((HEADS, MODEL, 3 * B), BF16),
        block(planes, rows=PLANE),
        block(8, rows=8, dtype=I32),
        block(8, dtype=I32),
        block(8, dtype=F32),
        block(8),
        block(8),
        block(8, dtype=F32),
        block(cols=MODEL),
        block(8, dtype=I32),
        block(8, dtype=F32),
        block(HEADS, cols=3 * B, dtype=F32),
        block(HEADS),
        block(HEADS, cols=2 * B),
        block(8),
        block(8, cols=2 * B),
        block(8),
        block(8, dtype=F32),
        block(8, dtype=F32),
        block(8),
        block(8, cols=2 * B),
        block(8),
        block(2, HEADS),
        block(HEADS, cols=2 * B),
        block(2, HEADS),
        block(dtype=F32),
        block(cols=MODEL, dtype=F32),
        block(8),
        block(8),
        block(2, half, rows=PLANE),
        block(2, half, rows=PLANE),
        block(2, rows=PLANE, dtype=F32),
        block(2, Y - 1, rows=ROWS),
        block(8, rows=ROWS),
        dma((14,)),
        dma((Y - 1,)), dma((Y - 1,)),
        dma((2, half, CHUNKS)), dma((2, half, CHUNKS)),
        dma((7,)), dma((7,)),
        dma((7,)), dma((7,)),
        dma((HEADS, 2)), dma((8,)),
        dma((HEADS,)), dma((8,)),
        dma((HEADS, 2)), dma((8,)),
        dma((8,)), dma((2, HEADS)),
        dma((8,)), dma((HEADS,)),
        dma((8,)), dma((2, HEADS)),
        dma((7,)), dma((7,)),
        dma((2, half, CHUNKS)), dma((2, half, CHUNKS)),
        dma((Y - 1,)), dma((Y - 1,)),
        dma((7,)), dma((7,)),
    ]
    attended, row_grads, new_masters, new_accum = pl.pallas_call(
        functools.partial(kernel, planes),
        out_shape=(
            jax.ShapeDtypeStruct((B, HEADS * B), BF16),
            jax.ShapeDtypeStruct((ROWS, MODEL), F32),
            jax.ShapeDtypeStruct((ROWS, MODEL), F32),
            jax.ShapeDtypeStruct((1, ROWS), F32),
        ),
        in_specs=[vmem, vmem, smem, hbm, vmem, vmem, vmem, hbm, vmem],
        out_specs=(vmem, vmem, vmem, vmem),
        scratch_shapes=scratch,
        compiler_params=pltpu.CompilerParams(
            collective_id=0, has_side_effects=True, vmem_limit_bytes=48 * 1024 * 1024
        ),
    )(
        item, action_id, history_len, masters, row_accum[None, :], action_table,
        norm_gain[None, :], w_qkv, d_attended[0],
    )
    return (attended[None], row_grads, new_masters, new_accum[0])


def solution(mesh):
    in_specs = (
        P("tab", "ctx", None),
        P("tab", "ctx"),
        P("tab", "ctx"),
        P("tab", None),
        P("tab", None),
        P("tab"),
        P(),
        P(),
        P(),
        P("tab", "ctx", None),
    )
    out_specs = (P("tab", "ctx", None), P("tab", None), P("tab", None), P("tab"))
    return jax.shard_map(
        per_device, mesh=mesh, in_specs=in_specs, out_specs=out_specs, check_vma=False
    )
```

```python
import math

import jax
import jax.numpy as jnp
from jax import lax
from jax.experimental import pallas as pl
from jax.experimental.pallas import tpu as pltpu
from jax.sharding import PartitionSpec as P

MESH = pl.DeviceIdType.MESH
F32 = jnp.float32
BF16 = jnp.bfloat16
I32 = jnp.int32

NORM_EPS = 1e-05
LEARN_RATE = 0.1

CTX = 8
Y = 4
B = 128
ROWS = 64
PLANE = Y * ROWS
MODEL = 1024
HEADS = 4
Z = 16
GROUPS = 4
SLOTS = (0, 1, -1, 2, -2, 3, -3, 4, -4, 5, -5, 6, -6, 7, -7, 8)
SLOT_OF = {distance: slot for slot, distance in enumerate(SLOTS)} | {-8: 15}
LEAP = 4
HALF = ROWS // 2
SPLIT = 3
REACH = 5
SCALE = 1.0 / math.sqrt(B)
FAR_FIRST = (4, 3, 5, 2, 6, 1, 7)

NT = (((1,), (1,)), ((), ()))
TN = (((0,), (0,)), ((), ()))


def dot(a, b, dims=(((1,), (0,)), ((), ()))):
    return lax.dot_general(a, b, dims, preferred_element_type=F32)


def kernel(
    owner_hbm, row_hbm, act_hbm, hist_hbm, masters_ref, accum_hbm, atab_hbm, gain_hbm, w_ref,
    dout_hbm,
    att_out, rg_out, nm_out, na_out,
    owner_ref, row_ref, act_ref, hist_ref, accum_ref, atab_ref, gain_ref, dout_ref,
    mslice, mfull, w_v, tbl, ids, high, low, high_row, low_row, gacc, g1, x1, xin, hn, startb, invb,
    pd, stq, stkv, qb, kvb, dob, attacc, dqacc, dqs, dkvs, atts, rdq, rdkv, ratt, dqf, gh,
    g2, gin, psum, own, yb, stage, agg, zb, fin,
    loc_s, y_s, y_r, z_s, z_r, id_s, id_r, a1_s, a1_r, q_s, q_r, kv_s, kv_r, do_s, do_r,
    dq_s, dq_r, dkv_s, dkv_r, at_s, at_r, a2_s, a2_r, ry_s, ry_r, ag_s, ag_r, rz_s, rz_r, f_s, f_r,
):
    c = lax.axis_index("ctx")
    t = lax.axis_index("tab")
    x, core = lax.div(c, 2), lax.rem(c, 2)
    z, y = lax.div(t, Y), lax.rem(t, Y)

    def ctx_at(d):
        return lax.rem(c + d, CTX)

    def tab_y(d):
        return z * Y + lax.rem(y + d + Y, Y)

    def z_at(d):
        return lax.rem(z + d + Z, Z)

    def tab_z(d):
        return z_at(d) * Y + y

    def remote(src, dst, ssem, rsem, to_ctx, to_tab):
        return pltpu.make_async_remote_copy(
            src_ref=src, dst_ref=dst, send_sem=ssem, recv_sem=rsem,
            device_id=(to_ctx, to_tab), device_id_type=MESH,
        )

    def got(dst, rsem, ssem):
        remote(dst, dst, ssem, rsem, c, t).wait_recv()

    def sent(src, ssem, rsem):
        remote(src, src, ssem, rsem, c, t).wait_send()

    cp_slice = pltpu.make_async_copy(
        masters_ref.at[:, pl.ds(pl.multiple_of(c * B, B), B)], mslice, loc_s.at[0]
    )
    cp_slice.start()
    cp_ids = []
    for i, (src, dst) in enumerate(((owner_hbm, owner_ref), (row_hbm, row_ref))):
        cp_ids.append(pltpu.make_async_copy(src, dst, loc_s.at[14 + i]))
        cp_ids[-1].start()
    cp_dout = pltpu.make_async_copy(dout_hbm, dout_ref, loc_s.at[16])
    cp_dout.start()
    cp_small = []
    for i, (src, dst) in enumerate(
        (
            (act_hbm, act_ref), (atab_hbm, atab_ref), (hist_hbm, hist_ref), (gain_hbm, gain_ref),
            (accum_hbm, accum_ref),
        )
    ):
        cp_small.append(pltpu.make_async_copy(src, dst, loc_s.at[17 + i]))
        cp_small[-1].start()
    cp_full = pltpu.make_async_copy(masters_ref, mfull, loc_s.at[1])
    cp_w = []
    for h in range(HEADS):
        for part in range(3):
            cp_w.append(
                pltpu.make_async_copy(
                    w_ref.at[:, pl.ds(part * HEADS * B + h * B, B)],
                    w_v.at[h, :, pl.ds(part * B, B)],
                    loc_s.at[2 + 3 * h + part],
                )
            )

    barrier = pltpu.get_barrier_semaphore()
    for d in range(1, LEAP + 1):
        for e in (d, -d):
            pl.semaphore_signal(barrier, inc=1, device_id=(c, tab_z(e)), device_id_type=MESH)
    for d in range(1, Y):
        pl.semaphore_signal(barrier, inc=1, device_id=(c, tab_y(d)), device_id_type=MESH)
    for d in range(1, CTX):
        pl.semaphore_signal(barrier, inc=1, device_id=(ctx_at(d), t), device_id_type=MESH)

    for copy in cp_ids:
        copy.wait()
    owner, row = owner_ref[...], row_ref[...]
    ahead = (lax.shift_right_logical(owner, 2) + Z - z) & (Z - 1)
    slot = jnp.where(ahead > Z // 2, 2 * (Z - ahead), jnp.maximum(2 * ahead - 1, 0))
    behind = (y + Y - (owner & (Y - 1))) & (Y - 1)
    ids[c] = jnp.broadcast_to(behind * (Z * ROWS) + slot * ROWS + row, (8, B))

    cp_slice.wait()
    tbl[0, 0] = mslice[...].astype(BF16)
    pl.semaphore_wait(barrier, CTX - 1 + Y - 1 + 2 * LEAP)

    half_rows = (pl.ds(0, HALF), pl.ds(HALF, HALF))

    def near_send(e):
        to = SLOT_OF[-e]
        return remote(tbl.at[0, 0], tbl.at[0, to], z_s.at[to], z_r.at[to], c, tab_z(e))

    def far_send(side, f):
        e = f if side == 0 else -f
        src = tbl.at[0, SLOT_OF[-LEAP if side == 0 else LEAP]]
        to = SLOT_OF[-LEAP - f if side == 0 else LEAP + f]
        if f < LEAP:
            return remote(src, tbl.at[0, to], z_s.at[to], z_r.at[to], c, tab_z(e))
        at = half_rows[side]
        return remote(
            src.at[at], tbl.at[0, to, at], z_s.at[15 + side], z_r.at[15 + side], c, tab_z(e)
        )

    def slot_got(to):
        if to < 15:
            got(tbl.at[0, to], z_r.at[to], z_s.at[to])
        else:
            for side in range(2):
                got(tbl.at[0, 15, half_rows[side]], z_r.at[15 + side], z_s.at[15 + side])

    nearest = [e for d in range(LEAP, 0, -1) for e in (d, -d)]
    for e in nearest:
        near_send(e).start()
    for d in FAR_FIRST:
        remote(ids.at[c], ids.at[c], id_s.at[d - 1], id_r.at[d - 1], ctx_at(d), t).start()

    def group_send(d, g):
        at = pl.ds(GROUPS * g, GROUPS)
        return remote(
            tbl.at[0, at], tbl.at[d, at], y_s.at[d - 1, g], y_r.at[d - 1, g], c, tab_y(d)
        )

    def group_got(d, g):
        got(tbl.at[d, pl.ds(GROUPS * g, GROUPS)], y_r.at[d - 1, g], y_s.at[d - 1, g])

    def sum_send(d, g):
        return remote(
            psum.at[d, g], yb.at[d - 1, g], ry_s.at[d - 1, g], ry_r.at[d - 1, g], c, tab_y(-d)
        )

    def sum_got(d, g):
        got(yb.at[d - 1, g], ry_r.at[d - 1, g], ry_s.at[d - 1, g])

    def gather_send(slot):
        distance = SLOTS[slot]
        copies = []
        for side in range(2) if slot == 15 else (0,) if distance > 0 else (1,):
            f = abs(distance) - LEAP
            at = half_rows[side] if slot == 15 else pl.ds(0, ROWS)
            copies.append(
                remote(
                    stage.at[slot, at], agg.at[side, f - 1, at],
                    ag_s.at[side, f - 1], ag_r.at[side, f - 1], c, tab_z(f if side == 0 else -f),
                )
            )
        return copies

    def gather_got(side, f):
        at = half_rows[side] if f == LEAP else pl.ds(0, ROWS)
        got(agg.at[side, f - 1, at], ag_r.at[side, f - 1], ag_s.at[side, f - 1])

    def target_send(slot):
        to = SLOT_OF[-SLOTS[slot]]
        return remote(
            stage.at[slot], zb.at[to - 1], rz_s.at[to - 1], rz_r.at[to - 1], c, tab_z(SLOTS[slot])
        )

    def target_got(to):
        got(zb.at[to - 1], rz_r.at[to - 1], rz_s.at[to - 1])

    holder = jnp.where(c >= SPLIT, 1, 0)

    def drain(upto=9):
        for d in range(1, Y):
            for g in range(GROUPS):
                group_send(d, g).wait_send()
                if upto >= 8:
                    sum_send(d, g).wait_send()
        for d in range(1, CTX):
            sent(ids.at[c], id_s.at[d - 1], id_r.at[d - 1])
            if upto >= 3:
                sent(g1.at[0], a1_s.at[d - 1], a1_r.at[d - 1])
            if upto >= 7:
                sent(g2.at[0], a2_s.at[d - 1], a2_r.at[d - 1])
            if upto >= 9:
                sent(fin.at[c], f_s.at[d - 1], f_r.at[d - 1])
        for e in nearest:
            near_send(e).wait_send()
        for side in range(2):
            for f in range(1, LEAP + 1):
                far_send(side, f).wait_send()
        for slot in range(1, Z) if upto >= 8 else ():
            for copy in gather_send(slot) if slot > 2 * LEAP else [target_send(slot)]:
                copy.wait_send()
        for h in range(HEADS):
            for s in range(2):
                need = (c <= SPLIT + REACH - 2) if s == 0 else (c >= SPLIT)

                @pl.when(need & (2 * h + s != c))
                def _():
                    sent(dob.at[0], do_s.at[h, s], do_r.at[0])
                    if upto >= 4:
                        sent(stq.at[h], q_s.at[h, s], q_r.at[0])

            if upto >= 4:
                @pl.when(2 * h + holder != c)
                def _():
                    sent(stkv.at[h], kv_s.at[h], kv_r.at[0])

        for b in range(8) if upto >= 5 else ():
            @pl.when((c != b) & (core == (0 if b < SPLIT else 1)))
            def _():
                sent(dkvs.at[b], dkv_s.at[b], dkv_r.at[0])

            for s in range(2):
                need = b <= SPLIT + REACH - 2 if s == 0 else b >= SPLIT
                if need:
                    @pl.when((c != b) & (core == s))
                    def _():
                        sent(dqs.at[b], dq_s.at[b], dq_r.at[0, 0])
                        sent(atts.at[b], at_s.at[b], at_r.at[0, 0])

    def to_heads(src_of, dst, ssem, rsem, local):
        for r in (2, 1, 3, 0):
            h = lax.rem(x + r, HEADS)
            for s in range(2):
                need = (c <= SPLIT + REACH - 2) if s == 0 else (c >= SPLIT)
                dev = 2 * h + s

                @pl.when(need & (dev != c))
                def _():
                    remote(src_of(h), dst.at[c], ssem.at[h, s], rsem.at[c], dev, t).start()

                @pl.when(need & (dev == c))
                def _():
                    local(h)

    def dout_of(h):
        return dout_ref.at[:, pl.ds(pl.multiple_of(h * B, B), B)]

    def dout_here(h):
        dob[c] = dout_ref[:, pl.ds(pl.multiple_of(h * B, B), B)]

    cp_dout.wait()
    to_heads(dout_of, dob, do_s, do_r, dout_here)
    for copy in cp_w:
        copy.start()
    cp_full.start()

    for copy in cp_small:
        copy.wait()
    actb = jnp.broadcast_to(act_ref[...], (B, B)).T
    for j in range(8):
        block = pl.ds(j * B, B)
        emb = jnp.broadcast_to(atab_ref[0:1, block], (B, B))
        for a in range(1, 8):
            emb = jnp.where(actb == a, atab_ref[a : a + 1, block], emb)
        xin[j] = emb
    h0, h1, h2, h3 = hist_ref[0, 0], hist_ref[0, 1], hist_ref[0, 2], hist_ref[0, 3]
    e0, e1, e2 = h0, h0 + h1, h0 + h1 + h2

    def spans(i, carry):
        p = lax.broadcasted_iota(I32, (B, B), 0) + i * B
        in0, in1, in2 = p < e0, p < e1, p < e2
        startb[i] = jnp.where(in0, 0, jnp.where(in1, e0, jnp.where(in2, e1, e2)))
        length = jnp.where(in0, h0, jnp.where(in1, h1, jnp.where(in2, h2, h3)))
        invb[i] = 1.0 / length.astype(F32)
        return carry

    lax.fori_loop(0, 8, spans, 0)
    for d in range(1, CTX):
        src = ctx_at(CTX - d)
        got(ids.at[src], id_r.at[d - 1], id_s.at[d - 1])

    def spread(j, carry):
        column = jnp.broadcast_to(ids[j, 0:1, :], (B, B)).T
        at = pl.ds(8 * j, 8)
        high[at] = lax.shift_right_logical(column, 8).astype(F32).astype(BF16).reshape(8, 16, B)
        low[at] = (column & (PLANE - 1)).astype(F32).astype(BF16).reshape(8, 16, B)
        line = jnp.broadcast_to(ids[j, 0:1, :], (16, B))
        high_row[j] = lax.shift_right_logical(line, 8).astype(F32).astype(BF16)
        low_row[j] = (line & (PLANE - 1)).astype(F32).astype(BF16)
        gacc[j] = jnp.zeros((B, B), F32)
        return carry

    lax.fori_loop(0, 8, spread, 0)

    one, zero, none = jnp.asarray(1, BF16), jnp.asarray(0, BF16), jnp.asarray(-1, BF16)
    lane = lax.broadcasted_iota(I32, (16, B), 1).astype(F32).astype(BF16)

    def gather_tile(d, g):
        this = jnp.asarray(d * GROUPS + g, BF16)
        wanted = jnp.where(high[...] == this, low[...], none)
        hot = jnp.concatenate(
            [
                jnp.where(wanted == (lane + jnp.asarray(k * B, BF16))[None], one, zero)
                .reshape(8 * B, B)
                for k in range(2)
            ],
            axis=1,
        )
        rows = tbl[d, GROUPS * g : GROUPS * (g + 1)].reshape(PLANE, B)
        gacc[...] = gacc[...] + dot(hot, rows).reshape(8, B, B)

    slot_got(SLOT_OF[-LEAP])
    for f in range(LEAP, 0, -1):
        far_send(0, f).start()
    slot_got(SLOT_OF[LEAP])
    for f in range(LEAP, 0, -1):
        far_send(1, f).start()

    def pass_on(g):
        for to in range(GROUPS * g, GROUPS * (g + 1)):
            if to and abs(SLOTS[to]) != LEAP:
                slot_got(to)
        for d in (2, 1, 3):
            group_send(d, g).start()

    pass_on(0)
    pass_on(1)
    gather_tile(0, 0)
    gather_tile(0, 1)
    for d in (1, 3, 2):
        group_got(d, 0)
        gather_tile(d, 0)
    pass_on(2)
    pass_on(3)
    gather_tile(0, 2)
    gather_tile(0, 3)
    for g in (1, 2, 3):
        for d in (1, 3, 2):
            group_got(d, g)
            gather_tile(d, g)

    for j in range(8):
        g1[j] = gacc[j].astype(BF16)
    for d in FAR_FIRST:
        dst = ctx_at(d)
        remote(g1.at[dst], x1.at[c], a1_s.at[d - 1], a1_r.at[d - 1], dst, t).start()
    x1[c] = g1[c]
    for d in range(1, CTX):
        src = ctx_at(CTX - d)
        got(x1.at[src], a1_r.at[d - 1], a1_s.at[d - 1])

    total = jnp.zeros((B, B), F32)
    for j in range(8):
        value = xin[j] + x1[j].astype(F32)
        xin[j] = value
        total = total + value
    mean = jnp.sum(total, axis=1, keepdims=True) * (1.0 / MODEL)
    total = jnp.zeros((B, B), F32)
    for j in range(8):
        centre = xin[j] - mean
        total = total + centre * centre
    inv_std = lax.rsqrt(jnp.sum(total, axis=1, keepdims=True) * (1.0 / MODEL) + NORM_EPS)
    for j in range(8):
        normed = (xin[j] - mean) * inv_std
        xin[j] = normed
        hn[:, j * B : (j + 1) * B] = (normed * gain_ref[:, j * B : (j + 1) * B]).astype(BF16)
    for copy in cp_w:
        copy.wait()

    def q_of(h):
        return stq.at[h]

    def q_here(h):
        qb[c] = stq[h]

    for r in (2, 1, 3, 0):
        h = lax.rem(x + r, HEADS)
        project = dot(hn[...], w_v[h])
        sig = jax.nn.sigmoid(project)
        pd[h] = sig * (1.0 + project * (1.0 - sig))
        active = (project * sig).astype(BF16)
        stq[h] = active[:, 0:B]
        stkv[h] = active[:, B : 3 * B]
        dev = 2 * h + holder

        @pl.when(dev != c)
        def _():
            remote(stkv.at[h], kvb.at[c], kv_s.at[h], kv_r.at[c], dev, t).start()

        @pl.when(dev == c)
        def _():
            kvb[c] = stkv[h]

        for s in (1, 0):
            need = (c <= SPLIT + REACH - 2) if s == 0 else (c >= SPLIT)
            to = 2 * h + s

            @pl.when(need & (to != c))
            def _():
                remote(stq.at[h], qb.at[c], q_s.at[h, s], q_r.at[c], to, t).start()

            @pl.when(need & (to == c))
            def _():
                q_here(h)

    def send_back(ready, ssem, rsem, dst, block):
        @pl.when(c != block)
        def _():
            remote(ready.at[block], dst, ssem.at[block], rsem, block, t).start()

        @pl.when(c == block)
        def _():
            dst[...] = ready[block]

    def attend(s):
        key_blocks = range(0, SPLIT) if s == 0 else range(SPLIT, 8)
        lowest = key_blocks[0]
        query_blocks = range(0, SPLIT + REACH - 1) if s == 0 else range(SPLIT, 8)
        waited = set()
        for kb in key_blocks:
            end = min(kb + REACH, 8)
            n = (end - kb) * B

            @pl.when(c != kb)
            def _():
                got(kvb.at[kb], kv_r.at[kb], kv_s.at[0])

            for b in range(kb, end):
                if b not in waited:
                    waited.add(b)

                    @pl.when(c != b)
                    def _():
                        got(qb.at[b], q_r.at[b], q_s.at[0, 0])
                        got(dob.at[b], do_r.at[b], do_s.at[0, 0])

            queries = qb[kb:end].reshape(n, B)
            grad_out = dob[kb:end].reshape(n, B)
            keys = kvb[kb, :, 0:B]
            values = kvb[kb, :, B : 2 * B]
            raw = dot(queries, keys, NT) * SCALE
            sig = jax.nn.sigmoid(raw)
            inv = invb[kb:end].reshape(n, B)
            k_pos = lax.broadcasted_iota(I32, (n, B), 1) + kb * B
            q_pos = lax.broadcasted_iota(I32, (n, B), 0) + kb * B
            allowed = (k_pos >= startb[kb:end].reshape(n, B)) & (k_pos <= q_pos)
            weights = jnp.where(allowed, raw * sig * inv, 0.0).astype(BF16)
            grad_w = dot(grad_out, values, NT)
            slope = sig * (1.0 + raw * (1.0 - sig))
            grad_raw = jnp.where(allowed, grad_w * slope * (inv * SCALE), 0.0).astype(BF16)
            dkvs[kb, :, 0:B] = dot(grad_raw, queries, TN).astype(BF16)
            dkvs[kb, :, B : 2 * B] = dot(weights, grad_out, TN).astype(BF16)
            send_back(dkvs, dkv_s, dkv_r.at[x], rdkv.at[x], kb)
            dq = dot(grad_raw, keys)
            at = dot(weights, values)
            for b in range(kb, end):
                rows = slice((b - kb) * B, (b - kb + 1) * B)
                first = kb == max(b - REACH + 1, lowest)
                last = kb == min(b, key_blocks[-1])
                dq_b = dq[rows] if first else dqacc[b] + dq[rows]
                at_b = at[rows] if first else attacc[b] + at[rows]
                if last:
                    dqs[b] = dq_b.astype(BF16)
                    send_back(dqs, dq_s, dq_r.at[s, x], rdq.at[s, x], b)
                    atts[b] = at_b.astype(BF16)
                else:
                    dqacc[b] = dq_b
                    attacc[b] = at_b
        for b in query_blocks:
            send_back(atts, at_s, at_r.at[s, x], ratt.at[s, x], b)

    for s in range(2):
        @pl.when(core == s)
        def _():
            attend(s)

    both = (c >= SPLIT) & (c <= SPLIT + REACH - 2)
    for r in (0, 1, 3, 2):
        h = lax.rem(x + r, HEADS)

        @pl.when(2 * h + holder != c)
        def _():
            got(rdkv.at[h], dkv_r.at[h], dkv_s.at[0])
            got(rdq.at[holder, h], dq_r.at[holder, h], dq_s.at[0])

        @pl.when(both & (2 * h != c))
        def _():
            got(rdq.at[0, h], dq_r.at[0, h], dq_s.at[0])

        dqf[...] = rdq[holder, h].astype(F32)

        @pl.when(both)
        def _():
            dqf[...] = dqf[...] + rdq[0, h].astype(F32)

        slope = pd[h]
        grad_project = jnp.concatenate(
            [
                (dqf[...] * slope[:, 0:B]).astype(BF16),
                (rdkv[h].astype(F32) * slope[:, B : 3 * B]).astype(BF16),
            ],
            axis=1,
        )
        part = dot(grad_project, w_v[h], NT)
        gh[...] = part if r == 0 else gh[...] + part

    total = jnp.zeros((B, B), F32)
    cross = jnp.zeros((B, B), F32)
    for j in range(8):
        cols = slice(j * B, (j + 1) * B)
        g = gh[:, cols] * gain_ref[:, cols]
        gh[:, cols] = g
        total = total + g
        cross = cross + g * xin[j]
    mean_g = jnp.sum(total, axis=1, keepdims=True) * (1.0 / MODEL)
    mean_c = jnp.sum(cross, axis=1, keepdims=True) * (1.0 / MODEL)
    for j in range(8):
        g = gh[:, j * B : (j + 1) * B]
        g2[j] = (inv_std * (g - mean_g - xin[j] * mean_c)).astype(BF16)

    for d in FAR_FIRST:
        dst = ctx_at(d)
        remote(g2.at[dst], gin.at[c], a2_s.at[d - 1], a2_r.at[d - 1], dst, t).start()
    gin[c] = g2[c]
    for d in range(1, CTX):
        src = ctx_at(CTX - d)
        got(gin.at[src], a2_r.at[d - 1], a2_s.at[d - 1])

    sub = lax.broadcasted_iota(I32, (PLANE, B), 0).astype(F32).astype(BF16).reshape(16, 16, B)

    def tile_sum(d, g):
        this = jnp.asarray(d * GROUPS + g, BF16)
        wanted = jnp.where(high_row[...] == this, low_row[...], none)
        hot = jnp.concatenate(
            [jnp.where(sub == wanted[j][None], one, zero).reshape(PLANE, B) for j in range(8)],
            axis=1,
        )
        return dot(hot, gin[...].reshape(8 * B, B))

    for g in (3, 2, 1, 0):
        for d in (2, 1, 3):
            psum[d, g] = tile_sum(d, g).astype(BF16)
            sum_send(d, g).start()
        own[g] = tile_sum(0, g)
    for g in (3, 2, 1, 0):
        value = own[g]
        for d in (1, 3, 2):
            sum_got(d, g)
            value = value + yb[d - 1, g].astype(F32)
        own[g] = value
        for i in range(GROUPS):
            slot = GROUPS * g + i
            if slot and abs(SLOTS[slot]) != LEAP:
                stage[slot] = value[i * ROWS : (i + 1) * ROWS].astype(BF16)
                for copy in gather_send(slot) if slot > 2 * LEAP else [target_send(slot)]:
                    copy.start()
    for side in range(2):
        slot = SLOT_OF[LEAP if side == 0 else -LEAP]
        i = slot % GROUPS
        total = own[slot // GROUPS, i * ROWS : (i + 1) * ROWS, :]
        for f in range(1, LEAP):
            gather_got(side, f)
            total = total + agg[side, f - 1].astype(F32)
        gather_got(side, LEAP)
        stage[slot] = total.astype(BF16)
        at = slice(side * HALF, (side + 1) * HALF)
        stage[slot, at, :] = (total[at] + agg[side, LEAP - 1, at, :].astype(F32)).astype(BF16)
        target_send(slot).start()

    for h in range(HEADS):
        @pl.when(2 * h + holder != c)
        def _():
            got(ratt.at[holder, h], at_r.at[holder, h], at_s.at[0])

        @pl.when(both & (2 * h != c))
        def _():
            got(ratt.at[0, h], at_r.at[0, h], at_s.at[0])

        dqf[...] = ratt[holder, h].astype(F32)

        @pl.when(both)
        def _():
            dqf[...] = dqf[...] + ratt[0, h].astype(F32)

        att_out[:, h * B : (h + 1) * B] = dqf[...].astype(BF16)

    value = own[0, 0:ROWS, :]
    for to in range(1, 2 * LEAP + 1):
        target_got(to)
        value = value + zb[to - 1].astype(F32)

    fin[c] = value.astype(BF16)
    for d in FAR_FIRST:
        remote(fin.at[c], fin.at[c], f_s.at[d - 1], f_r.at[d - 1], ctx_at(d), t).start()
    cp_full.wait()
    for d in range(1, CTX):
        src = ctx_at(CTX - d)
        got(fin.at[src], f_r.at[d - 1], f_s.at[d - 1])

    total = jnp.zeros((ROWS, B), F32)
    for j in range(8):
        g = fin[j].astype(F32)
        rg_out[:, j * B : (j + 1) * B] = g
        total = total + g * g
    diagonal = lax.broadcasted_iota(I32, (ROWS, ROWS), 0) == lax.broadcasted_iota(
        I32, (ROWS, ROWS), 1
    )
    before = jnp.sum(jnp.where(diagonal, accum_ref[...], 0.0), axis=1, keepdims=True)
    after = before + jnp.sum(total, axis=1, keepdims=True) * (1.0 / MODEL)
    na_out[...] = jnp.sum(jnp.where(diagonal, after, 0.0), axis=0, keepdims=True)
    rate = LEARN_RATE * lax.rsqrt(after)
    for j in range(8):
        cols = slice(j * B, (j + 1) * B)
        nm_out[:, cols] = mfull[:, cols] - fin[j].astype(F32) * rate

    drain()


def per_device(
    item_owner, item_row, action_id, history_len, masters, row_accum, action_table, norm_gain,
    w_qkv, d_attended,
):
    vmem = pl.BlockSpec(memory_space=pltpu.VMEM)
    hbm = pl.BlockSpec(memory_space=pltpu.HBM)
    dma = pltpu.SemaphoreType.DMA

    def block(*lead, rows=B, cols=B, dtype=BF16):
        return pltpu.VMEM((*lead, rows, cols), dtype)

    scratch = [
        pltpu.VMEM((1, B), I32),
        pltpu.VMEM((1, B), I32),
        pltpu.VMEM((1, B), I32),
        pltpu.SMEM((1, 4), I32),
        pltpu.VMEM((1, ROWS), F32),
        pltpu.VMEM((8, MODEL), F32),
        pltpu.VMEM((1, MODEL), F32),
        pltpu.VMEM((B, HEADS * B), BF16),
        pltpu.VMEM((ROWS, B), F32),
        pltpu.VMEM((ROWS, MODEL), F32),
        pltpu.VMEM((HEADS, MODEL, 3 * B), BF16),
        block(Y, Z, rows=ROWS),
        block(8, rows=8, dtype=I32),
        block(HEADS * 16, rows=16),
        block(HEADS * 16, rows=16),
        block(8, rows=16),
        block(8, rows=16),
        block(8, dtype=F32),
        block(8),
        block(8),
        block(8, dtype=F32),
        block(cols=MODEL),
        block(8, dtype=I32),
        block(8, dtype=F32),
        block(HEADS, cols=3 * B, dtype=F32),
        block(HEADS),
        block(HEADS, cols=2 * B),
        block(8),
        block(8, cols=2 * B),
        block(8),
        block(8, dtype=F32),
        block(8, dtype=F32),
        block(8),
        block(8, cols=2 * B),
        block(8),
        block(2, HEADS),
        block(HEADS, cols=2 * B),
        block(2, HEADS),
        block(dtype=F32),
        block(cols=MODEL, dtype=F32),
        block(8),
        block(8),
        block(Y, GROUPS, rows=PLANE),
        block(GROUPS, rows=PLANE, dtype=F32),
        block(Y - 1, GROUPS, rows=PLANE),
        block(Z, rows=ROWS),
        block(2, LEAP, rows=ROWS),
        block(2 * LEAP, rows=ROWS),
        block(8, rows=ROWS),
        dma((22,)),
        dma((Y - 1, GROUPS)), dma((Y - 1, GROUPS)),
        dma((Z + 1,)), dma((Z + 1,)),
        dma((7,)), dma((7,)),
        dma((7,)), dma((7,)),
        dma((HEADS, 2)), dma((8,)),
        dma((HEADS,)), dma((8,)),
        dma((HEADS, 2)), dma((8,)),
        dma((8,)), dma((2, HEADS)),
        dma((8,)), dma((HEADS,)),
        dma((8,)), dma((2, HEADS)),
        dma((7,)), dma((7,)),
        dma((Y - 1, GROUPS)), dma((Y - 1, GROUPS)),
        dma((2, LEAP)), dma((2, LEAP)),
        dma((2 * LEAP,)), dma((2 * LEAP,)),
        dma((7,)), dma((7,)),
    ]
    attended, row_grads, new_masters, new_accum = pl.pallas_call(
        kernel,
        out_shape=(
            jax.ShapeDtypeStruct((B, HEADS * B), BF16),
            jax.ShapeDtypeStruct((ROWS, MODEL), F32),
            jax.ShapeDtypeStruct((ROWS, MODEL), F32),
            jax.ShapeDtypeStruct((1, ROWS), F32),
        ),
        in_specs=[hbm] * 10,
        out_specs=(vmem, vmem, vmem, vmem),
        scratch_shapes=scratch,
        compiler_params=pltpu.CompilerParams(
            collective_id=0, has_side_effects=True, vmem_limit_bytes=63 * 1024 * 1024
        ),
    )(
        item_owner[:, :, 0], item_row, action_id, history_len, masters, row_accum[None, :], action_table,
        norm_gain[None, :], w_qkv, d_attended[0],
    )
    return (attended[None], row_grads, new_masters, new_accum[0])


def solution(mesh):
    in_specs = (
        P("tab", "ctx", None),
        P("tab", "ctx"),
        P("tab", "ctx"),
        P("tab", None),
        P("tab", None),
        P("tab"),
        P(),
        P(),
        P(),
        P("tab", "ctx", None),
    )
    out_specs = (P("tab", "ctx", None), P("tab", None), P("tab", None), P("tab"))
    return jax.shard_map(
        per_device, mesh=mesh, in_specs=in_specs, out_specs=out_specs, check_vma=False
    )
```

```python
import math

import jax
import jax.numpy as jnp
from jax import lax
from jax.experimental import pallas as pl
from jax.experimental.pallas import tpu as pltpu
from jax.sharding import PartitionSpec as P

MESH = pl.DeviceIdType.MESH
F32 = jnp.float32
BF16 = jnp.bfloat16
I32 = jnp.int32

NORM_EPS = 1e-05
LEARN_RATE = 0.1

CTX = 8
Y = 4
B = 128
ROWS = 64
PLANE = Y * ROWS
MODEL = 1024
HEADS = 4
Z = 16
GROUPS = 4
SLOTS = (0, 1, -1, 2, -2, 3, -3, 4, -4, 5, -5, 6, -6, 7, -7, 8)
SLOT_OF = {distance: slot for slot, distance in enumerate(SLOTS)} | {-8: 15}
LEAP = 4
HALF = ROWS // 2
VMEM_BYTES = 63 * 1024 * 1024
SPLIT = 3
REACH = 5
SCALE = 1.0 / math.sqrt(B)
FAR_FIRST = (4, 3, 5, 2, 6, 1, 7)

NT = (((1,), (1,)), ((), ()))
TN = (((0,), (0,)), ((), ()))


def sigmoid(value):
    return 0.5 * jnp.tanh(0.5 * value) + 0.5


def dot(a, b, dims=(((1,), (0,)), ((), ()))):
    return lax.dot_general(a, b, dims, preferred_element_type=F32)


def kernel(
    owner_hbm, row_hbm, act_hbm, hist_hbm, masters_ref, atab_hbm, gain_hbm, w_ref,
    dout_hbm,
    att_out, grad_out,
    owner_ref, row_ref, act_ref, hist_ref, atab_ref, gain_ref, dout_ref,
    mslice, w_v, tbl, ids, high, low, high_row, low_row, gacc, g1, x1, xin, hn, startb, invb,
    pd, stq, stkv, qb, kvb, dob, attacc, dqacc, dqs, dkvs, atts, rdq, rdkv, ratt, dqf, gh,
    g2, gin, psum, own, yb, stage, agg, zb, fin,
    loc_s, y_s, y_r, z_s, z_r, id_s, id_r, a1_s, a1_r, q_s, q_r, kv_s, kv_r, do_s, do_r,
    dq_s, dq_r, dkv_s, dkv_r, at_s, at_r, a2_s, a2_r, ry_s, ry_r, ag_s, ag_r, rz_s, rz_r, f_s, f_r,
):
    c = lax.axis_index("ctx")
    t = lax.axis_index("tab")
    x, core = lax.div(c, 2), lax.rem(c, 2)
    z, y = lax.div(t, Y), lax.rem(t, Y)

    def ctx_at(d):
        return lax.rem(c + d, CTX)

    def tab_y(d):
        return z * Y + lax.rem(y + d + Y, Y)

    def z_at(d):
        return lax.rem(z + d + Z, Z)

    def tab_z(d):
        return z_at(d) * Y + y

    def remote(src, dst, ssem, rsem, to_ctx, to_tab):
        return pltpu.make_async_remote_copy(
            src_ref=src, dst_ref=dst, send_sem=ssem, recv_sem=rsem,
            device_id=(to_ctx, to_tab), device_id_type=MESH,
        )

    def got(dst, rsem, ssem):
        remote(dst, dst, ssem, rsem, c, t).wait_recv()

    def sent(src, ssem, rsem):
        remote(src, src, ssem, rsem, c, t).wait_send()

    cp_slice = pltpu.make_async_copy(
        masters_ref.at[:, pl.ds(pl.multiple_of(c * B, B), B)], mslice, loc_s.at[0]
    )
    cp_slice.start()
    cp_ids = []
    for i, (src, dst) in enumerate(((owner_hbm, owner_ref), (row_hbm, row_ref))):
        cp_ids.append(pltpu.make_async_copy(src, dst, loc_s.at[14 + i]))
        cp_ids[-1].start()
    cp_dout = pltpu.make_async_copy(dout_hbm, dout_ref, loc_s.at[16])
    cp_dout.start()
    cp_small = []
    for i, (src, dst) in enumerate(
        (
            (act_hbm, act_ref), (atab_hbm, atab_ref), (hist_hbm, hist_ref), (gain_hbm, gain_ref),
        )
    ):
        cp_small.append(pltpu.make_async_copy(src, dst, loc_s.at[17 + i]))
        cp_small[-1].start()
    cp_w = []
    for h in range(HEADS):
        for part in range(3):
            cp_w.append(
                pltpu.make_async_copy(
                    w_ref.at[:, pl.ds(part * HEADS * B + h * B, B)],
                    w_v.at[h, :, pl.ds(part * B, B)],
                    loc_s.at[2 + 3 * h + part],
                )
            )

    barrier = pltpu.get_barrier_semaphore()
    for d in range(1, LEAP + 1):
        for e in (d, -d):
            pl.semaphore_signal(barrier, inc=1, device_id=(c, tab_z(e)), device_id_type=MESH)
    for d in range(1, Y):
        pl.semaphore_signal(barrier, inc=1, device_id=(c, tab_y(d)), device_id_type=MESH)
    for d in range(1, CTX):
        pl.semaphore_signal(barrier, inc=1, device_id=(ctx_at(d), t), device_id_type=MESH)

    cp_slice.wait()
    tbl[0, 0] = mslice[...].astype(BF16)
    pl.semaphore_wait(barrier, CTX - 1 + Y - 1 + 2 * LEAP)

    half_rows = (pl.ds(0, HALF), pl.ds(HALF, HALF))

    def near_send(e):
        to = SLOT_OF[-e]
        return remote(tbl.at[0, 0], tbl.at[0, to], z_s.at[to], z_r.at[to], c, tab_z(e))

    def far_send(side, f):
        e = f if side == 0 else -f
        src = tbl.at[0, SLOT_OF[-LEAP if side == 0 else LEAP]]
        to = SLOT_OF[-LEAP - f if side == 0 else LEAP + f]
        if f < LEAP:
            return remote(src, tbl.at[0, to], z_s.at[to], z_r.at[to], c, tab_z(e))
        at = half_rows[side]
        return remote(
            src.at[at], tbl.at[0, to, at], z_s.at[15 + side], z_r.at[15 + side], c, tab_z(e)
        )

    def slot_got(to):
        if to < 15:
            got(tbl.at[0, to], z_r.at[to], z_s.at[to])
        else:
            for side in range(2):
                got(tbl.at[0, 15, half_rows[side]], z_r.at[15 + side], z_s.at[15 + side])

    nearest = [e for d in range(LEAP, 0, -1) for e in (d, -d)]
    for e in nearest:
        near_send(e).start()
    for copy in cp_ids:
        copy.wait()
    owner, row = owner_ref[...], row_ref[...]
    ahead = (lax.shift_right_logical(owner, 2) + Z - z) & (Z - 1)
    slot = jnp.where(ahead > Z // 2, 2 * (Z - ahead), jnp.maximum(2 * ahead - 1, 0))
    behind = (y + Y - (owner & (Y - 1))) & (Y - 1)
    ids[c] = jnp.broadcast_to(behind * (Z * ROWS) + slot * ROWS + row, (8, B))

    for d in FAR_FIRST:
        remote(ids.at[c], ids.at[c], id_s.at[d - 1], id_r.at[d - 1], ctx_at(d), t).start()

    def group_send(d, g):
        at = pl.ds(GROUPS * g, GROUPS)
        return remote(
            tbl.at[0, at], tbl.at[d, at], y_s.at[d - 1, g], y_r.at[d - 1, g], c, tab_y(d)
        )

    def group_got(d, g):
        got(tbl.at[d, pl.ds(GROUPS * g, GROUPS)], y_r.at[d - 1, g], y_s.at[d - 1, g])

    def sum_send(d, g):
        return remote(
            psum.at[d, g], yb.at[d - 1, g], ry_s.at[d - 1, g], ry_r.at[d - 1, g], c, tab_y(-d)
        )

    def sum_got(d, g):
        got(yb.at[d - 1, g], ry_r.at[d - 1, g], ry_s.at[d - 1, g])

    def gather_send(slot):
        distance = SLOTS[slot]
        copies = []
        for side in range(2) if slot == 15 else (0,) if distance > 0 else (1,):
            f = abs(distance) - LEAP
            at = half_rows[side] if slot == 15 else pl.ds(0, ROWS)
            copies.append(
                remote(
                    stage.at[slot, at], agg.at[side, f - 1, at],
                    ag_s.at[side, f - 1], ag_r.at[side, f - 1], c, tab_z(f if side == 0 else -f),
                )
            )
        return copies

    def gather_got(side, f):
        at = half_rows[side] if f == LEAP else pl.ds(0, ROWS)
        got(agg.at[side, f - 1, at], ag_r.at[side, f - 1], ag_s.at[side, f - 1])

    def target_send(slot):
        to = SLOT_OF[-SLOTS[slot]]
        return remote(
            stage.at[slot], zb.at[to - 1], rz_s.at[to - 1], rz_r.at[to - 1], c, tab_z(SLOTS[slot])
        )

    def target_got(to):
        got(zb.at[to - 1], rz_r.at[to - 1], rz_s.at[to - 1])

    holder = jnp.where(c >= SPLIT, 1, 0)

    def drain(upto=9):
        for d in range(1, Y):
            for g in range(GROUPS):
                group_send(d, g).wait_send()
                if upto >= 8:
                    sum_send(d, g).wait_send()
        for d in range(1, CTX):
            sent(ids.at[c], id_s.at[d - 1], id_r.at[d - 1])
            if upto >= 3:
                sent(g1.at[0], a1_s.at[d - 1], a1_r.at[d - 1])
            if upto >= 7:
                sent(g2.at[0], a2_s.at[d - 1], a2_r.at[d - 1])
            if upto >= 9:
                sent(fin.at[c], f_s.at[d - 1], f_r.at[d - 1])
        for e in nearest:
            near_send(e).wait_send()
        for side in range(2):
            for f in range(1, LEAP + 1):
                far_send(side, f).wait_send()
        for slot in range(1, Z) if upto >= 8 else ():
            for copy in gather_send(slot) if slot > 2 * LEAP else [target_send(slot)]:
                copy.wait_send()
        for h in range(HEADS):
            for s in range(2):
                need = (c <= SPLIT + REACH - 2) if s == 0 else (c >= SPLIT)

                @pl.when(need & (2 * h + s != c))
                def _():
                    sent(dob.at[0], do_s.at[h, s], do_r.at[0])
                    if upto >= 4:
                        sent(stq.at[h], q_s.at[h, s], q_r.at[0])

            if upto >= 4:
                @pl.when(2 * h + holder != c)
                def _():
                    sent(stkv.at[h], kv_s.at[h], kv_r.at[0])

        for b in range(8) if upto >= 5 else ():
            @pl.when((c != b) & (core == (0 if b < SPLIT else 1)))
            def _():
                sent(dkvs.at[b], dkv_s.at[b], dkv_r.at[0])

            for s in range(2):
                need = b <= SPLIT + REACH - 2 if s == 0 else b >= SPLIT
                if need:
                    @pl.when((c != b) & (core == s))
                    def _():
                        sent(dqs.at[b], dq_s.at[b], dq_r.at[0, 0])
                        sent(atts.at[b], at_s.at[b], at_r.at[0, 0])

    def to_heads(src_of, dst, ssem, rsem, local):
        for r in (2, 1, 3, 0):
            h = lax.rem(x + r, HEADS)
            for s in range(2):
                need = (c <= SPLIT + REACH - 2) if s == 0 else (c >= SPLIT)
                dev = 2 * h + s

                @pl.when(need & (dev != c))
                def _():
                    remote(src_of(h), dst.at[c], ssem.at[h, s], rsem.at[c], dev, t).start()

                @pl.when(need & (dev == c))
                def _():
                    local(h)

    def dout_of(h):
        return dout_ref.at[:, pl.ds(pl.multiple_of(h * B, B), B)]

    def dout_here(h):
        dob[c] = dout_ref[:, pl.ds(pl.multiple_of(h * B, B), B)]

    cp_dout.wait()
    to_heads(dout_of, dob, do_s, do_r, dout_here)
    for copy in cp_w:
        copy.start()

    for copy in cp_small:
        copy.wait()
    actb = jnp.broadcast_to(act_ref[...], (B, B)).T
    for j in range(8):
        block = pl.ds(j * B, B)
        emb = jnp.broadcast_to(atab_ref[0:1, block], (B, B))
        for a in range(1, 8):
            emb = jnp.where(actb == a, atab_ref[a : a + 1, block], emb)
        xin[j] = emb
    h0, h1, h2, h3 = hist_ref[0, 0], hist_ref[0, 1], hist_ref[0, 2], hist_ref[0, 3]
    e0, e1, e2 = h0, h0 + h1, h0 + h1 + h2

    def spans(i, carry):
        p = lax.broadcasted_iota(I32, (B, B), 0) + i * B
        in0, in1, in2 = p < e0, p < e1, p < e2
        startb[i] = jnp.where(in0, 0, jnp.where(in1, e0, jnp.where(in2, e1, e2)))
        length = jnp.where(in0, h0, jnp.where(in1, h1, jnp.where(in2, h2, h3)))
        invb[i] = 1.0 / length.astype(F32)
        return carry

    lax.fori_loop(0, 8, spans, 0)
    for d in range(1, CTX):
        src = ctx_at(CTX - d)
        got(ids.at[src], id_r.at[d - 1], id_s.at[d - 1])

    def spread(j, carry):
        column = jnp.broadcast_to(ids[j, 0:1, :], (B, B)).T
        at = pl.ds(8 * j, 8)
        high[at] = lax.shift_right_logical(column, 8).astype(F32).astype(BF16).reshape(8, 16, B)
        low[at] = (column & (PLANE - 1)).astype(F32).astype(BF16).reshape(8, 16, B)
        line = jnp.broadcast_to(ids[j, 0:1, :], (16, B))
        high_row[j] = lax.shift_right_logical(line, 8).astype(F32).astype(BF16)
        low_row[j] = (line & (PLANE - 1)).astype(F32).astype(BF16)
        gacc[j] = jnp.zeros((B, B), F32)
        return carry

    lax.fori_loop(0, 8, spread, 0)

    one, zero, none = jnp.asarray(1, BF16), jnp.asarray(0, BF16), jnp.asarray(-1, BF16)
    lane = lax.broadcasted_iota(I32, (16, B), 1).astype(F32).astype(BF16)

    def gather_tile(d, g):
        this = jnp.asarray(d * GROUPS + g, BF16)
        wanted = jnp.where(high[...] == this, low[...], none)
        hot = jnp.concatenate(
            [
                jnp.where(wanted == (lane + jnp.asarray(k * B, BF16))[None], one, zero)
                .reshape(8 * B, B)
                for k in range(2)
            ],
            axis=1,
        )
        rows = tbl[d, GROUPS * g : GROUPS * (g + 1)].reshape(PLANE, B)
        gacc[...] = gacc[...] + dot(hot, rows).reshape(8, B, B)

    slot_got(SLOT_OF[-LEAP])
    for f in range(LEAP, 0, -1):
        far_send(0, f).start()
    slot_got(SLOT_OF[LEAP])
    for f in range(LEAP, 0, -1):
        far_send(1, f).start()

    def pass_on(g):
        for to in range(GROUPS * g, GROUPS * (g + 1)):
            if to and abs(SLOTS[to]) != LEAP:
                slot_got(to)
        for d in (2, 1, 3):
            group_send(d, g).start()

    pass_on(0)
    pass_on(1)
    gather_tile(0, 0)
    gather_tile(0, 1)
    for d in (1, 3, 2):
        group_got(d, 0)
        gather_tile(d, 0)
    pass_on(2)
    pass_on(3)
    gather_tile(0, 2)
    gather_tile(0, 3)
    for g in (1, 2, 3):
        for d in (1, 3, 2):
            group_got(d, g)
            gather_tile(d, g)

    for j in range(8):
        g1[j] = gacc[j].astype(BF16)
    for d in FAR_FIRST:
        dst = ctx_at(d)
        remote(g1.at[dst], x1.at[c], a1_s.at[d - 1], a1_r.at[d - 1], dst, t).start()
    x1[c] = g1[c]
    for d in range(1, CTX):
        src = ctx_at(CTX - d)
        got(x1.at[src], a1_r.at[d - 1], a1_s.at[d - 1])

    total = jnp.zeros((B, B), F32)
    for j in range(8):
        value = xin[j] + x1[j].astype(F32)
        xin[j] = value
        total = total + value
    mean = jnp.sum(total, axis=1, keepdims=True) * (1.0 / MODEL)
    total = jnp.zeros((B, B), F32)
    for j in range(8):
        centre = xin[j] - mean
        total = total + centre * centre
    inv_std = lax.rsqrt(jnp.sum(total, axis=1, keepdims=True) * (1.0 / MODEL) + NORM_EPS)
    for j in range(8):
        normed = (xin[j] - mean) * inv_std
        xin[j] = normed
        hn[:, j * B : (j + 1) * B] = (normed * gain_ref[:, j * B : (j + 1) * B]).astype(BF16)
    for copy in cp_w:
        copy.wait()

    def q_of(h):
        return stq.at[h]

    def q_here(h):
        qb[c] = stq[h]

    for r in (2, 1, 3, 0):
        h = lax.rem(x + r, HEADS)
        project = dot(hn[...], w_v[h])
        sig = sigmoid(project)
        pd[h] = sig * (1.0 + project * (1.0 - sig))
        active = (project * sig).astype(BF16)
        stq[h] = active[:, 0:B]
        stkv[h] = active[:, B : 3 * B]
        dev = 2 * h + holder

        @pl.when(dev != c)
        def _():
            remote(stkv.at[h], kvb.at[c], kv_s.at[h], kv_r.at[c], dev, t).start()

        @pl.when(dev == c)
        def _():
            kvb[c] = stkv[h]

        for s in (1, 0):
            need = (c <= SPLIT + REACH - 2) if s == 0 else (c >= SPLIT)
            to = 2 * h + s

            @pl.when(need & (to != c))
            def _():
                remote(stq.at[h], qb.at[c], q_s.at[h, s], q_r.at[c], to, t).start()

            @pl.when(need & (to == c))
            def _():
                q_here(h)

    def send_back(ready, ssem, rsem, dst, block):
        @pl.when(c != block)
        def _():
            remote(ready.at[block], dst, ssem.at[block], rsem, block, t).start()

        @pl.when(c == block)
        def _():
            dst[...] = ready[block]

    def attend(s):
        key_blocks = range(0, SPLIT) if s == 0 else range(SPLIT, 8)
        lowest = key_blocks[0]
        waited = set()
        for kb in key_blocks:
            end = min(kb + REACH, 8)
            n = (end - kb) * B

            @pl.when(c != kb)
            def _():
                got(kvb.at[kb], kv_r.at[kb], kv_s.at[0])

            for b in range(kb, end):
                if b not in waited:
                    waited.add(b)

                    @pl.when(c != b)
                    def _():
                        got(qb.at[b], q_r.at[b], q_s.at[0, 0])
                        got(dob.at[b], do_r.at[b], do_s.at[0, 0])

            queries = qb[kb:end].reshape(n, B)
            cotangent = dob[kb:end].reshape(n, B)
            keys = kvb[kb, :, 0:B]
            values = kvb[kb, :, B : 2 * B]
            raw = dot(queries, keys, NT) * SCALE
            sig = sigmoid(raw)
            inv = invb[kb:end].reshape(n, B)
            k_pos = lax.broadcasted_iota(I32, (n, B), 1) + kb * B
            q_pos = lax.broadcasted_iota(I32, (n, B), 0) + kb * B
            allowed = (k_pos >= startb[kb:end].reshape(n, B)) & (k_pos <= q_pos)
            weights = jnp.where(allowed, raw * sig * inv, 0.0).astype(BF16)
            grad_w = dot(cotangent, values, NT)
            slope = sig * (1.0 + raw * (1.0 - sig))
            grad_raw = jnp.where(allowed, grad_w * slope * (inv * SCALE), 0.0).astype(BF16)
            dkvs[kb, :, 0:B] = dot(grad_raw, queries, TN).astype(BF16)
            dkvs[kb, :, B : 2 * B] = dot(weights, cotangent, TN).astype(BF16)
            send_back(dkvs, dkv_s, dkv_r.at[x], rdkv.at[x], kb)
            dq = dot(grad_raw, keys)
            at = dot(weights, values)
            for b in range(kb, end):
                rows = slice((b - kb) * B, (b - kb + 1) * B)
                first = kb == max(b - REACH + 1, lowest)
                last = kb == min(b, key_blocks[-1])
                dq_b = dq[rows] if first else dqacc[b] + dq[rows]
                at_b = at[rows] if first else attacc[b] + at[rows]
                if last:
                    dqs[b] = dq_b.astype(BF16)
                    send_back(dqs, dq_s, dq_r.at[s, x], rdq.at[s, x], b)
                    atts[b] = at_b.astype(BF16)
                else:
                    dqacc[b] = dq_b
                    attacc[b] = at_b

    for s in range(2):
        @pl.when(core == s)
        def _():
            attend(s)

    both = (c >= SPLIT) & (c <= SPLIT + REACH - 2)
    for r in (0, 1, 3, 2):
        h = lax.rem(x + r, HEADS)

        @pl.when(2 * h + holder != c)
        def _():
            got(rdkv.at[h], dkv_r.at[h], dkv_s.at[0])
            got(rdq.at[holder, h], dq_r.at[holder, h], dq_s.at[0])

        @pl.when(both & (2 * h != c))
        def _():
            got(rdq.at[0, h], dq_r.at[0, h], dq_s.at[0])

        dqf[...] = rdq[holder, h].astype(F32)

        @pl.when(both)
        def _():
            dqf[...] = dqf[...] + rdq[0, h].astype(F32)

        slope = pd[h]
        grad_project = jnp.concatenate(
            [
                (dqf[...] * slope[:, 0:B]).astype(BF16),
                (rdkv[h].astype(F32) * slope[:, B : 3 * B]).astype(BF16),
            ],
            axis=1,
        )
        part = dot(grad_project, w_v[h], NT)
        gh[...] = part if r == 0 else gh[...] + part

    total = jnp.zeros((B, B), F32)
    cross = jnp.zeros((B, B), F32)
    for j in range(8):
        cols = slice(j * B, (j + 1) * B)
        g = gh[:, cols] * gain_ref[:, cols]
        gh[:, cols] = g
        total = total + g
        cross = cross + g * xin[j]
    mean_g = jnp.sum(total, axis=1, keepdims=True) * (1.0 / MODEL)
    mean_c = jnp.sum(cross, axis=1, keepdims=True) * (1.0 / MODEL)
    for j in range(8):
        g = gh[:, j * B : (j + 1) * B]
        g2[j] = (inv_std * (g - mean_g - xin[j] * mean_c)).astype(BF16)

    for d in FAR_FIRST:
        dst = ctx_at(d)
        remote(g2.at[dst], gin.at[c], a2_s.at[d - 1], a2_r.at[d - 1], dst, t).start()
    gin[c] = g2[c]
    for d in range(1, CTX):
        src = ctx_at(CTX - d)
        got(gin.at[src], a2_r.at[d - 1], a2_s.at[d - 1])

    for s in range(2):
        @pl.when(core == s)
        def _():
            for b in range(0, SPLIT + REACH - 1) if s == 0 else range(SPLIT, 8):
                send_back(atts, at_s, at_r.at[s, x], ratt.at[s, x], b)

    sub = lax.broadcasted_iota(I32, (PLANE, B), 0).astype(F32).astype(BF16).reshape(16, 16, B)

    def tile_sum(d, g):
        this = jnp.asarray(d * GROUPS + g, BF16)
        wanted = jnp.where(high_row[...] == this, low_row[...], none)
        hot = jnp.concatenate(
            [jnp.where(sub == wanted[j][None], one, zero).reshape(PLANE, B) for j in range(8)],
            axis=1,
        )
        return dot(hot, gin[...].reshape(8 * B, B))

    for g in (3, 2, 1, 0):
        for d in (2, 1, 3):
            psum[d, g] = tile_sum(d, g).astype(BF16)
            sum_send(d, g).start()
        own[g] = tile_sum(0, g)
    for g in (3, 2, 1, 0):
        value = own[g]
        for d in (1, 3, 2):
            sum_got(d, g)
            value = value + yb[d - 1, g].astype(F32)
        own[g] = value
        for i in range(GROUPS):
            slot = GROUPS * g + i
            if slot and abs(SLOTS[slot]) != LEAP:
                stage[slot] = value[i * ROWS : (i + 1) * ROWS].astype(BF16)
                for copy in gather_send(slot) if slot > 2 * LEAP else [target_send(slot)]:
                    copy.start()
    for side in range(2):
        slot = SLOT_OF[LEAP if side == 0 else -LEAP]
        i = slot % GROUPS
        total = own[slot // GROUPS, i * ROWS : (i + 1) * ROWS, :]
        for f in range(1, LEAP):
            gather_got(side, f)
            total = total + agg[side, f - 1].astype(F32)
        gather_got(side, LEAP)
        stage[slot] = total.astype(BF16)
        at = slice(side * HALF, (side + 1) * HALF)
        stage[slot, at, :] = (total[at] + agg[side, LEAP - 1, at, :].astype(F32)).astype(BF16)
        target_send(slot).start()

    for h in range(HEADS):
        @pl.when(2 * h + holder != c)
        def _():
            got(ratt.at[holder, h], at_r.at[holder, h], at_s.at[0])

        @pl.when(both & (2 * h != c))
        def _():
            got(ratt.at[0, h], at_r.at[0, h], at_s.at[0])

        dqf[...] = ratt[holder, h].astype(F32)

        @pl.when(both)
        def _():
            dqf[...] = dqf[...] + ratt[0, h].astype(F32)

        att_out[:, h * B : (h + 1) * B] = dqf[...].astype(BF16)

    value = own[0, 0:ROWS, :]
    for to in range(1, 2 * LEAP + 1):
        target_got(to)
        value = value + zb[to - 1].astype(F32)

    fin[c] = value.astype(BF16)
    for d in FAR_FIRST:
        remote(fin.at[c], fin.at[c], f_s.at[d - 1], f_r.at[d - 1], ctx_at(d), t).start()
    for d in range(1, CTX):
        src = ctx_at(CTX - d)
        got(fin.at[src], f_r.at[d - 1], f_s.at[d - 1])

    grad_out[...] = fin[...]
    drain()


def adagrad(
    grad_hbm, att_hbm, masters_hbm, accum_hbm, att_out, rg_out, nm_out, na_out,
    grad, rows, accum, rg, nm, na, sem,
):
    copies = [
        pltpu.make_async_copy(src, dst, sem.at[i])
        for i, (src, dst) in enumerate(
            ((grad_hbm, grad), (masters_hbm, rows), (accum_hbm, accum), (att_hbm, att_out))
        )
    ]
    for copy in copies:
        copy.start()
    copies[0].wait()
    total = jnp.zeros((ROWS, B), F32)
    for j in range(8):
        g = grad[j].astype(F32)
        rg[:, j * B : (j + 1) * B] = g
        total = total + g * g
    results = [
        pltpu.make_async_copy(src, dst, sem.at[4 + i])
        for i, (src, dst) in enumerate(((rg, rg_out), (nm, nm_out), (na, na_out)))
    ]
    results[0].start()
    copies[2].wait()
    diagonal = lax.broadcasted_iota(I32, (ROWS, ROWS), 0) == lax.broadcasted_iota(
        I32, (ROWS, ROWS), 1
    )
    before = jnp.sum(jnp.where(diagonal, accum[...], 0.0), axis=1, keepdims=True)
    after = before + jnp.sum(total, axis=1, keepdims=True) * (1.0 / MODEL)
    rate = LEARN_RATE * lax.rsqrt(after)
    copies[1].wait()
    for j in range(8):
        cols = slice(j * B, (j + 1) * B)
        nm[:, cols] = rows[:, cols] - rg[:, cols] * rate
    results[1].start()
    na[...] = jnp.sum(jnp.where(diagonal, after, 0.0), axis=0, keepdims=True)
    results[2].start()
    copies[3].wait()
    for copy in results:
        copy.wait()


def per_device(
    item_owner, item_row, action_id, history_len, masters, row_accum, action_table, norm_gain,
    w_qkv, d_attended,
):
    vmem = pl.BlockSpec(memory_space=pltpu.VMEM)
    hbm = pl.BlockSpec(memory_space=pltpu.HBM)
    dma = pltpu.SemaphoreType.DMA

    def block(*lead, rows=B, cols=B, dtype=BF16):
        return pltpu.VMEM((*lead, rows, cols), dtype)

    scratch = [
        pltpu.VMEM((1, B), I32),
        pltpu.VMEM((1, B), I32),
        pltpu.VMEM((1, B), I32),
        pltpu.SMEM((1, 4), I32),
        pltpu.VMEM((8, MODEL), F32),
        pltpu.VMEM((1, MODEL), F32),
        pltpu.VMEM((B, HEADS * B), BF16),
        pltpu.VMEM((ROWS, B), F32),
        pltpu.VMEM((HEADS, MODEL, 3 * B), BF16),
        block(Y, Z, rows=ROWS),
        block(8, rows=8, dtype=I32),
        block(HEADS * 16, rows=16),
        block(HEADS * 16, rows=16),
        block(8, rows=16),
        block(8, rows=16),
        block(8, dtype=F32),
        block(8),
        block(8),
        block(8, dtype=F32),
        block(cols=MODEL),
        block(8, dtype=I32),
        block(8, dtype=F32),
        block(HEADS, cols=3 * B, dtype=F32),
        block(HEADS),
        block(HEADS, cols=2 * B),
        block(8),
        block(8, cols=2 * B),
        block(8),
        block(8, dtype=F32),
        block(8, dtype=F32),
        block(8),
        block(8, cols=2 * B),
        block(8),
        block(2, HEADS),
        block(HEADS, cols=2 * B),
        block(2, HEADS),
        block(dtype=F32),
        block(cols=MODEL, dtype=F32),
        block(8),
        block(8),
        block(Y, GROUPS, rows=PLANE),
        block(GROUPS, rows=PLANE, dtype=F32),
        block(Y - 1, GROUPS, rows=PLANE),
        block(Z, rows=ROWS),
        block(2, LEAP, rows=ROWS),
        block(2 * LEAP, rows=ROWS),
        block(8, rows=ROWS),
        dma((22,)),
        dma((Y - 1, GROUPS)), dma((Y - 1, GROUPS)),
        dma((Z + 1,)), dma((Z + 1,)),
        dma((7,)), dma((7,)),
        dma((7,)), dma((7,)),
        dma((HEADS, 2)), dma((8,)),
        dma((HEADS,)), dma((8,)),
        dma((HEADS, 2)), dma((8,)),
        dma((8,)), dma((2, HEADS)),
        dma((8,)), dma((HEADS,)),
        dma((8,)), dma((2, HEADS)),
        dma((7,)), dma((7,)),
        dma((Y - 1, GROUPS)), dma((Y - 1, GROUPS)),
        dma((2, LEAP)), dma((2, LEAP)),
        dma((2 * LEAP,)), dma((2 * LEAP,)),
        dma((7,)), dma((7,)),
    ]
    attended, grads = pl.pallas_call(
        kernel,
        out_shape=(
            jax.ShapeDtypeStruct((B, HEADS * B), BF16),
            jax.ShapeDtypeStruct((8, ROWS, B), BF16),
        ),
        in_specs=[hbm] * 9,
        out_specs=(vmem, vmem),
        scratch_shapes=scratch,
        compiler_params=pltpu.CompilerParams(
            collective_id=0, has_side_effects=True, vmem_limit_bytes=VMEM_BYTES
        ),
    )(
        item_owner[:, :, 0], item_row, action_id, history_len, masters, action_table,
        norm_gain[None, :], w_qkv, d_attended[0],
    )
    attended, row_grads, new_masters, new_accum = pl.pallas_call(
        adagrad,
        out_shape=(
            jax.ShapeDtypeStruct((B, HEADS * B), BF16),
            jax.ShapeDtypeStruct((ROWS, MODEL), F32),
            jax.ShapeDtypeStruct((ROWS, MODEL), F32),
            jax.ShapeDtypeStruct((1, ROWS), F32),
        ),
        in_specs=[hbm] * 4,
        out_specs=(hbm, hbm, hbm, hbm),
        scratch_shapes=[
            block(8, rows=ROWS),
            pltpu.VMEM((ROWS, MODEL), F32),
            pltpu.VMEM((1, ROWS), F32),
            pltpu.VMEM((ROWS, MODEL), F32),
            pltpu.VMEM((ROWS, MODEL), F32),
            pltpu.VMEM((1, ROWS), F32),
            dma((7,)),
        ],
        compiler_params=pltpu.CompilerParams(vmem_limit_bytes=VMEM_BYTES),
    )(grads, attended, masters, row_accum[None, :])
    return (attended[None], row_grads, new_masters, new_accum[0])


def solution(mesh):
    in_specs = (
        P("tab", "ctx", None),
        P("tab", "ctx"),
        P("tab", "ctx"),
        P("tab", None),
        P("tab", None),
        P("tab"),
        P(),
        P(),
        P(),
        P("tab", "ctx", None),
    )
    out_specs = (P("tab", "ctx", None), P("tab", None), P("tab", None), P("tab"))
    return jax.shard_map(
        per_device, mesh=mesh, in_specs=in_specs, out_specs=out_specs, check_vma=False
    )
```

```python
import math

import jax
import jax.numpy as jnp
from jax import lax
from jax.experimental import pallas as pl
from jax.experimental.pallas import tpu as pltpu
from jax.sharding import PartitionSpec as P

MESH = pl.DeviceIdType.MESH
F32 = jnp.float32
BF16 = jnp.bfloat16
I32 = jnp.int32

NORM_EPS = 1e-05
LEARN_RATE = 0.1

CTX = 8
Y = 4
B = 128
ROWS = 64
PLANE = Y * ROWS
MODEL = 1024
HEADS = 4
Z = 16
GROUPS = 4
SLOTS = (0, 1, -1, 2, -2, 3, -3, 4, -4, 5, -5, 6, -6, 7, -7, 8)
SLOT_OF = {distance: slot for slot, distance in enumerate(SLOTS)} | {-8: 15}
LEAP = 4
HALF = ROWS // 2
ASKED = 64
VMEM_BYTES = 63 * 1024 * 1024
SPLIT = 3
REACH = 5
SCALE = 1.0 / math.sqrt(B)
FAR_FIRST = (4, 3, 5, 2, 6, 1, 7)

NT = (((1,), (1,)), ((), ()))
TN = (((0,), (0,)), ((), ()))


def sigmoid(value):
    return 0.5 * jnp.tanh(0.5 * value) + 0.5


def dot(a, b, dims=(((1,), (0,)), ((), ()))):
    return lax.dot_general(a, b, dims, preferred_element_type=F32)


def kernel(
    owner_hbm, row_hbm, act_hbm, hist_hbm, masters_ref, atab_hbm, gain_hbm, w_ref,
    dout_hbm,
    att_out, grad_out,
    owner_ref, row_ref, act_ref, hist_ref, atab_ref, gain_ref, dout_ref,
    mslice, w_v, tbl, ids, high, low, high_row, low_row, unpack, wish_out, wishes,
    gacc, picked, x1, xin, hn, startb, invb,
    pd, stq, stkv, qb, kvb, dob, attacc, dqacc, dqs, dkvs, atts, rdq, rdkv, ratt, dqf, gh,
    g2, gin, psum, own, yb, stage, agg, zb, fin,
    loc_s, w_s, w_r, z_s, z_r, id_s, id_r, a1_s, a1_r, q_s, q_r, kv_s, kv_r, do_s, do_r,
    dq_s, dq_r, dkv_s, dkv_r, at_s, at_r, a2_s, a2_r, ry_s, ry_r, ag_s, ag_r, rz_s, rz_r, f_s, f_r,
):
    c = lax.axis_index("ctx")
    t = lax.axis_index("tab")
    x, core = lax.div(c, 2), lax.rem(c, 2)
    z, y = lax.div(t, Y), lax.rem(t, Y)

    def ctx_at(d):
        return lax.rem(c + d, CTX)

    def tab_y(d):
        return z * Y + lax.rem(y + d + Y, Y)

    def z_at(d):
        return lax.rem(z + d + Z, Z)

    def tab_z(d):
        return z_at(d) * Y + y

    def remote(src, dst, ssem, rsem, to_ctx, to_tab):
        return pltpu.make_async_remote_copy(
            src_ref=src, dst_ref=dst, send_sem=ssem, recv_sem=rsem,
            device_id=(to_ctx, to_tab), device_id_type=MESH,
        )

    def got(dst, rsem, ssem):
        remote(dst, dst, ssem, rsem, c, t).wait_recv()

    def sent(src, ssem, rsem):
        remote(src, src, ssem, rsem, c, t).wait_send()

    cp_slice = pltpu.make_async_copy(
        masters_ref.at[:, pl.ds(pl.multiple_of(c * B, B), B)], mslice, loc_s.at[0]
    )
    cp_slice.start()
    cp_ids = []
    for i, (src, dst) in enumerate(((owner_hbm, owner_ref), (row_hbm, row_ref))):
        cp_ids.append(pltpu.make_async_copy(src, dst, loc_s.at[14 + i]))
        cp_ids[-1].start()
    cp_dout = pltpu.make_async_copy(dout_hbm, dout_ref, loc_s.at[16])
    cp_dout.start()
    cp_small = []
    for i, (src, dst) in enumerate(
        (
            (act_hbm, act_ref), (atab_hbm, atab_ref), (hist_hbm, hist_ref), (gain_hbm, gain_ref),
        )
    ):
        cp_small.append(pltpu.make_async_copy(src, dst, loc_s.at[17 + i]))
        cp_small[-1].start()
    cp_w = []
    for h in range(HEADS):
        for part in range(3):
            cp_w.append(
                pltpu.make_async_copy(
                    w_ref.at[:, pl.ds(part * HEADS * B + h * B, B)],
                    w_v.at[h, :, pl.ds(part * B, B)],
                    loc_s.at[2 + 3 * h + part],
                )
            )

    barrier = pltpu.get_barrier_semaphore()
    for d in range(1, LEAP + 1):
        for e in (d, -d):
            pl.semaphore_signal(barrier, inc=1, device_id=(c, tab_z(e)), device_id_type=MESH)
    for e in range(Y):
        for d in range(CTX):
            if e or d:
                pl.semaphore_signal(
                    barrier, inc=1, device_id=(ctx_at(d), tab_y(e)), device_id_type=MESH
                )

    cp_slice.wait()
    tbl[0] = mslice[...].astype(BF16)
    pl.semaphore_wait(barrier, Y * CTX - 1 + 2 * LEAP)

    half_rows = (pl.ds(0, HALF), pl.ds(HALF, HALF))

    def near_send(e):
        to = SLOT_OF[-e]
        return remote(tbl.at[0], tbl.at[to], z_s.at[to], z_r.at[to], c, tab_z(e))

    def far_send(side, f):
        e = f if side == 0 else -f
        src = tbl.at[SLOT_OF[-LEAP if side == 0 else LEAP]]
        to = SLOT_OF[-LEAP - f if side == 0 else LEAP + f]
        if f < LEAP:
            return remote(src, tbl.at[to], z_s.at[to], z_r.at[to], c, tab_z(e))
        at = half_rows[side]
        return remote(
            src.at[at], tbl.at[to, at], z_s.at[15 + side], z_r.at[15 + side], c, tab_z(e)
        )

    def slot_got(to):
        if to < 15:
            got(tbl.at[to], z_r.at[to], z_s.at[to])
        else:
            for side in range(2):
                got(tbl.at[15, half_rows[side]], z_r.at[15 + side], z_s.at[15 + side])

    nearest = [e for d in range(LEAP, 0, -1) for e in (d, -d)]
    for e in nearest:
        near_send(e).start()
    for copy in cp_ids:
        copy.wait()
    owner, row = owner_ref[...], row_ref[...]
    ahead = (lax.shift_right_logical(owner, 2) + Z - z) & (Z - 1)
    slot = jnp.where(ahead > Z // 2, 2 * (Z - ahead), jnp.maximum(2 * ahead - 1, 0))
    asked = slot * ROWS + row
    owner_y = owner & (Y - 1)
    behind = (y + Y - owner_y) & (Y - 1)
    ids[c] = jnp.broadcast_to(behind * (Z * ROWS) + asked, (8, B))

    lane = lax.broadcasted_iota(I32, (B, B), 1)
    sub = lax.broadcasted_iota(I32, (B, B), 0)
    column = jnp.broadcast_to(owner_y * (Z * ROWS) + asked, (B, B)).T
    column_y = lax.shift_right_logical(column, 10)
    asked_of = (column & (Z * ROWS - 1)).astype(F32) + 1.0
    earlier = (column_y == jnp.broadcast_to(owner_y, (B, B))) & (lane < sub)
    rank = jnp.sum(jnp.where(earlier, 1.0, 0.0), axis=1, keepdims=True)
    pos = column_y * ASKED + jnp.broadcast_to(rank, (B, B)).astype(I32)
    for k in range(2):
        unpack[:, k * B : (k + 1) * B] = jnp.where(pos == lane + k * B, 1.0, 0.0).astype(BF16)
    number = lane - core * ASKED
    valid = (number >= 0) & (number < ASKED)
    for e in range(Y):
        mine = valid & (pos == number + ((y + Y - e) & (Y - 1)) * ASKED)
        wish = jnp.sum(jnp.where(mine, asked_of, 0.0), axis=0, keepdims=True)
        wish_out[e] = jnp.broadcast_to(wish, (8, B))

    def wish_send(e, d):
        return remote(
            wish_out.at[e], wishes.at[e, c], w_s.at[e, d], w_r.at[e, c], ctx_at(d), tab_y(-e)
        )

    for e in (2, 1, 3, 0):
        for d in FAR_FIRST + ((0,) if e else ()):
            wish_send(e, d).start()
    wishes[0, c] = wish_out[0]
    for d in FAR_FIRST:
        remote(ids.at[c], ids.at[c], id_s.at[d - 1], id_r.at[d - 1], ctx_at(d), t).start()

    def row_send(e, d):
        to = ctx_at(d)
        at = pl.ds(pl.multiple_of(lax.rem(to, 2) * ASKED, ASKED), ASKED)
        return remote(
            picked.at[e * 4 + lax.div(to, 2), at],
            x1.at[c, pl.ds(pl.multiple_of(y * ASKED, ASKED), ASKED)],
            a1_s.at[e, d], a1_r.at[e, c], to, tab_y(e),
        )

    def row_got(e, src):
        at = pl.ds(pl.multiple_of(((y + Y - e) & (Y - 1)) * ASKED, ASKED), ASKED)
        got(x1.at[src, at], a1_r.at[e, src], a1_s.at[0, 0])

    def sum_send(d, g):
        return remote(
            psum.at[d, g], yb.at[d - 1, g], ry_s.at[d - 1, g], ry_r.at[d - 1, g], c, tab_y(-d)
        )

    def sum_got(d, g):
        got(yb.at[d - 1, g], ry_r.at[d - 1, g], ry_s.at[d - 1, g])

    def gather_send(slot):
        distance = SLOTS[slot]
        copies = []
        for side in range(2) if slot == 15 else (0,) if distance > 0 else (1,):
            f = abs(distance) - LEAP
            at = half_rows[side] if slot == 15 else pl.ds(0, ROWS)
            copies.append(
                remote(
                    stage.at[slot, at], agg.at[side, f - 1, at],
                    ag_s.at[side, f - 1], ag_r.at[side, f - 1], c, tab_z(f if side == 0 else -f),
                )
            )
        return copies

    def gather_got(side, f):
        at = half_rows[side] if f == LEAP else pl.ds(0, ROWS)
        got(agg.at[side, f - 1, at], ag_r.at[side, f - 1], ag_s.at[side, f - 1])

    def target_send(slot):
        to = SLOT_OF[-SLOTS[slot]]
        return remote(
            stage.at[slot], zb.at[to - 1], rz_s.at[to - 1], rz_r.at[to - 1], c, tab_z(SLOTS[slot])
        )

    def target_got(to):
        got(zb.at[to - 1], rz_r.at[to - 1], rz_s.at[to - 1])

    holder = jnp.where(c >= SPLIT, 1, 0)

    def drain(upto=9):
        for d in range(1, Y):
            for g in range(GROUPS):
                if upto >= 8:
                    sum_send(d, g).wait_send()
        for d in range(1, CTX):
            sent(ids.at[c], id_s.at[d - 1], id_r.at[d - 1])
            if upto >= 7:
                sent(g2.at[0], a2_s.at[d - 1], a2_r.at[d - 1])
            if upto >= 9:
                sent(fin.at[c], f_s.at[d - 1], f_r.at[d - 1])
        for e in nearest:
            near_send(e).wait_send()
        for e in range(Y):
            for d in range(CTX):
                if e or d:
                    wish_send(e, d).wait_send()
                    if upto >= 3:
                        row_send(e, d).wait_send()
        for side in range(2):
            for f in range(1, LEAP + 1):
                far_send(side, f).wait_send()
        for slot in range(1, Z) if upto >= 8 else ():
            for copy in gather_send(slot) if slot > 2 * LEAP else [target_send(slot)]:
                copy.wait_send()
        for h in range(HEADS):
            for s in range(2):
                need = (c <= SPLIT + REACH - 2) if s == 0 else (c >= SPLIT)

                @pl.when(need & (2 * h + s != c))
                def _():
                    sent(dob.at[0], do_s.at[h, s], do_r.at[0])
                    if upto >= 4:
                        sent(stq.at[h], q_s.at[h, s], q_r.at[0])

            if upto >= 4:
                @pl.when(2 * h + holder != c)
                def _():
                    sent(stkv.at[h], kv_s.at[h], kv_r.at[0])

        for b in range(8) if upto >= 5 else ():
            @pl.when((c != b) & (core == (0 if b < SPLIT else 1)))
            def _():
                sent(dkvs.at[b], dkv_s.at[b], dkv_r.at[0])

            for s in range(2):
                need = b <= SPLIT + REACH - 2 if s == 0 else b >= SPLIT
                if need:
                    @pl.when((c != b) & (core == s))
                    def _():
                        sent(dqs.at[b], dq_s.at[b], dq_r.at[0, 0])
                        sent(atts.at[b], at_s.at[b], at_r.at[0, 0])

    def to_heads(src_of, dst, ssem, rsem, local):
        for r in (2, 1, 3, 0):
            h = lax.rem(x + r, HEADS)
            for s in range(2):
                need = (c <= SPLIT + REACH - 2) if s == 0 else (c >= SPLIT)
                dev = 2 * h + s

                @pl.when(need & (dev != c))
                def _():
                    remote(src_of(h), dst.at[c], ssem.at[h, s], rsem.at[c], dev, t).start()

                @pl.when(need & (dev == c))
                def _():
                    local(h)

    def dout_of(h):
        return dout_ref.at[:, pl.ds(pl.multiple_of(h * B, B), B)]

    def dout_here(h):
        dob[c] = dout_ref[:, pl.ds(pl.multiple_of(h * B, B), B)]

    cp_dout.wait()
    to_heads(dout_of, dob, do_s, do_r, dout_here)
    for copy in cp_w:
        copy.start()

    slot_got(SLOT_OF[-LEAP])
    for f in range(LEAP, 0, -1):
        far_send(0, f).start()
    slot_got(SLOT_OF[LEAP])
    for f in range(LEAP, 0, -1):
        far_send(1, f).start()

    for copy in cp_small:
        copy.wait()
    actb = jnp.broadcast_to(act_ref[...], (B, B)).T
    for j in range(8):
        block = pl.ds(j * B, B)
        emb = jnp.broadcast_to(atab_ref[0:1, block], (B, B))
        for a in range(1, 8):
            emb = jnp.where(actb == a, atab_ref[a : a + 1, block], emb)
        xin[j] = emb
    h0, h1, h2, h3 = hist_ref[0, 0], hist_ref[0, 1], hist_ref[0, 2], hist_ref[0, 3]
    e0, e1, e2 = h0, h0 + h1, h0 + h1 + h2

    def spans(i, carry):
        p = lax.broadcasted_iota(I32, (B, B), 0) + i * B
        in0, in1, in2 = p < e0, p < e1, p < e2
        startb[i] = jnp.where(in0, 0, jnp.where(in1, e0, jnp.where(in2, e1, e2)))
        length = jnp.where(in0, h0, jnp.where(in1, h1, jnp.where(in2, h2, h3)))
        invb[i] = 1.0 / length.astype(F32)
        return carry

    lax.fori_loop(0, 8, spans, 0)
    for d in range(1, CTX):
        src = ctx_at(CTX - d)
        got(ids.at[src], id_r.at[d - 1], id_s.at[d - 1])

    def spread(j, carry):
        line = jnp.broadcast_to(ids[j, 0:1, :], (16, B))
        high_row[j] = lax.shift_right_logical(line, 8).astype(F32).astype(BF16)
        low_row[j] = (line & (PLANE - 1)).astype(F32).astype(BF16)
        return carry

    lax.fori_loop(0, 8, spread, 0)

    for e in range(Y):
        for d in range(CTX):
            if e or d:
                src = ctx_at(CTX - d)
                got(wishes.at[e, src], w_r.at[e, src], w_s.at[0, 0])

    def spread_wish(i, carry):
        e, chip = lax.div(i, 4), lax.rem(i, 4)
        line = wishes[e, 2 * chip, 0:1, :] + wishes[e, 2 * chip + 1, 0:1, :]
        wish = jnp.broadcast_to(line, (B, B)).T.astype(I32) - 1
        at = pl.ds(8 * i, 8)
        high[at] = lax.shift_right_arithmetic(wish, 8).astype(F32).astype(BF16).reshape(8, 16, B)
        low[at] = (wish & (PLANE - 1)).astype(F32).astype(BF16).reshape(8, 16, B)
        return carry

    lax.fori_loop(0, 16, spread_wish, 0)

    one, zero, none = jnp.asarray(1, BF16), jnp.asarray(0, BF16), jnp.asarray(-1, BF16)
    lane16 = lax.broadcasted_iota(I32, (16, B), 1).astype(F32).astype(BF16)

    def pick(e, g):
        at = slice(32 * e, 32 * (e + 1))
        wanted = jnp.where(high[at] == jnp.asarray(g, BF16), low[at], none)
        hot = jnp.concatenate(
            [
                jnp.where(wanted == (lane16 + jnp.asarray(k * B, BF16))[None], one, zero)
                .reshape(4 * B, B)
                for k in range(2)
            ],
            axis=1,
        )
        rows = tbl[GROUPS * g : GROUPS * (g + 1)].reshape(PLANE, B)
        return dot(hot, rows).reshape(4, B, B)

    for g in range(GROUPS):
        for to in range(GROUPS * g, GROUPS * (g + 1)):
            if to and abs(SLOTS[to]) != LEAP:
                slot_got(to)
        for e in (2, 1, 3, 0):
            at = slice(4 * e, 4 * (e + 1))
            found = pick(e, g) if g == 0 else gacc[at] + pick(e, g)
            if g < GROUPS - 1:
                gacc[at] = found
            else:
                picked[at] = found.astype(BF16)
                for d in FAR_FIRST + ((0,) if e else ()):
                    row_send(e, d).start()
    here = pl.ds(pl.multiple_of(core * ASKED, ASKED), ASKED)
    x1[c, pl.ds(pl.multiple_of(y * ASKED, ASKED), ASKED)] = picked[x, here]
    for e in (0, 1, 3, 2):
        for d in range(CTX):
            if e or d:
                row_got(e, ctx_at(CTX - d))

    total = jnp.zeros((B, B), F32)
    for j in range(8):
        value = xin[j] + dot(unpack[...], x1[j])
        xin[j] = value
        total = total + value
    mean = jnp.sum(total, axis=1, keepdims=True) * (1.0 / MODEL)
    total = jnp.zeros((B, B), F32)
    for j in range(8):
        centre = xin[j] - mean
        total = total + centre * centre
    inv_std = lax.rsqrt(jnp.sum(total, axis=1, keepdims=True) * (1.0 / MODEL) + NORM_EPS)
    for j in range(8):
        normed = (xin[j] - mean) * inv_std
        xin[j] = normed
        hn[:, j * B : (j + 1) * B] = (normed * gain_ref[:, j * B : (j + 1) * B]).astype(BF16)
    for copy in cp_w:
        copy.wait()

    def q_of(h):
        return stq.at[h]

    def q_here(h):
        qb[c] = stq[h]

    for r in (2, 1, 3, 0):
        h = lax.rem(x + r, HEADS)
        project = dot(hn[...], w_v[h])
        sig = sigmoid(project)
        pd[h] = sig * (1.0 + project * (1.0 - sig))
        active = (project * sig).astype(BF16)
        stq[h] = active[:, 0:B]
        stkv[h] = active[:, B : 3 * B]
        dev = 2 * h + holder

        @pl.when(dev != c)
        def _():
            remote(stkv.at[h], kvb.at[c], kv_s.at[h], kv_r.at[c], dev, t).start()

        @pl.when(dev == c)
        def _():
            kvb[c] = stkv[h]

        for s in (1, 0):
            need = (c <= SPLIT + REACH - 2) if s == 0 else (c >= SPLIT)
            to = 2 * h + s

            @pl.when(need & (to != c))
            def _():
                remote(stq.at[h], qb.at[c], q_s.at[h, s], q_r.at[c], to, t).start()

            @pl.when(need & (to == c))
            def _():
                q_here(h)

    def send_back(ready, ssem, rsem, dst, block):
        @pl.when(c != block)
        def _():
            remote(ready.at[block], dst, ssem.at[block], rsem, block, t).start()

        @pl.when(c == block)
        def _():
            dst[...] = ready[block]

    def attend(s):
        key_blocks = range(0, SPLIT) if s == 0 else range(SPLIT, 8)
        lowest = key_blocks[0]
        waited = set()
        for kb in key_blocks:
            end = min(kb + REACH, 8)
            n = (end - kb) * B

            @pl.when(c != kb)
            def _():
                got(kvb.at[kb], kv_r.at[kb], kv_s.at[0])

            for b in range(kb, end):
                if b not in waited:
                    waited.add(b)

                    @pl.when(c != b)
                    def _():
                        got(qb.at[b], q_r.at[b], q_s.at[0, 0])
                        got(dob.at[b], do_r.at[b], do_s.at[0, 0])

            queries = qb[kb:end].reshape(n, B)
            cotangent = dob[kb:end].reshape(n, B)
            keys = kvb[kb, :, 0:B]
            values = kvb[kb, :, B : 2 * B]
            raw = dot(queries, keys, NT) * SCALE
            sig = sigmoid(raw)
            inv = invb[kb:end].reshape(n, B)
            k_pos = lax.broadcasted_iota(I32, (n, B), 1) + kb * B
            q_pos = lax.broadcasted_iota(I32, (n, B), 0) + kb * B
            allowed = (k_pos >= startb[kb:end].reshape(n, B)) & (k_pos <= q_pos)
            weights = jnp.where(allowed, raw * sig * inv, 0.0).astype(BF16)
            grad_w = dot(cotangent, values, NT)
            slope = sig * (1.0 + raw * (1.0 - sig))
            grad_raw = jnp.where(allowed, grad_w * slope * (inv * SCALE), 0.0).astype(BF16)
            dkvs[kb, :, 0:B] = dot(grad_raw, queries, TN).astype(BF16)
            dkvs[kb, :, B : 2 * B] = dot(weights, cotangent, TN).astype(BF16)
            send_back(dkvs, dkv_s, dkv_r.at[x], rdkv.at[x], kb)
            dq = dot(grad_raw, keys)
            at = dot(weights, values)
            for b in range(kb, end):
                rows = slice((b - kb) * B, (b - kb + 1) * B)
                first = kb == max(b - REACH + 1, lowest)
                last = kb == min(b, key_blocks[-1])
                dq_b = dq[rows] if first else dqacc[b] + dq[rows]
                at_b = at[rows] if first else attacc[b] + at[rows]
                if last:
                    dqs[b] = dq_b.astype(BF16)
                    send_back(dqs, dq_s, dq_r.at[s, x], rdq.at[s, x], b)
                    atts[b] = at_b.astype(BF16)
                else:
                    dqacc[b] = dq_b
                    attacc[b] = at_b

    for s in range(2):
        @pl.when(core == s)
        def _():
            attend(s)

    both = (c >= SPLIT) & (c <= SPLIT + REACH - 2)
    for r in (0, 1, 3, 2):
        h = lax.rem(x + r, HEADS)

        @pl.when(2 * h + holder != c)
        def _():
            got(rdkv.at[h], dkv_r.at[h], dkv_s.at[0])
            got(rdq.at[holder, h], dq_r.at[holder, h], dq_s.at[0])

        @pl.when(both & (2 * h != c))
        def _():
            got(rdq.at[0, h], dq_r.at[0, h], dq_s.at[0])

        dqf[...] = rdq[holder, h].astype(F32)

        @pl.when(both)
        def _():
            dqf[...] = dqf[...] + rdq[0, h].astype(F32)

        slope = pd[h]
        grad_project = jnp.concatenate(
            [
                (dqf[...] * slope[:, 0:B]).astype(BF16),
                (rdkv[h].astype(F32) * slope[:, B : 3 * B]).astype(BF16),
            ],
            axis=1,
        )
        part = dot(grad_project, w_v[h], NT)
        gh[...] = part if r == 0 else gh[...] + part

    total = jnp.zeros((B, B), F32)
    cross = jnp.zeros((B, B), F32)
    for j in range(8):
        cols = slice(j * B, (j + 1) * B)
        g = gh[:, cols] * gain_ref[:, cols]
        gh[:, cols] = g
        total = total + g
        cross = cross + g * xin[j]
    mean_g = jnp.sum(total, axis=1, keepdims=True) * (1.0 / MODEL)
    mean_c = jnp.sum(cross, axis=1, keepdims=True) * (1.0 / MODEL)
    for j in range(8):
        g = gh[:, j * B : (j + 1) * B]
        g2[j] = (inv_std * (g - mean_g - xin[j] * mean_c)).astype(BF16)

    for d in FAR_FIRST:
        dst = ctx_at(d)
        remote(g2.at[dst], gin.at[c], a2_s.at[d - 1], a2_r.at[d - 1], dst, t).start()
    gin[c] = g2[c]
    for d in range(1, CTX):
        src = ctx_at(CTX - d)
        got(gin.at[src], a2_r.at[d - 1], a2_s.at[d - 1])

    for s in range(2):
        @pl.when(core == s)
        def _():
            for b in range(0, SPLIT + REACH - 1) if s == 0 else range(SPLIT, 8):
                send_back(atts, at_s, at_r.at[s, x], ratt.at[s, x], b)

    sub16 = lax.broadcasted_iota(I32, (PLANE, B), 0).astype(F32).astype(BF16).reshape(16, 16, B)

    def tile_sum(d, g):
        this = jnp.asarray(d * GROUPS + g, BF16)
        wanted = jnp.where(high_row[...] == this, low_row[...], none)
        hot = jnp.concatenate(
            [jnp.where(sub16 == wanted[j][None], one, zero).reshape(PLANE, B) for j in range(8)],
            axis=1,
        )
        return dot(hot, gin[...].reshape(8 * B, B))

    for g in (3, 2, 1, 0):
        for d in (2, 1, 3):
            psum[d, g] = tile_sum(d, g).astype(BF16)
            sum_send(d, g).start()
        own[g] = tile_sum(0, g)
    for g in (3, 2, 1, 0):
        value = own[g]
        for d in (1, 3, 2):
            sum_got(d, g)
            value = value + yb[d - 1, g].astype(F32)
        own[g] = value
        for i in range(GROUPS):
            slot = GROUPS * g + i
            if slot and abs(SLOTS[slot]) != LEAP:
                stage[slot] = value[i * ROWS : (i + 1) * ROWS].astype(BF16)
                for copy in gather_send(slot) if slot > 2 * LEAP else [target_send(slot)]:
                    copy.start()
    for side in range(2):
        slot = SLOT_OF[LEAP if side == 0 else -LEAP]
        i = slot % GROUPS
        total = own[slot // GROUPS, i * ROWS : (i + 1) * ROWS, :]
        for f in range(1, LEAP):
            gather_got(side, f)
            total = total + agg[side, f - 1].astype(F32)
        gather_got(side, LEAP)
        stage[slot] = total.astype(BF16)
        at = slice(side * HALF, (side + 1) * HALF)
        stage[slot, at, :] = (total[at] + agg[side, LEAP - 1, at, :].astype(F32)).astype(BF16)
        target_send(slot).start()

    for h in range(HEADS):
        @pl.when(2 * h + holder != c)
        def _():
            got(ratt.at[holder, h], at_r.at[holder, h], at_s.at[0])

        @pl.when(both & (2 * h != c))
        def _():
            got(ratt.at[0, h], at_r.at[0, h], at_s.at[0])

        dqf[...] = ratt[holder, h].astype(F32)

        @pl.when(both)
        def _():
            dqf[...] = dqf[...] + ratt[0, h].astype(F32)

        att_out[:, h * B : (h + 1) * B] = dqf[...].astype(BF16)

    value = own[0, 0:ROWS, :]
    for to in range(1, 2 * LEAP + 1):
        target_got(to)
        value = value + zb[to - 1].astype(F32)

    fin[c] = value.astype(BF16)
    for d in FAR_FIRST:
        remote(fin.at[c], fin.at[c], f_s.at[d - 1], f_r.at[d - 1], ctx_at(d), t).start()
    for d in range(1, CTX):
        src = ctx_at(CTX - d)
        got(fin.at[src], f_r.at[d - 1], f_s.at[d - 1])

    grad_out[...] = fin[...]
    drain()


def adagrad(grad, att, rows, accum, att_out, rg_out, nm_out, na_out):
    att_out[...] = att[...]
    total = jnp.zeros((ROWS, B), F32)
    for j in range(8):
        g = grad[j].astype(F32)
        rg_out[:, j * B : (j + 1) * B] = g
        total = total + g * g
    diagonal = lax.broadcasted_iota(I32, (ROWS, ROWS), 0) == lax.broadcasted_iota(
        I32, (ROWS, ROWS), 1
    )
    before = jnp.sum(jnp.where(diagonal, accum[...], 0.0), axis=1, keepdims=True)
    after = before + jnp.sum(total, axis=1, keepdims=True) * (1.0 / MODEL)
    rate = LEARN_RATE * lax.rsqrt(after)
    for j in range(8):
        cols = slice(j * B, (j + 1) * B)
        nm_out[:, cols] = rows[:, cols] - grad[j].astype(F32) * rate
    na_out[...] = jnp.sum(jnp.where(diagonal, after, 0.0), axis=0, keepdims=True)


def per_device(
    item_owner, item_row, action_id, history_len, masters, row_accum, action_table, norm_gain,
    w_qkv, d_attended,
):
    vmem = pl.BlockSpec(memory_space=pltpu.VMEM)
    hbm = pl.BlockSpec(memory_space=pltpu.HBM)
    dma = pltpu.SemaphoreType.DMA

    def block(*lead, rows=B, cols=B, dtype=BF16):
        return pltpu.VMEM((*lead, rows, cols), dtype)

    scratch = [
        pltpu.VMEM((1, B), I32),
        pltpu.VMEM((1, B), I32),
        pltpu.VMEM((1, B), I32),
        pltpu.SMEM((1, 4), I32),
        pltpu.VMEM((8, MODEL), F32),
        pltpu.VMEM((1, MODEL), F32),
        pltpu.VMEM((B, HEADS * B), BF16),
        pltpu.VMEM((ROWS, B), F32),
        pltpu.VMEM((HEADS, MODEL, 3 * B), BF16),
        block(Z, rows=ROWS),
        block(8, rows=8, dtype=I32),
        block(128, rows=16),
        block(128, rows=16),
        block(8, rows=16),
        block(8, rows=16),
        block(cols=2 * B),
        block(Y, rows=8, dtype=F32),
        block(Y, CTX, rows=8, dtype=F32),
        block(16, dtype=F32),
        block(16),
        block(8, rows=Y * ASKED),
        block(8, dtype=F32),
        block(cols=MODEL),
        block(8, dtype=I32),
        block(8, dtype=F32),
        block(HEADS, cols=3 * B, dtype=F32),
        block(HEADS),
        block(HEADS, cols=2 * B),
        block(8),
        block(8, cols=2 * B),
        block(8),
        block(8, dtype=F32),
        block(8, dtype=F32),
        block(8),
        block(8, cols=2 * B),
        block(8),
        block(2, HEADS),
        block(HEADS, cols=2 * B),
        block(2, HEADS),
        block(dtype=F32),
        block(cols=MODEL, dtype=F32),
        block(8),
        block(8),
        block(Y, GROUPS, rows=PLANE),
        block(GROUPS, rows=PLANE, dtype=F32),
        block(Y - 1, GROUPS, rows=PLANE),
        block(Z, rows=ROWS),
        block(2, LEAP, rows=ROWS),
        block(2 * LEAP, rows=ROWS),
        block(8, rows=ROWS),
        dma((22,)),
        dma((Y, CTX)), dma((Y, CTX)),
        dma((Z + 1,)), dma((Z + 1,)),
        dma((7,)), dma((7,)),
        dma((Y, CTX)), dma((Y, CTX)),
        dma((HEADS, 2)), dma((8,)),
        dma((HEADS,)), dma((8,)),
        dma((HEADS, 2)), dma((8,)),
        dma((8,)), dma((2, HEADS)),
        dma((8,)), dma((HEADS,)),
        dma((8,)), dma((2, HEADS)),
        dma((7,)), dma((7,)),
        dma((Y - 1, GROUPS)), dma((Y - 1, GROUPS)),
        dma((2, LEAP)), dma((2, LEAP)),
        dma((2 * LEAP,)), dma((2 * LEAP,)),
        dma((7,)), dma((7,)),
    ]
    attended, grads = pl.pallas_call(
        kernel,
        out_shape=(
            jax.ShapeDtypeStruct((B, HEADS * B), BF16),
            jax.ShapeDtypeStruct((8, ROWS, B), BF16),
        ),
        in_specs=[hbm] * 9,
        out_specs=(vmem, vmem),
        scratch_shapes=scratch,
        compiler_params=pltpu.CompilerParams(
            collective_id=0, has_side_effects=True, vmem_limit_bytes=VMEM_BYTES
        ),
    )(
        item_owner[:, :, 0], item_row, action_id, history_len, masters, action_table,
        norm_gain[None, :], w_qkv, d_attended[0],
    )
    attended, row_grads, new_masters, new_accum = pl.pallas_call(
        adagrad,
        out_shape=(
            jax.ShapeDtypeStruct((B, HEADS * B), BF16),
            jax.ShapeDtypeStruct((ROWS, MODEL), F32),
            jax.ShapeDtypeStruct((ROWS, MODEL), F32),
            jax.ShapeDtypeStruct((1, ROWS), F32),
        ),
        in_specs=[vmem] * 4,
        out_specs=(vmem, vmem, vmem, vmem),
        compiler_params=pltpu.CompilerParams(vmem_limit_bytes=VMEM_BYTES),
    )(grads, attended, masters, row_accum[None, :])
    return (attended[None], row_grads, new_masters, new_accum[0])


def solution(mesh):
    in_specs = (
        P("tab", "ctx", None),
        P("tab", "ctx"),
        P("tab", "ctx"),
        P("tab", None),
        P("tab", None),
        P("tab"),
        P(),
        P(),
        P(),
        P("tab", "ctx", None),
    )
    out_specs = (P("tab", "ctx", None), P("tab", None), P("tab", None), P("tab"))
    return jax.shard_map(
        per_device, mesh=mesh, in_specs=in_specs, out_specs=out_specs, check_vma=False
    )
```

```python
import math

import jax
import jax.numpy as jnp
from jax import lax
from jax.experimental import pallas as pl
from jax.experimental.pallas import tpu as pltpu
from jax.sharding import PartitionSpec as P

MESH = pl.DeviceIdType.MESH
F32 = jnp.float32
BF16 = jnp.bfloat16
I32 = jnp.int32

NORM_EPS = 1e-05
LEARN_RATE = 0.1

CTX = 8
Y = 4
B = 128
ROWS = 64
PLANE = Y * ROWS
MODEL = 1024
HEADS = 4
Z = 16
GROUPS = 4
SLOTS = (0, 1, -1, 2, -2, 3, -3, 4, -4, 5, -5, 6, -6, 7, -7, 8)
SLOT_OF = {distance: slot for slot, distance in enumerate(SLOTS)} | {-8: 15}
LEAP = 4
HALF = ROWS // 2
ASKED = 64
VMEM_BYTES = 63 * 1024 * 1024
SPLIT = 3
REACH = 5
SCALE = 1.0 / math.sqrt(B)
FAR_FIRST = (4, 3, 5, 2, 6, 1, 7)

NT = (((1,), (1,)), ((), ()))
TN = (((0,), (0,)), ((), ()))


def sigmoid(value):
    return 0.5 * jnp.tanh(0.5 * value) + 0.5


def dot(a, b, dims=(((1,), (0,)), ((), ()))):
    return lax.dot_general(a, b, dims, preferred_element_type=F32)


def kernel(
    owner_hbm, row_hbm, act_hbm, hist_hbm, masters_ref, atab_hbm, gain_hbm, w_ref,
    dout_hbm,
    att_out, grad_out,
    owner_ref, row_ref, act_ref, hist_ref, atab_ref, gain_ref, dout_ref,
    mslice, w_v, tbl, high, low, high_row, low_row, unpack, pack, wish_out, wishes,
    gacc, picked, x1, xin, hn, startb, invb,
    pd, stq, stkv, qb, kvb, dob, attacc, dqacc, dqs, dkvs, atts, rdq, rdkv, ratt, dqf, gh,
    g2, packed, gin, own, stage, agg, zb, fin,
    loc_s, w_s, w_r, z_s, z_r, a1_s, a1_r, q_s, q_r, kv_s, kv_r, do_s, do_r,
    dq_s, dq_r, dkv_s, dkv_r, at_s, at_r, a2_s, a2_r, ag_s, ag_r, rz_s, rz_r, f_s, f_r,
):
    c = lax.axis_index("ctx")
    t = lax.axis_index("tab")
    x, core = lax.div(c, 2), lax.rem(c, 2)
    z, y = lax.div(t, Y), lax.rem(t, Y)

    def ctx_at(d):
        return lax.rem(c + d, CTX)

    def tab_y(d):
        return z * Y + lax.rem(y + d + Y, Y)

    def z_at(d):
        return lax.rem(z + d + Z, Z)

    def tab_z(d):
        return z_at(d) * Y + y

    def remote(src, dst, ssem, rsem, to_ctx, to_tab):
        return pltpu.make_async_remote_copy(
            src_ref=src, dst_ref=dst, send_sem=ssem, recv_sem=rsem,
            device_id=(to_ctx, to_tab), device_id_type=MESH,
        )

    def got(dst, rsem, ssem):
        remote(dst, dst, ssem, rsem, c, t).wait_recv()

    def sent(src, ssem, rsem):
        remote(src, src, ssem, rsem, c, t).wait_send()

    cp_slice = pltpu.make_async_copy(
        masters_ref.at[:, pl.ds(pl.multiple_of(c * B, B), B)], mslice, loc_s.at[0]
    )
    cp_slice.start()

    barrier = pltpu.get_barrier_semaphore()
    for d in range(LEAP, 0, -1):
        for e in (d, -d):
            pl.semaphore_signal(barrier, inc=1, device_id=(c, tab_z(e)), device_id_type=MESH)
    for e in (2, 1, 3, 0):
        for d in FAR_FIRST + ((0,) if e else ()):
            pl.semaphore_signal(
                barrier, inc=1, device_id=(ctx_at(d), tab_y(e)), device_id_type=MESH
            )

    cp_ids = []
    for i, (src, dst) in enumerate(((owner_hbm, owner_ref), (row_hbm, row_ref))):
        cp_ids.append(pltpu.make_async_copy(src, dst, loc_s.at[14 + i]))
        cp_ids[-1].start()
    cp_dout = pltpu.make_async_copy(dout_hbm, dout_ref, loc_s.at[16])
    cp_dout.start()
    cp_small = []
    for i, (src, dst) in enumerate(
        (
            (act_hbm, act_ref), (atab_hbm, atab_ref), (hist_hbm, hist_ref), (gain_hbm, gain_ref),
        )
    ):
        cp_small.append(pltpu.make_async_copy(src, dst, loc_s.at[17 + i]))
        cp_small[-1].start()
    cp_w = []
    for h in range(HEADS):
        for part in range(3):
            cp_w.append(
                pltpu.make_async_copy(
                    w_ref.at[:, pl.ds(part * HEADS * B + h * B, B)],
                    w_v.at[h, :, pl.ds(part * B, B)],
                    loc_s.at[2 + 3 * h + part],
                )
            )

    cp_slice.wait()
    tbl[0] = mslice[...].astype(BF16)
    pl.semaphore_wait(barrier, Y * CTX - 1 + 2 * LEAP)

    half_rows = (pl.ds(0, HALF), pl.ds(HALF, HALF))

    def near_send(e):
        to = SLOT_OF[-e]
        return remote(tbl.at[0], tbl.at[to], z_s.at[to], z_r.at[to], c, tab_z(e))

    def far_send(side, f):
        e = f if side == 0 else -f
        src = tbl.at[SLOT_OF[-LEAP if side == 0 else LEAP]]
        to = SLOT_OF[-LEAP - f if side == 0 else LEAP + f]
        if f < LEAP:
            return remote(src, tbl.at[to], z_s.at[to], z_r.at[to], c, tab_z(e))
        at = half_rows[side]
        return remote(
            src.at[at], tbl.at[to, at], z_s.at[15 + side], z_r.at[15 + side], c, tab_z(e)
        )

    def slot_got(to):
        if to < 15:
            got(tbl.at[to], z_r.at[to], z_s.at[to])
        else:
            for side in range(2):
                got(tbl.at[15, half_rows[side]], z_r.at[15 + side], z_s.at[15 + side])

    nearest = [e for d in range(LEAP, 0, -1) for e in (d, -d)]
    for e in nearest:
        near_send(e).start()
    for copy in cp_ids:
        copy.wait()
    owner, row = owner_ref[...], row_ref[...]
    ahead = (lax.shift_right_logical(owner, 2) + Z - z) & (Z - 1)
    slot = jnp.where(ahead > Z // 2, 2 * (Z - ahead), jnp.maximum(2 * ahead - 1, 0))
    asked = slot * ROWS + row
    owner_y = owner & (Y - 1)

    lane = lax.broadcasted_iota(I32, (B, B), 1)
    sub = lax.broadcasted_iota(I32, (B, B), 0)
    column = jnp.broadcast_to(owner_y * (Z * ROWS) + asked, (B, B)).T
    column_y = lax.shift_right_logical(column, 10)
    asked_of = (column & (Z * ROWS - 1)).astype(F32) + 1.0
    earlier = (column_y == jnp.broadcast_to(owner_y, (B, B))) & (lane < sub)
    rank = jnp.sum(jnp.where(earlier, 1.0, 0.0), axis=1, keepdims=True)
    pos = column_y * ASKED + jnp.broadcast_to(rank, (B, B)).astype(I32)
    for k in range(2):
        unpack[:, k * B : (k + 1) * B] = jnp.where(pos == lane + k * B, 1.0, 0.0).astype(BF16)
        pack[k * B : (k + 1) * B] = jnp.where(pos.T == sub + k * B, 1.0, 0.0).astype(BF16)
    number = lane - core * ASKED
    valid = (number >= 0) & (number < ASKED)
    for e in range(Y):
        mine = valid & (pos == number + ((y + Y - e) & (Y - 1)) * ASKED)
        wish = jnp.sum(jnp.where(mine, asked_of, 0.0), axis=0, keepdims=True)
        wish_out[e] = jnp.broadcast_to(wish, (8, B))

    def wish_send(e, d):
        return remote(
            wish_out.at[e], wishes.at[e, c], w_s.at[e, d], w_r.at[e, c], ctx_at(d), tab_y(-e)
        )

    for e in (2, 1, 3, 0):
        for d in FAR_FIRST + ((0,) if e else ()):
            wish_send(e, d).start()
    wishes[0, c] = wish_out[0]

    def row_send(e, d):
        to = ctx_at(d)
        at = pl.ds(pl.multiple_of(lax.rem(to, 2) * ASKED, ASKED), ASKED)
        return remote(
            picked.at[e * 4 + lax.div(to, 2), at],
            x1.at[c, pl.ds(pl.multiple_of(y * ASKED, ASKED), ASKED)],
            a1_s.at[e, d], a1_r.at[e, c], to, tab_y(e),
        )

    def row_got(e, src):
        at = pl.ds(pl.multiple_of(((y + Y - e) & (Y - 1)) * ASKED, ASKED), ASKED)
        got(x1.at[src, at], a1_r.at[e, src], a1_s.at[0, 0])

    def grad_send(e, d):
        to = ctx_at(d)
        at = pl.ds(pl.multiple_of(((y + Y - e) & (Y - 1)) * ASKED, ASKED), ASKED)
        return remote(
            packed.at[to, at],
            gin.at[e * 4 + x, pl.ds(pl.multiple_of(core * ASKED, ASKED), ASKED)],
            a2_s.at[e, d], a2_r.at[e, c], to, tab_y(-e),
        )

    def grad_got(e, src):
        at = pl.ds(pl.multiple_of(lax.rem(src, 2) * ASKED, ASKED), ASKED)
        got(gin.at[e * 4 + lax.div(src, 2), at], a2_r.at[e, src], a2_s.at[0, 0])

    def gather_send(slot):
        distance = SLOTS[slot]
        copies = []
        for side in range(2) if slot == 15 else (0,) if distance > 0 else (1,):
            f = abs(distance) - LEAP
            at = half_rows[side] if slot == 15 else pl.ds(0, ROWS)
            copies.append(
                remote(
                    stage.at[slot, at], agg.at[side, f - 1, at],
                    ag_s.at[side, f - 1], ag_r.at[side, f - 1], c, tab_z(f if side == 0 else -f),
                )
            )
        return copies

    def gather_got(side, f):
        at = half_rows[side] if f == LEAP else pl.ds(0, ROWS)
        got(agg.at[side, f - 1, at], ag_r.at[side, f - 1], ag_s.at[side, f - 1])

    def target_send(slot):
        to = SLOT_OF[-SLOTS[slot]]
        return remote(
            stage.at[slot], zb.at[to - 1], rz_s.at[to - 1], rz_r.at[to - 1], c, tab_z(SLOTS[slot])
        )

    def target_got(to):
        got(zb.at[to - 1], rz_r.at[to - 1], rz_s.at[to - 1])

    holder = jnp.where(c >= SPLIT, 1, 0)

    def drain(upto=9):
        for d in range(1, CTX) if upto >= 9 else ():
            sent(fin.at[c], f_s.at[d - 1], f_r.at[d - 1])
        for e in nearest:
            near_send(e).wait_send()
        for e in range(Y):
            for d in range(CTX):
                if e or d:
                    wish_send(e, d).wait_send()
                    if upto >= 3:
                        row_send(e, d).wait_send()
                    if upto >= 7:
                        grad_send(e, d).wait_send()
        for side in range(2):
            for f in range(1, LEAP + 1):
                far_send(side, f).wait_send()
        for slot in range(1, Z) if upto >= 8 else ():
            for copy in gather_send(slot) if slot > 2 * LEAP else [target_send(slot)]:
                copy.wait_send()
        for h in range(HEADS):
            for s in range(2):
                need = (c <= SPLIT + REACH - 2) if s == 0 else (c >= SPLIT)

                @pl.when(need & (2 * h + s != c))
                def _():
                    sent(dob.at[0], do_s.at[h, s], do_r.at[0])
                    if upto >= 4:
                        sent(stq.at[h], q_s.at[h, s], q_r.at[0])

            if upto >= 4:
                @pl.when(2 * h + holder != c)
                def _():
                    sent(stkv.at[h], kv_s.at[h], kv_r.at[0])

        for b in range(8) if upto >= 5 else ():
            @pl.when((c != b) & (core == (0 if b < SPLIT else 1)))
            def _():
                sent(dkvs.at[b], dkv_s.at[b], dkv_r.at[0])

            for s in range(2):
                need = b <= SPLIT + REACH - 2 if s == 0 else b >= SPLIT
                if need:
                    @pl.when((c != b) & (core == s))
                    def _():
                        sent(dqs.at[b], dq_s.at[b], dq_r.at[0, 0])
                        if upto >= 8:
                            sent(atts.at[b], at_s.at[b], at_r.at[0, 0])

    def to_heads(src_of, dst, ssem, rsem, local):
        for r in (2, 1, 3, 0):
            h = lax.rem(x + r, HEADS)
            for s in range(2):
                need = (c <= SPLIT + REACH - 2) if s == 0 else (c >= SPLIT)
                dev = 2 * h + s

                @pl.when(need & (dev != c))
                def _():
                    remote(src_of(h), dst.at[c], ssem.at[h, s], rsem.at[c], dev, t).start()

                @pl.when(need & (dev == c))
                def _():
                    local(h)

    def dout_of(h):
        return dout_ref.at[:, pl.ds(pl.multiple_of(h * B, B), B)]

    def dout_here(h):
        dob[c] = dout_ref[:, pl.ds(pl.multiple_of(h * B, B), B)]

    cp_dout.wait()
    to_heads(dout_of, dob, do_s, do_r, dout_here)
    for copy in cp_w:
        copy.start()

    slot_got(SLOT_OF[-LEAP])
    for f in range(LEAP, 0, -1):
        far_send(0, f).start()
    slot_got(SLOT_OF[LEAP])
    for f in range(LEAP, 0, -1):
        far_send(1, f).start()

    for copy in cp_small:
        copy.wait()
    actb = jnp.broadcast_to(act_ref[...], (B, B)).T
    for j in range(8):
        block = pl.ds(j * B, B)
        emb = jnp.broadcast_to(atab_ref[0:1, block], (B, B))
        for a in range(1, 8):
            emb = jnp.where(actb == a, atab_ref[a : a + 1, block], emb)
        xin[j] = emb
    h0, h1, h2, h3 = hist_ref[0, 0], hist_ref[0, 1], hist_ref[0, 2], hist_ref[0, 3]
    e0, e1, e2 = h0, h0 + h1, h0 + h1 + h2

    def spans(i, carry):
        p = lax.broadcasted_iota(I32, (B, B), 0) + i * B
        in0, in1, in2 = p < e0, p < e1, p < e2
        startb[i] = jnp.where(in0, 0, jnp.where(in1, e0, jnp.where(in2, e1, e2)))
        length = jnp.where(in0, h0, jnp.where(in1, h1, jnp.where(in2, h2, h3)))
        invb[i] = 1.0 / length.astype(F32)
        return carry

    lax.fori_loop(0, 8, spans, 0)
    for e in range(Y):
        for d in range(CTX):
            if e or d:
                src = ctx_at(CTX - d)
                got(wishes.at[e, src], w_r.at[e, src], w_s.at[0, 0])

    def spread_wish(i, carry):
        e, chip = lax.div(i, 4), lax.rem(i, 4)
        line = wishes[e, 2 * chip, 0:1, :] + wishes[e, 2 * chip + 1, 0:1, :]
        wish = jnp.broadcast_to(line, (B, B)).T.astype(I32) - 1
        at = pl.ds(8 * i, 8)
        high[at] = lax.shift_right_arithmetic(wish, 8).astype(F32).astype(BF16).reshape(8, 16, B)
        low[at] = (wish & (PLANE - 1)).astype(F32).astype(BF16).reshape(8, 16, B)
        line = jnp.broadcast_to(line, (16, B)).astype(I32) - 1
        high_row[i] = lax.shift_right_arithmetic(line, 8).astype(F32).astype(BF16)
        low_row[i] = (line & (PLANE - 1)).astype(F32).astype(BF16)
        return carry

    lax.fori_loop(0, 16, spread_wish, 0)

    one, zero, none = jnp.asarray(1, BF16), jnp.asarray(0, BF16), jnp.asarray(-1, BF16)
    lane16 = lax.broadcasted_iota(I32, (16, B), 1).astype(F32).astype(BF16)

    def pick(e, g):
        at = slice(32 * e, 32 * (e + 1))
        wanted = jnp.where(high[at] == jnp.asarray(g, BF16), low[at], none)
        hot = jnp.concatenate(
            [
                jnp.where(wanted == (lane16 + jnp.asarray(k * B, BF16))[None], one, zero)
                .reshape(4 * B, B)
                for k in range(2)
            ],
            axis=1,
        )
        rows = tbl[GROUPS * g : GROUPS * (g + 1)].reshape(PLANE, B)
        return dot(hot, rows).reshape(4, B, B)

    for g in range(GROUPS):
        for to in range(GROUPS * g, GROUPS * (g + 1)):
            if to and abs(SLOTS[to]) != LEAP:
                slot_got(to)
        for e in (2, 1, 3, 0):
            at = slice(4 * e, 4 * (e + 1))
            found = pick(e, g) if g == 0 else gacc[at] + pick(e, g)
            if g < GROUPS - 1:
                gacc[at] = found
            else:
                picked[at] = found.astype(BF16)
                for d in FAR_FIRST + ((0,) if e else ()):
                    row_send(e, d).start()
    here = pl.ds(pl.multiple_of(core * ASKED, ASKED), ASKED)
    x1[c, pl.ds(pl.multiple_of(y * ASKED, ASKED), ASKED)] = picked[x, here]
    for e in (0, 1, 3, 2):
        for d in range(CTX):
            if e or d:
                row_got(e, ctx_at(CTX - d))

    total = jnp.zeros((B, B), F32)
    for j in range(8):
        value = xin[j] + dot(unpack[...], x1[j])
        xin[j] = value
        total = total + value
    mean = jnp.sum(total, axis=1, keepdims=True) * (1.0 / MODEL)
    total = jnp.zeros((B, B), F32)
    for j in range(8):
        centre = xin[j] - mean
        total = total + centre * centre
    inv_std = lax.rsqrt(jnp.sum(total, axis=1, keepdims=True) * (1.0 / MODEL) + NORM_EPS)
    for j in range(8):
        normed = (xin[j] - mean) * inv_std
        xin[j] = normed
        hn[:, j * B : (j + 1) * B] = (normed * gain_ref[:, j * B : (j + 1) * B]).astype(BF16)
    for copy in cp_w:
        copy.wait()

    def q_of(h):
        return stq.at[h]

    def q_here(h):
        qb[c] = stq[h]

    for r in (2, 1, 3, 0):
        h = lax.rem(x + r, HEADS)
        project = dot(hn[...], w_v[h])
        sig = sigmoid(project)
        pd[h] = sig * (1.0 + project * (1.0 - sig))
        active = (project * sig).astype(BF16)
        stq[h] = active[:, 0:B]
        stkv[h] = active[:, B : 3 * B]
        dev = 2 * h + holder

        @pl.when(dev != c)
        def _():
            remote(stkv.at[h], kvb.at[c], kv_s.at[h], kv_r.at[c], dev, t).start()

        @pl.when(dev == c)
        def _():
            kvb[c] = stkv[h]

        for s in (1, 0):
            need = (c <= SPLIT + REACH - 2) if s == 0 else (c >= SPLIT)
            to = 2 * h + s

            @pl.when(need & (to != c))
            def _():
                remote(stq.at[h], qb.at[c], q_s.at[h, s], q_r.at[c], to, t).start()

            @pl.when(need & (to == c))
            def _():
                q_here(h)

    def send_back(ready, ssem, rsem, dst, block):
        @pl.when(c != block)
        def _():
            remote(ready.at[block], dst, ssem.at[block], rsem, block, t).start()

        @pl.when(c == block)
        def _():
            dst[...] = ready[block]

    def attend(s):
        key_blocks = range(0, SPLIT) if s == 0 else range(SPLIT, 8)
        lowest = key_blocks[0]
        waited = set()
        for kb in key_blocks:
            end = min(kb + REACH, 8)
            n = (end - kb) * B

            @pl.when(c != kb)
            def _():
                got(kvb.at[kb], kv_r.at[kb], kv_s.at[0])

            for b in range(kb, end):
                if b not in waited:
                    waited.add(b)

                    @pl.when(c != b)
                    def _():
                        got(qb.at[b], q_r.at[b], q_s.at[0, 0])
                        got(dob.at[b], do_r.at[b], do_s.at[0, 0])

            queries = qb[kb:end].reshape(n, B)
            cotangent = dob[kb:end].reshape(n, B)
            keys = kvb[kb, :, 0:B]
            values = kvb[kb, :, B : 2 * B]
            raw = dot(queries, keys, NT) * SCALE
            sig = sigmoid(raw)
            inv = invb[kb:end].reshape(n, B)
            k_pos = lax.broadcasted_iota(I32, (n, B), 1) + kb * B
            q_pos = lax.broadcasted_iota(I32, (n, B), 0) + kb * B
            allowed = (k_pos >= startb[kb:end].reshape(n, B)) & (k_pos <= q_pos)
            weights = jnp.where(allowed, raw * sig * inv, 0.0).astype(BF16)
            grad_w = dot(cotangent, values, NT)
            slope = sig * (1.0 + raw * (1.0 - sig))
            grad_raw = jnp.where(allowed, grad_w * slope * (inv * SCALE), 0.0).astype(BF16)
            dkvs[kb, :, 0:B] = dot(grad_raw, queries, TN).astype(BF16)
            dkvs[kb, :, B : 2 * B] = dot(weights, cotangent, TN).astype(BF16)
            send_back(dkvs, dkv_s, dkv_r.at[x], rdkv.at[x], kb)
            dq = dot(grad_raw, keys)
            at = dot(weights, values)
            for b in range(kb, end):
                rows = slice((b - kb) * B, (b - kb + 1) * B)
                first = kb == max(b - REACH + 1, lowest)
                last = kb == min(b, key_blocks[-1])
                dq_b = dq[rows] if first else dqacc[b] + dq[rows]
                at_b = at[rows] if first else attacc[b] + at[rows]
                if last:
                    dqs[b] = dq_b.astype(BF16)
                    send_back(dqs, dq_s, dq_r.at[s, x], rdq.at[s, x], b)
                    atts[b] = at_b.astype(BF16)
                else:
                    dqacc[b] = dq_b
                    attacc[b] = at_b

    for s in range(2):
        @pl.when(core == s)
        def _():
            attend(s)

    both = (c >= SPLIT) & (c <= SPLIT + REACH - 2)
    for r in (0, 1, 3, 2):
        h = lax.rem(x + r, HEADS)

        @pl.when(2 * h + holder != c)
        def _():
            got(rdkv.at[h], dkv_r.at[h], dkv_s.at[0])
            got(rdq.at[holder, h], dq_r.at[holder, h], dq_s.at[0])

        @pl.when(both & (2 * h != c))
        def _():
            got(rdq.at[0, h], dq_r.at[0, h], dq_s.at[0])

        dqf[...] = rdq[holder, h].astype(F32)

        @pl.when(both)
        def _():
            dqf[...] = dqf[...] + rdq[0, h].astype(F32)

        slope = pd[h]
        grad_project = jnp.concatenate(
            [
                (dqf[...] * slope[:, 0:B]).astype(BF16),
                (rdkv[h].astype(F32) * slope[:, B : 3 * B]).astype(BF16),
            ],
            axis=1,
        )
        part = dot(grad_project, w_v[h], NT)
        gh[...] = part if r == 0 else gh[...] + part

    total = jnp.zeros((B, B), F32)
    cross = jnp.zeros((B, B), F32)
    for j in range(8):
        cols = slice(j * B, (j + 1) * B)
        g = gh[:, cols] * gain_ref[:, cols]
        gh[:, cols] = g
        total = total + g
        cross = cross + g * xin[j]
    mean_g = jnp.sum(total, axis=1, keepdims=True) * (1.0 / MODEL)
    mean_c = jnp.sum(cross, axis=1, keepdims=True) * (1.0 / MODEL)
    for j in range(8):
        g = gh[:, j * B : (j + 1) * B]
        g2[j] = (inv_std * (g - mean_g - xin[j] * mean_c)).astype(BF16)

    for d in FAR_FIRST + (0,):
        to = ctx_at(d)
        packed[to] = dot(pack[...], g2[to]).astype(BF16)
        for e in (2, 1, 3, 0):
            if e or d:
                grad_send(e, d).start()
    gin[x, here] = packed[c, pl.ds(pl.multiple_of(y * ASKED, ASKED), ASKED)]
    for e in (0, 1, 3, 2):
        for d in range(CTX):
            if e or d:
                grad_got(e, ctx_at(CTX - d))

    sub16 = lax.broadcasted_iota(I32, (PLANE, B), 0).astype(F32).astype(BF16).reshape(16, 16, B)

    for g in (3, 2, 1, 0):
        wanted = jnp.where(high_row[...] == jnp.asarray(g, BF16), low_row[...], none)
        hot = jnp.concatenate(
            [jnp.where(sub16 == wanted[j][None], one, zero).reshape(PLANE, B) for j in range(16)],
            axis=1,
        )
        value = dot(hot, gin[...].reshape(16 * B, B))
        own[g] = value
        for i in range(GROUPS):
            slot = GROUPS * g + i
            if slot and abs(SLOTS[slot]) != LEAP:
                stage[slot] = value[i * ROWS : (i + 1) * ROWS].astype(BF16)
                for copy in gather_send(slot) if slot > 2 * LEAP else [target_send(slot)]:
                    copy.start()

    for s in range(2):
        @pl.when(core == s)
        def _():
            for b in range(0, SPLIT + REACH - 1) if s == 0 else range(SPLIT, 8):
                send_back(atts, at_s, at_r.at[s, x], ratt.at[s, x], b)

    for side in range(2):
        slot = SLOT_OF[LEAP if side == 0 else -LEAP]
        i = slot % GROUPS
        total = own[slot // GROUPS, i * ROWS : (i + 1) * ROWS, :]
        for f in range(1, LEAP):
            gather_got(side, f)
            total = total + agg[side, f - 1].astype(F32)
        gather_got(side, LEAP)
        stage[slot] = total.astype(BF16)
        at = slice(side * HALF, (side + 1) * HALF)
        stage[slot, at, :] = (total[at] + agg[side, LEAP - 1, at, :].astype(F32)).astype(BF16)
        target_send(slot).start()

    for h in range(HEADS):
        @pl.when(2 * h + holder != c)
        def _():
            got(ratt.at[holder, h], at_r.at[holder, h], at_s.at[0])

        @pl.when(both & (2 * h != c))
        def _():
            got(ratt.at[0, h], at_r.at[0, h], at_s.at[0])

        dqf[...] = ratt[holder, h].astype(F32)

        @pl.when(both)
        def _():
            dqf[...] = dqf[...] + ratt[0, h].astype(F32)

        att_out[:, h * B : (h + 1) * B] = dqf[...].astype(BF16)

    value = own[0, 0:ROWS, :]
    for to in range(1, 2 * LEAP + 1):
        target_got(to)
        value = value + zb[to - 1].astype(F32)

    fin[c] = value.astype(BF16)
    for d in FAR_FIRST:
        remote(fin.at[c], fin.at[c], f_s.at[d - 1], f_r.at[d - 1], ctx_at(d), t).start()
    for d in range(1, CTX):
        src = ctx_at(CTX - d)
        got(fin.at[src], f_r.at[d - 1], f_s.at[d - 1])

    grad_out[...] = fin[...]
    drain()


def adagrad(grad, att, rows, accum, att_out, rg_out, nm_out, na_out):
    att_out[...] = att[...]
    total = jnp.zeros((ROWS, B), F32)
    for j in range(8):
        g = grad[j].astype(F32)
        rg_out[:, j * B : (j + 1) * B] = g
        total = total + g * g
    diagonal = lax.broadcasted_iota(I32, (ROWS, ROWS), 0) == lax.broadcasted_iota(
        I32, (ROWS, ROWS), 1
    )
    before = jnp.sum(jnp.where(diagonal, accum[...], 0.0), axis=1, keepdims=True)
    after = before + jnp.sum(total, axis=1, keepdims=True) * (1.0 / MODEL)
    rate = LEARN_RATE * lax.rsqrt(after)
    for j in range(8):
        cols = slice(j * B, (j + 1) * B)
        nm_out[:, cols] = rows[:, cols] - grad[j].astype(F32) * rate
    na_out[...] = jnp.sum(jnp.where(diagonal, after, 0.0), axis=0, keepdims=True)


def per_device(
    item_owner, item_row, action_id, history_len, masters, row_accum, action_table, norm_gain,
    w_qkv, d_attended,
):
    vmem = pl.BlockSpec(memory_space=pltpu.VMEM)
    hbm = pl.BlockSpec(memory_space=pltpu.HBM)
    dma = pltpu.SemaphoreType.DMA

    def block(*lead, rows=B, cols=B, dtype=BF16):
        return pltpu.VMEM((*lead, rows, cols), dtype)

    scratch = [
        pltpu.VMEM((1, B), I32),
        pltpu.VMEM((1, B), I32),
        pltpu.VMEM((1, B), I32),
        pltpu.SMEM((1, 4), I32),
        pltpu.VMEM((8, MODEL), F32),
        pltpu.VMEM((1, MODEL), F32),
        pltpu.VMEM((B, HEADS * B), BF16),
        pltpu.VMEM((ROWS, B), F32),
        pltpu.VMEM((HEADS, MODEL, 3 * B), BF16),
        block(Z, rows=ROWS),
        block(128, rows=16),
        block(128, rows=16),
        block(16, rows=16),
        block(16, rows=16),
        block(cols=2 * B),
        block(rows=2 * B),
        block(Y, rows=8, dtype=F32),
        block(Y, CTX, rows=8, dtype=F32),
        block(16, dtype=F32),
        block(16),
        block(8, rows=Y * ASKED),
        block(8, dtype=F32),
        block(cols=MODEL),
        block(8, dtype=I32),
        block(8, dtype=F32),
        block(HEADS, cols=3 * B, dtype=F32),
        block(HEADS),
        block(HEADS, cols=2 * B),
        block(8),
        block(8, cols=2 * B),
        block(8),
        block(8, dtype=F32),
        block(8, dtype=F32),
        block(8),
        block(8, cols=2 * B),
        block(8),
        block(2, HEADS),
        block(HEADS, cols=2 * B),
        block(2, HEADS),
        block(dtype=F32),
        block(cols=MODEL, dtype=F32),
        block(8),
        block(8, rows=Y * ASKED),
        block(16),
        block(GROUPS, rows=PLANE, dtype=F32),
        block(Z, rows=ROWS),
        block(2, LEAP, rows=ROWS),
        block(2 * LEAP, rows=ROWS),
        block(8, rows=ROWS),
        dma((22,)),
        dma((Y, CTX)), dma((Y, CTX)),
        dma((Z + 1,)), dma((Z + 1,)),
        dma((Y, CTX)), dma((Y, CTX)),
        dma((HEADS, 2)), dma((8,)),
        dma((HEADS,)), dma((8,)),
        dma((HEADS, 2)), dma((8,)),
        dma((8,)), dma((2, HEADS)),
        dma((8,)), dma((HEADS,)),
        dma((8,)), dma((2, HEADS)),
        dma((Y, CTX)), dma((Y, CTX)),
        dma((2, LEAP)), dma((2, LEAP)),
        dma((2 * LEAP,)), dma((2 * LEAP,)),
        dma((7,)), dma((7,)),
    ]
    attended, grads = pl.pallas_call(
        kernel,
        out_shape=(
            jax.ShapeDtypeStruct((B, HEADS * B), BF16),
            jax.ShapeDtypeStruct((8, ROWS, B), BF16),
        ),
        in_specs=[hbm] * 9,
        out_specs=(vmem, vmem),
        scratch_shapes=scratch,
        compiler_params=pltpu.CompilerParams(
            collective_id=0, has_side_effects=True, vmem_limit_bytes=VMEM_BYTES
        ),
    )(
        item_owner[:, :, 0], item_row, action_id, history_len, masters, action_table,
        norm_gain[None, :], w_qkv, d_attended[0],
    )
    attended, row_grads, new_masters, new_accum = pl.pallas_call(
        adagrad,
        out_shape=(
            jax.ShapeDtypeStruct((B, HEADS * B), BF16),
            jax.ShapeDtypeStruct((ROWS, MODEL), F32),
            jax.ShapeDtypeStruct((ROWS, MODEL), F32),
            jax.ShapeDtypeStruct((1, ROWS), F32),
        ),
        in_specs=[vmem] * 4,
        out_specs=(vmem, vmem, vmem, vmem),
        compiler_params=pltpu.CompilerParams(vmem_limit_bytes=VMEM_BYTES),
    )(grads, attended, masters, row_accum[None, :])
    return (attended[None], row_grads, new_masters, new_accum[0])


def solution(mesh):
    in_specs = (
        P("tab", "ctx", None),
        P("tab", "ctx"),
        P("tab", "ctx"),
        P("tab", None),
        P("tab", None),
        P("tab"),
        P(),
        P(),
        P(),
        P("tab", "ctx", None),
    )
    out_specs = (P("tab", "ctx", None), P("tab", None), P("tab", None), P("tab"))
    return jax.shard_map(
        per_device, mesh=mesh, in_specs=in_specs, out_specs=out_specs, check_vma=False
    )
```

```python
import math

import jax
import jax.numpy as jnp
from jax import lax
from jax.experimental import pallas as pl
from jax.experimental.pallas import tpu as pltpu
from jax.sharding import PartitionSpec as P

MESH = pl.DeviceIdType.MESH
F32 = jnp.float32
BF16 = jnp.bfloat16
I32 = jnp.int32

NORM_EPS = 1e-05
LEARN_RATE = 0.1

CTX = 8
Y = 4
B = 128
ROWS = 64
PLANE = Y * ROWS
MODEL = 1024
HEADS = 4
Z = 16
GROUPS = 4
SLOTS = (0, 1, -1, 2, -2, 3, -3, 4, -4, 5, -5, 6, -6, 7, -7, 8)
SLOT_OF = {distance: slot for slot, distance in enumerate(SLOTS)} | {-8: 15}
LEAP = 4
HALF = ROWS // 2
ASKED = 64
VMEM_BYTES = 63 * 1024 * 1024
SPLIT = 3
REACH = 5
SCALE = 1.0 / math.sqrt(B)
FAR_FIRST = (4, 3, 5, 2, 6, 1, 7)

NT = (((1,), (1,)), ((), ()))
TN = (((0,), (0,)), ((), ()))


def sigmoid(value):
    return 0.5 * jnp.tanh(0.5 * value) + 0.5


def dot(a, b, dims=(((1,), (0,)), ((), ()))):
    return lax.dot_general(a, b, dims, preferred_element_type=F32)


def kernel(
    owner_hbm, row_hbm, act_hbm, hist_hbm, masters_ref, atab_hbm, gain_hbm, w_ref,
    dout_hbm,
    att_out, grad_out,
    owner_ref, row_ref, act_ref, hist_ref, atab_ref, gain_ref, dout_ref,
    mslice, w_v, tbl, high, low, high_row, low_row, unpack, pack, wish_out, wishes,
    gacc, picked, x1, xin, hn, startb, invb,
    pd, sqkv, qkv, qf, dob, dkvacc, attacc, dqacc, dqs, dkvs, atts, rdq, rdkv, ratt, dqf, gh,
    g2, packed, gin, own, stage, agg, zb, fin,
    loc_s, w_s, w_r, z_s, z_r, a1_s, a1_r, qkv_s, qkv_r, qf_s, qf_r, do_s, do_r,
    dq_s, dq_r, dkv_s, dkv_r, at_s, at_r, a2_s, a2_r, ag_s, ag_r, rz_s, rz_r, f_s, f_r,
):
    c = lax.axis_index("ctx")
    t = lax.axis_index("tab")
    x, core = lax.div(c, 2), lax.rem(c, 2)
    z, y = lax.div(t, Y), lax.rem(t, Y)

    def ctx_at(d):
        return lax.rem(c + d, CTX)

    def tab_y(d):
        return z * Y + lax.rem(y + d + Y, Y)

    def z_at(d):
        return lax.rem(z + d + Z, Z)

    def tab_z(d):
        return z_at(d) * Y + y

    def remote(src, dst, ssem, rsem, to_ctx, to_tab):
        return pltpu.make_async_remote_copy(
            src_ref=src, dst_ref=dst, send_sem=ssem, recv_sem=rsem,
            device_id=(to_ctx, to_tab), device_id_type=MESH,
        )

    def got(dst, rsem, ssem):
        remote(dst, dst, ssem, rsem, c, t).wait_recv()

    def sent(src, ssem, rsem):
        remote(src, src, ssem, rsem, c, t).wait_send()

    cp_slice = pltpu.make_async_copy(
        masters_ref.at[:, pl.ds(pl.multiple_of(c * B, B), B)], mslice, loc_s.at[0]
    )
    cp_slice.start()

    barrier = pltpu.get_barrier_semaphore()
    for d in range(LEAP, 0, -1):
        for e in (d, -d):
            pl.semaphore_signal(barrier, inc=1, device_id=(c, tab_z(e)), device_id_type=MESH)
    for e in (2, 1, 3, 0):
        for d in FAR_FIRST + ((0,) if e else ()):
            pl.semaphore_signal(
                barrier, inc=1, device_id=(ctx_at(d), tab_y(e)), device_id_type=MESH
            )

    cp_ids = []
    for i, (src, dst) in enumerate(((owner_hbm, owner_ref), (row_hbm, row_ref))):
        cp_ids.append(pltpu.make_async_copy(src, dst, loc_s.at[14 + i]))
        cp_ids[-1].start()
    cp_dout = pltpu.make_async_copy(dout_hbm, dout_ref, loc_s.at[16])
    cp_dout.start()
    cp_small = []
    for i, (src, dst) in enumerate(
        (
            (act_hbm, act_ref), (atab_hbm, atab_ref), (hist_hbm, hist_ref), (gain_hbm, gain_ref),
        )
    ):
        cp_small.append(pltpu.make_async_copy(src, dst, loc_s.at[17 + i]))
        cp_small[-1].start()
    cp_w = []
    for h in range(HEADS):
        for part in range(3):
            cp_w.append(
                pltpu.make_async_copy(
                    w_ref.at[:, pl.ds(part * HEADS * B + h * B, B)],
                    w_v.at[h, :, pl.ds(part * B, B)],
                    loc_s.at[2 + 3 * h + part],
                )
            )

    cp_slice.wait()
    tbl[0] = mslice[...].astype(BF16)
    pl.semaphore_wait(barrier, Y * CTX - 1 + 2 * LEAP)

    half_rows = (pl.ds(0, HALF), pl.ds(HALF, HALF))

    def near_send(e):
        to = SLOT_OF[-e]
        return remote(tbl.at[0], tbl.at[to], z_s.at[to], z_r.at[to], c, tab_z(e))

    def far_send(side, f):
        e = f if side == 0 else -f
        src = tbl.at[SLOT_OF[-LEAP if side == 0 else LEAP]]
        to = SLOT_OF[-LEAP - f if side == 0 else LEAP + f]
        if f < LEAP:
            return remote(src, tbl.at[to], z_s.at[to], z_r.at[to], c, tab_z(e))
        at = half_rows[side]
        return remote(
            src.at[at], tbl.at[to, at], z_s.at[15 + side], z_r.at[15 + side], c, tab_z(e)
        )

    def slot_got(to):
        if to < 15:
            got(tbl.at[to], z_r.at[to], z_s.at[to])
        else:
            for side in range(2):
                got(tbl.at[15, half_rows[side]], z_r.at[15 + side], z_s.at[15 + side])

    nearest = [e for d in range(LEAP, 0, -1) for e in (d, -d)]
    for e in nearest:
        near_send(e).start()
    for copy in cp_ids:
        copy.wait()
    owner, row = owner_ref[...], row_ref[...]
    ahead = (lax.shift_right_logical(owner, 2) + Z - z) & (Z - 1)
    slot = jnp.where(ahead > Z // 2, 2 * (Z - ahead), jnp.maximum(2 * ahead - 1, 0))
    asked = slot * ROWS + row
    owner_y = owner & (Y - 1)

    lane = lax.broadcasted_iota(I32, (B, B), 1)
    sub = lax.broadcasted_iota(I32, (B, B), 0)
    column = jnp.broadcast_to(owner_y * (Z * ROWS) + asked, (B, B)).T
    column_y = lax.shift_right_logical(column, 10)
    asked_of = (column & (Z * ROWS - 1)).astype(F32) + 1.0
    earlier = (column_y == jnp.broadcast_to(owner_y, (B, B))) & (lane < sub)
    rank = jnp.sum(jnp.where(earlier, 1.0, 0.0), axis=1, keepdims=True)
    pos = column_y * ASKED + jnp.broadcast_to(rank, (B, B)).astype(I32)
    for k in range(2):
        unpack[:, k * B : (k + 1) * B] = jnp.where(pos == lane + k * B, 1.0, 0.0).astype(BF16)
        pack[k * B : (k + 1) * B] = jnp.where(pos.T == sub + k * B, 1.0, 0.0).astype(BF16)
    number = lane - core * ASKED
    valid = (number >= 0) & (number < ASKED)
    for e in range(Y):
        mine = valid & (pos == number + ((y + Y - e) & (Y - 1)) * ASKED)
        wish = jnp.sum(jnp.where(mine, asked_of, 0.0), axis=0, keepdims=True)
        wish_out[e] = jnp.broadcast_to(wish, (8, B))

    def wish_send(e, d):
        return remote(
            wish_out.at[e], wishes.at[e, c], w_s.at[e, d], w_r.at[e, c], ctx_at(d), tab_y(-e)
        )

    for e in (2, 1, 3, 0):
        for d in FAR_FIRST + ((0,) if e else ()):
            wish_send(e, d).start()
    wishes[0, c] = wish_out[0]

    def row_send(e, d):
        to = ctx_at(d)
        at = pl.ds(pl.multiple_of(lax.rem(to, 2) * ASKED, ASKED), ASKED)
        return remote(
            picked.at[e * 4 + lax.div(to, 2), at],
            x1.at[c, pl.ds(pl.multiple_of(y * ASKED, ASKED), ASKED)],
            a1_s.at[e, d], a1_r.at[e, c], to, tab_y(e),
        )

    def row_got(e, src):
        at = pl.ds(pl.multiple_of(((y + Y - e) & (Y - 1)) * ASKED, ASKED), ASKED)
        got(x1.at[src, at], a1_r.at[e, src], a1_s.at[0, 0])

    def grad_send(e, d):
        to = ctx_at(d)
        at = pl.ds(pl.multiple_of(((y + Y - e) & (Y - 1)) * ASKED, ASKED), ASKED)
        return remote(
            packed.at[to, at],
            gin.at[e * 4 + x, pl.ds(pl.multiple_of(core * ASKED, ASKED), ASKED)],
            a2_s.at[e, d], a2_r.at[e, c], to, tab_y(-e),
        )

    def grad_got(e, src):
        at = pl.ds(pl.multiple_of(lax.rem(src, 2) * ASKED, ASKED), ASKED)
        got(gin.at[e * 4 + lax.div(src, 2), at], a2_r.at[e, src], a2_s.at[0, 0])

    def gather_send(slot):
        distance = SLOTS[slot]
        copies = []
        for side in range(2) if slot == 15 else (0,) if distance > 0 else (1,):
            f = abs(distance) - LEAP
            at = half_rows[side] if slot == 15 else pl.ds(0, ROWS)
            copies.append(
                remote(
                    stage.at[slot, at], agg.at[side, f - 1, at],
                    ag_s.at[side, f - 1], ag_r.at[side, f - 1], c, tab_z(f if side == 0 else -f),
                )
            )
        return copies

    def gather_got(side, f):
        at = half_rows[side] if f == LEAP else pl.ds(0, ROWS)
        got(agg.at[side, f - 1, at], ag_r.at[side, f - 1], ag_s.at[side, f - 1])

    def target_send(slot):
        to = SLOT_OF[-SLOTS[slot]]
        return remote(
            stage.at[slot], zb.at[to - 1], rz_s.at[to - 1], rz_r.at[to - 1], c, tab_z(SLOTS[slot])
        )

    def target_got(to):
        got(zb.at[to - 1], rz_r.at[to - 1], rz_s.at[to - 1])

    holder = jnp.where(c >= SPLIT, 1, 0)

    def drain(upto=9):
        for d in range(1, CTX) if upto >= 9 else ():
            sent(fin.at[c], f_s.at[d - 1], f_r.at[d - 1])
        for e in nearest:
            near_send(e).wait_send()
        for e in range(Y):
            for d in range(CTX):
                if e or d:
                    wish_send(e, d).wait_send()
                    if upto >= 3:
                        row_send(e, d).wait_send()
                    if upto >= 7:
                        grad_send(e, d).wait_send()
        for side in range(2):
            for f in range(1, LEAP + 1):
                far_send(side, f).wait_send()
        for slot in range(1, Z) if upto >= 8 else ():
            for copy in gather_send(slot) if slot > 2 * LEAP else [target_send(slot)]:
                copy.wait_send()
        for h in range(HEADS):
            for s in range(2):
                need = (c <= SPLIT + REACH - 2) if s == 0 else (c >= SPLIT)

                @pl.when(need & (2 * h + s != c))
                def _():
                    sent(dob.at[0], do_s.at[h, s], do_r.at[0])

            if upto >= 4:
                @pl.when(2 * h + holder != c)
                def _():
                    sent(sqkv.at[h], qkv_s.at[h], qkv_r.at[0])

        for b in range(SPLIT, SPLIT + REACH - 1) if upto >= 5 else ():
            @pl.when((core == 1) & (c != b + 1))
            def _():
                sent(qf.at[b], qf_s.at[b], qf_r.at[0])

        for b in range(8) if upto >= 5 else ():
            @pl.when((c != b) & (core == (0 if b < SPLIT else 1)))
            def _():
                sent(dkvs.at[b], dkv_s.at[b], dkv_r.at[0])

            for s in range(2):
                need = b <= SPLIT + REACH - 2 if s == 0 else b >= SPLIT
                if need:
                    @pl.when((c != b) & (core == s))
                    def _():
                        sent(dqs.at[b], dq_s.at[b], dq_r.at[0, 0])
                        if upto >= 8:
                            sent(atts.at[b], at_s.at[b], at_r.at[0, 0])

    def to_heads(src_of, dst, ssem, rsem, local):
        for r in (2, 1, 3, 0):
            h = lax.rem(x + r, HEADS)
            for s in range(2):
                need = (c <= SPLIT + REACH - 2) if s == 0 else (c >= SPLIT)
                dev = 2 * h + s

                @pl.when(need & (dev != c))
                def _():
                    remote(src_of(h), dst.at[c], ssem.at[h, s], rsem.at[c], dev, t).start()

                @pl.when(need & (dev == c))
                def _():
                    local(h)

    def dout_of(h):
        return dout_ref.at[:, pl.ds(pl.multiple_of(h * B, B), B)]

    def dout_here(h):
        dob[c] = dout_ref[:, pl.ds(pl.multiple_of(h * B, B), B)]

    cp_dout.wait()
    to_heads(dout_of, dob, do_s, do_r, dout_here)
    for copy in cp_w:
        copy.start()

    slot_got(SLOT_OF[-LEAP])
    for f in range(LEAP, 0, -1):
        far_send(0, f).start()
    slot_got(SLOT_OF[LEAP])
    for f in range(LEAP, 0, -1):
        far_send(1, f).start()

    for copy in cp_small:
        copy.wait()
    actb = jnp.broadcast_to(act_ref[...], (B, B)).T
    for j in range(8):
        block = pl.ds(j * B, B)
        emb = jnp.broadcast_to(atab_ref[0:1, block], (B, B))
        for a in range(1, 8):
            emb = jnp.where(actb == a, atab_ref[a : a + 1, block], emb)
        xin[j] = emb
    h0, h1, h2, h3 = hist_ref[0, 0], hist_ref[0, 1], hist_ref[0, 2], hist_ref[0, 3]
    e0, e1, e2 = h0, h0 + h1, h0 + h1 + h2

    def spans(i, carry):
        p = lax.broadcasted_iota(I32, (B, B), 0) + i * B
        in0, in1, in2 = p < e0, p < e1, p < e2
        startb[i] = jnp.where(in0, 0, jnp.where(in1, e0, jnp.where(in2, e1, e2)))
        length = jnp.where(in0, h0, jnp.where(in1, h1, jnp.where(in2, h2, h3)))
        invb[i] = 1.0 / length.astype(F32)
        return carry

    lax.fori_loop(0, 8, spans, 0)
    for e in range(Y):
        for d in range(CTX):
            if e or d:
                src = ctx_at(CTX - d)
                got(wishes.at[e, src], w_r.at[e, src], w_s.at[0, 0])

    def spread_wish(i, carry):
        e, chip = lax.div(i, 4), lax.rem(i, 4)
        line = wishes[e, 2 * chip, 0:1, :] + wishes[e, 2 * chip + 1, 0:1, :]
        wish = jnp.broadcast_to(line, (B, B)).T.astype(I32) - 1
        at = pl.ds(8 * i, 8)
        high[at] = lax.shift_right_arithmetic(wish, 8).astype(F32).astype(BF16).reshape(8, 16, B)
        low[at] = (wish & (PLANE - 1)).astype(F32).astype(BF16).reshape(8, 16, B)
        line = jnp.broadcast_to(line, (16, B)).astype(I32) - 1
        high_row[i] = lax.shift_right_arithmetic(line, 8).astype(F32).astype(BF16)
        low_row[i] = (line & (PLANE - 1)).astype(F32).astype(BF16)
        return carry

    lax.fori_loop(0, 16, spread_wish, 0)

    one, zero, none = jnp.asarray(1, BF16), jnp.asarray(0, BF16), jnp.asarray(-1, BF16)
    lane16 = lax.broadcasted_iota(I32, (16, B), 1).astype(F32).astype(BF16)

    def pick(e, g):
        at = slice(32 * e, 32 * (e + 1))
        wanted = jnp.where(high[at] == jnp.asarray(g, BF16), low[at], none)
        hot = jnp.concatenate(
            [
                jnp.where(wanted == (lane16 + jnp.asarray(k * B, BF16))[None], one, zero)
                .reshape(4 * B, B)
                for k in range(2)
            ],
            axis=1,
        )
        rows = tbl[GROUPS * g : GROUPS * (g + 1)].reshape(PLANE, B)
        return dot(hot, rows).reshape(4, B, B)

    for g in range(GROUPS):
        for to in range(GROUPS * g, GROUPS * (g + 1)):
            if to and abs(SLOTS[to]) != LEAP:
                slot_got(to)
        for e in (2, 1, 3, 0):
            at = slice(4 * e, 4 * (e + 1))
            found = pick(e, g) if g == 0 else gacc[at] + pick(e, g)
            if g < GROUPS - 1:
                gacc[at] = found
            else:
                picked[at] = found.astype(BF16)
                for d in FAR_FIRST + ((0,) if e else ()):
                    row_send(e, d).start()
    here = pl.ds(pl.multiple_of(core * ASKED, ASKED), ASKED)
    x1[c, pl.ds(pl.multiple_of(y * ASKED, ASKED), ASKED)] = picked[x, here]
    for e in (0, 1, 3, 2):
        for d in range(CTX):
            if e or d:
                row_got(e, ctx_at(CTX - d))

    total = jnp.zeros((B, B), F32)
    for j in range(8):
        value = xin[j] + dot(unpack[...], x1[j])
        xin[j] = value
        total = total + value
    mean = jnp.sum(total, axis=1, keepdims=True) * (1.0 / MODEL)
    total = jnp.zeros((B, B), F32)
    for j in range(8):
        centre = xin[j] - mean
        total = total + centre * centre
    inv_std = lax.rsqrt(jnp.sum(total, axis=1, keepdims=True) * (1.0 / MODEL) + NORM_EPS)
    for j in range(8):
        normed = (xin[j] - mean) * inv_std
        xin[j] = normed
        hn[:, j * B : (j + 1) * B] = (normed * gain_ref[:, j * B : (j + 1) * B]).astype(BF16)
    for copy in cp_w:
        copy.wait()

    for r in (2, 1, 3, 0):
        h = lax.rem(x + r, HEADS)
        project = dot(hn[...], w_v[h])
        sig = sigmoid(project)
        pd[h] = sig * (1.0 + project * (1.0 - sig))
        active = (project * sig).astype(BF16)
        sqkv[h] = active
        dev = 2 * h + holder

        @pl.when(dev != c)
        def _():
            remote(sqkv.at[h], qkv.at[c], qkv_s.at[h], qkv_r.at[c], dev, t).start()

        @pl.when(dev == c)
        def _():
            qkv[c] = sqkv[h]

    both = (c >= SPLIT) & (c <= SPLIT + REACH - 2)

    @pl.when(both & (core == 0))
    def _():
        qf[c] = sqkv[x, :, 0:B]

    def send_back(ready, ssem, rsem, dst, block):
        @pl.when(c != block)
        def _():
            remote(ready.at[block], dst, ssem.at[block], rsem, block, t).start()

        @pl.when(c == block)
        def _():
            dst[...] = ready[block]

    def block_got(b):
        @pl.when(c != b)
        def _():
            got(qkv.at[b], qkv_r.at[b], qkv_s.at[0])
            got(dob.at[b], do_r.at[b], do_s.at[0, 0])

    def tile(kb, low_q, end_q, queries):
        n = (end_q - low_q) * B
        queries = queries.reshape(n, B)
        cotangent = dob[low_q:end_q].reshape(n, B)
        keys = qkv[kb, :, B : 2 * B]
        values = qkv[kb, :, 2 * B : 3 * B]
        raw = dot(queries, keys, NT) * SCALE
        sig = sigmoid(raw)
        inv = invb[low_q:end_q].reshape(n, B)
        k_pos = lax.broadcasted_iota(I32, (n, B), 1) + kb * B
        q_pos = lax.broadcasted_iota(I32, (n, B), 0) + low_q * B
        allowed = (k_pos >= startb[low_q:end_q].reshape(n, B)) & (k_pos <= q_pos)
        weights = jnp.where(allowed, raw * sig * inv, 0.0).astype(BF16)
        grad_w = dot(cotangent, values, NT)
        slope = sig * (1.0 + raw * (1.0 - sig))
        grad_raw = jnp.where(allowed, grad_w * slope * (inv * SCALE), 0.0).astype(BF16)
        dkv = jnp.concatenate([dot(grad_raw, queries, TN), dot(weights, cotangent, TN)], axis=1)
        return dkv, dot(grad_raw, keys), dot(weights, values)

    def keep(s, kb, low_q, end_q, dq, at):
        lowest, highest = (0, SPLIT - 1) if s == 0 else (SPLIT, 7)
        for b in range(low_q, end_q):
            rows = slice((b - low_q) * B, (b - low_q + 1) * B)
            first = kb == max(b - REACH + 1, lowest)
            dq_b = dq[rows] if first else dqacc[b] + dq[rows]
            at_b = at[rows] if first else attacc[b] + at[rows]
            if kb == min(b, highest):
                dqs[b] = dq_b.astype(BF16)
                send_back(dqs, dq_s, dq_r.at[s, x], rdq.at[s, x], b)
                atts[b] = at_b.astype(BF16)
            else:
                dqacc[b] = dq_b
                attacc[b] = at_b

    def dkv_back(kb, dkv):
        dkvs[kb] = dkv.astype(BF16)
        send_back(dkvs, dkv_s, dkv_r.at[x], rdkv.at[x], kb)

    def hand_on(b):
        return remote(
            qkv.at[b, :, pl.ds(0, B)], qf.at[b], qf_s.at[b], qf_r.at[b], 2 * x, t
        )

    shared = range(SPLIT, SPLIT + REACH - 1)

    @pl.when(core == 0)
    def _():
        for b in range(SPLIT):
            block_got(b)
        for kb in range(SPLIT):
            dkv, dq, at = tile(kb, kb, SPLIT, qkv[kb:SPLIT, :, 0:B])
            dkvacc[kb] = dkv
            keep(0, kb, kb, SPLIT, dq, at)
        for b in shared:
            @pl.when(c != b)
            def _():
                got(qf.at[b], qf_r.at[b], qf_s.at[0])
                got(dob.at[b], do_r.at[b], do_s.at[0, 0])

        for kb in range(SPLIT):
            dkv, dq, at = tile(kb, SPLIT, kb + REACH, qf[SPLIT : kb + REACH])
            dkv_back(kb, dkvacc[kb] + dkv)
            keep(0, kb, SPLIT, kb + REACH, dq, at)

    @pl.when(core == 1)
    def _():
        for b in shared:
            block_got(b)

            @pl.when(c != b + 1)
            def _():
                hand_on(b).start()

        for b in range(SPLIT + REACH - 1, 8):
            block_got(b)
        for kb in range(SPLIT, 8):
            end = min(kb + REACH, 8)
            dkv, dq, at = tile(kb, kb, end, qkv[kb:end, :, 0:B])
            dkv_back(kb, dkv)
            keep(1, kb, kb, end, dq, at)

    for r in (0, 1, 3, 2):
        h = lax.rem(x + r, HEADS)

        @pl.when(2 * h + holder != c)
        def _():
            got(rdkv.at[h], dkv_r.at[h], dkv_s.at[0])
            got(rdq.at[holder, h], dq_r.at[holder, h], dq_s.at[0])

        @pl.when(both & (2 * h != c))
        def _():
            got(rdq.at[0, h], dq_r.at[0, h], dq_s.at[0])

        dqf[...] = rdq[holder, h].astype(F32)

        @pl.when(both)
        def _():
            dqf[...] = dqf[...] + rdq[0, h].astype(F32)

        slope = pd[h]
        grad_project = jnp.concatenate(
            [
                (dqf[...] * slope[:, 0:B]).astype(BF16),
                (rdkv[h].astype(F32) * slope[:, B : 3 * B]).astype(BF16),
            ],
            axis=1,
        )
        part = dot(grad_project, w_v[h], NT)
        gh[...] = part if r == 0 else gh[...] + part

    total = jnp.zeros((B, B), F32)
    cross = jnp.zeros((B, B), F32)
    for j in range(8):
        cols = slice(j * B, (j + 1) * B)
        g = gh[:, cols] * gain_ref[:, cols]
        gh[:, cols] = g
        total = total + g
        cross = cross + g * xin[j]
    mean_g = jnp.sum(total, axis=1, keepdims=True) * (1.0 / MODEL)
    mean_c = jnp.sum(cross, axis=1, keepdims=True) * (1.0 / MODEL)
    for j in range(8):
        g = gh[:, j * B : (j + 1) * B]
        g2[j] = (inv_std * (g - mean_g - xin[j] * mean_c)).astype(BF16)

    for d in FAR_FIRST + (0,):
        to = ctx_at(d)
        packed[to] = dot(pack[...], g2[to]).astype(BF16)
        for e in (2, 1, 3, 0):
            if e or d:
                grad_send(e, d).start()
    gin[x, here] = packed[c, pl.ds(pl.multiple_of(y * ASKED, ASKED), ASKED)]
    for e in (0, 1, 3, 2):
        for d in range(CTX):
            if e or d:
                grad_got(e, ctx_at(CTX - d))

    sub16 = lax.broadcasted_iota(I32, (PLANE, B), 0).astype(F32).astype(BF16).reshape(16, 16, B)

    for g in (3, 2, 1, 0):
        wanted = jnp.where(high_row[...] == jnp.asarray(g, BF16), low_row[...], none)
        hot = jnp.concatenate(
            [jnp.where(sub16 == wanted[j][None], one, zero).reshape(PLANE, B) for j in range(16)],
            axis=1,
        )
        value = dot(hot, gin[...].reshape(16 * B, B))
        own[g] = value
        for i in range(GROUPS):
            slot = GROUPS * g + i
            if slot and abs(SLOTS[slot]) != LEAP:
                stage[slot] = value[i * ROWS : (i + 1) * ROWS].astype(BF16)
                for copy in gather_send(slot) if slot > 2 * LEAP else [target_send(slot)]:
                    copy.start()

    for s in range(2):
        @pl.when(core == s)
        def _():
            for b in range(0, SPLIT + REACH - 1) if s == 0 else range(SPLIT, 8):
                send_back(atts, at_s, at_r.at[s, x], ratt.at[s, x], b)

    for side in range(2):
        slot = SLOT_OF[LEAP if side == 0 else -LEAP]
        i = slot % GROUPS
        total = own[slot // GROUPS, i * ROWS : (i + 1) * ROWS, :]
        for f in range(1, LEAP):
            gather_got(side, f)
            total = total + agg[side, f - 1].astype(F32)
        gather_got(side, LEAP)
        stage[slot] = total.astype(BF16)
        at = slice(side * HALF, (side + 1) * HALF)
        stage[slot, at, :] = (total[at] + agg[side, LEAP - 1, at, :].astype(F32)).astype(BF16)
        target_send(slot).start()

    for h in range(HEADS):
        @pl.when(2 * h + holder != c)
        def _():
            got(ratt.at[holder, h], at_r.at[holder, h], at_s.at[0])

        @pl.when(both & (2 * h != c))
        def _():
            got(ratt.at[0, h], at_r.at[0, h], at_s.at[0])

        dqf[...] = ratt[holder, h].astype(F32)

        @pl.when(both)
        def _():
            dqf[...] = dqf[...] + ratt[0, h].astype(F32)

        att_out[:, h * B : (h + 1) * B] = dqf[...].astype(BF16)

    value = own[0, 0:ROWS, :]
    for to in range(1, 2 * LEAP + 1):
        target_got(to)
        value = value + zb[to - 1].astype(F32)

    fin[c] = value.astype(BF16)
    for d in FAR_FIRST:
        remote(fin.at[c], fin.at[c], f_s.at[d - 1], f_r.at[d - 1], ctx_at(d), t).start()
    for d in range(1, CTX):
        src = ctx_at(CTX - d)
        got(fin.at[src], f_r.at[d - 1], f_s.at[d - 1])

    grad_out[...] = fin[...]
    drain()


def adagrad(grad, att, rows, accum, att_out, rg_out, nm_out, na_out):
    att_out[...] = att[...]
    total = jnp.zeros((ROWS, B), F32)
    for j in range(8):
        g = grad[j].astype(F32)
        rg_out[:, j * B : (j + 1) * B] = g
        total = total + g * g
    diagonal = lax.broadcasted_iota(I32, (ROWS, ROWS), 0) == lax.broadcasted_iota(
        I32, (ROWS, ROWS), 1
    )
    before = jnp.sum(jnp.where(diagonal, accum[...], 0.0), axis=1, keepdims=True)
    after = before + jnp.sum(total, axis=1, keepdims=True) * (1.0 / MODEL)
    rate = LEARN_RATE * lax.rsqrt(after)
    for j in range(8):
        cols = slice(j * B, (j + 1) * B)
        nm_out[:, cols] = rows[:, cols] - grad[j].astype(F32) * rate
    na_out[...] = jnp.sum(jnp.where(diagonal, after, 0.0), axis=0, keepdims=True)


def per_device(
    item_owner, item_row, action_id, history_len, masters, row_accum, action_table, norm_gain,
    w_qkv, d_attended,
):
    vmem = pl.BlockSpec(memory_space=pltpu.VMEM)
    hbm = pl.BlockSpec(memory_space=pltpu.HBM)
    dma = pltpu.SemaphoreType.DMA

    def block(*lead, rows=B, cols=B, dtype=BF16):
        return pltpu.VMEM((*lead, rows, cols), dtype)

    scratch = [
        pltpu.VMEM((1, B), I32),
        pltpu.VMEM((1, B), I32),
        pltpu.VMEM((1, B), I32),
        pltpu.SMEM((1, 4), I32),
        pltpu.VMEM((8, MODEL), F32),
        pltpu.VMEM((1, MODEL), F32),
        pltpu.VMEM((B, HEADS * B), BF16),
        pltpu.VMEM((ROWS, B), F32),
        pltpu.VMEM((HEADS, MODEL, 3 * B), BF16),
        block(Z, rows=ROWS),
        block(128, rows=16),
        block(128, rows=16),
        block(16, rows=16),
        block(16, rows=16),
        block(cols=2 * B),
        block(rows=2 * B),
        block(Y, rows=8, dtype=F32),
        block(Y, CTX, rows=8, dtype=F32),
        block(16, dtype=F32),
        block(16),
        block(8, rows=Y * ASKED),
        block(8, dtype=F32),
        block(cols=MODEL),
        block(8, dtype=I32),
        block(8, dtype=F32),
        block(HEADS, cols=3 * B, dtype=F32),
        block(HEADS, cols=3 * B),
        block(8, cols=3 * B),
        block(8),
        block(8),
        block(SPLIT, cols=2 * B, dtype=F32),
        block(8, dtype=F32),
        block(8, dtype=F32),
        block(8),
        block(8, cols=2 * B),
        block(8),
        block(2, HEADS),
        block(HEADS, cols=2 * B),
        block(2, HEADS),
        block(dtype=F32),
        block(cols=MODEL, dtype=F32),
        block(8),
        block(8, rows=Y * ASKED),
        block(16),
        block(GROUPS, rows=PLANE, dtype=F32),
        block(Z, rows=ROWS),
        block(2, LEAP, rows=ROWS),
        block(2 * LEAP, rows=ROWS),
        block(8, rows=ROWS),
        dma((22,)),
        dma((Y, CTX)), dma((Y, CTX)),
        dma((Z + 1,)), dma((Z + 1,)),
        dma((Y, CTX)), dma((Y, CTX)),
        dma((HEADS,)), dma((8,)),
        dma((8,)), dma((8,)),
        dma((HEADS, 2)), dma((8,)),
        dma((8,)), dma((2, HEADS)),
        dma((8,)), dma((HEADS,)),
        dma((8,)), dma((2, HEADS)),
        dma((Y, CTX)), dma((Y, CTX)),
        dma((2, LEAP)), dma((2, LEAP)),
        dma((2 * LEAP,)), dma((2 * LEAP,)),
        dma((7,)), dma((7,)),
    ]
    attended, grads = pl.pallas_call(
        kernel,
        out_shape=(
            jax.ShapeDtypeStruct((B, HEADS * B), BF16),
            jax.ShapeDtypeStruct((8, ROWS, B), BF16),
        ),
        in_specs=[hbm] * 9,
        out_specs=(vmem, vmem),
        scratch_shapes=scratch,
        compiler_params=pltpu.CompilerParams(
            collective_id=0, has_side_effects=True, vmem_limit_bytes=VMEM_BYTES
        ),
    )(
        item_owner[:, :, 0], item_row, action_id, history_len, masters, action_table,
        norm_gain[None, :], w_qkv, d_attended[0],
    )
    attended, row_grads, new_masters, new_accum = pl.pallas_call(
        adagrad,
        out_shape=(
            jax.ShapeDtypeStruct((B, HEADS * B), BF16),
            jax.ShapeDtypeStruct((ROWS, MODEL), F32),
            jax.ShapeDtypeStruct((ROWS, MODEL), F32),
            jax.ShapeDtypeStruct((1, ROWS), F32),
        ),
        in_specs=[vmem] * 4,
        out_specs=(vmem, vmem, vmem, vmem),
        compiler_params=pltpu.CompilerParams(vmem_limit_bytes=VMEM_BYTES),
    )(grads, attended, masters, row_accum[None, :])
    return (attended[None], row_grads, new_masters, new_accum[0])


def solution(mesh):
    in_specs = (
        P("tab", "ctx", None),
        P("tab", "ctx"),
        P("tab", "ctx"),
        P("tab", None),
        P("tab", None),
        P("tab"),
        P(),
        P(),
        P(),
        P("tab", "ctx", None),
    )
    out_specs = (P("tab", "ctx", None), P("tab", None), P("tab", None), P("tab"))
    return jax.shard_map(
        per_device, mesh=mesh, in_specs=in_specs, out_specs=out_specs, check_vma=False
    )
```

```python
import math

import jax
import jax.numpy as jnp
from jax import lax
from jax.experimental import pallas as pl
from jax.experimental.pallas import tpu as pltpu
from jax.sharding import PartitionSpec as P

MESH = pl.DeviceIdType.MESH
F32 = jnp.float32
BF16 = jnp.bfloat16
I32 = jnp.int32

NORM_EPS = 1e-05
LEARN_RATE = 0.1

CTX = 8
Y = 4
B = 128
ROWS = 64
PLANE = Y * ROWS
MODEL = 1024
HEADS = 4
Z = 16
GROUPS = 4
SLOTS = (0, 1, -1, 2, -2, 3, -3, 4, -4, 5, -5, 6, -6, 7, -7, 8)
SLOT_OF = {distance: slot for slot, distance in enumerate(SLOTS)} | {-8: 15}
LEAP = 4
HALF = ROWS // 2
ASKED = 64
VMEM_BYTES = 63 * 1024 * 1024
SPLIT = 3
REACH = 5
SCALE = 1.0 / math.sqrt(B)
FAR_FIRST = (4, 3, 5, 2, 6, 1, 7)

NT = (((1,), (1,)), ((), ()))
TN = (((0,), (0,)), ((), ()))


def sigmoid(value):
    return 0.5 * jnp.tanh(0.5 * value) + 0.5


def dot(a, b, dims=(((1,), (0,)), ((), ()))):
    return lax.dot_general(a, b, dims, preferred_element_type=F32)


def kernel(
    owner_hbm, row_hbm, act_hbm, hist_hbm, masters_ref, atab_hbm, gain_hbm, w_ref,
    dout_hbm,
    att_out, grad_out,
    owner_ref, row_ref, act_ref, hist_ref, atab_ref, gain_ref, dout_ref,
    mslice, w_v, tbl, high, low, high_row, low_row, unpack, pack, wish_out, wishes,
    gacc, picked, x1, xin, hn, startb, invb,
    pd, sqkv, qkv, qf, dob, dkvacc, attacc, dqacc, dqs, dkvs, atts, rdq, rdkv, ratt, dqf, gh,
    g2, packed, gin, own, stage, agg, zb, fin,
    loc_s, w_s, w_r, z_s, z_r, a1_s, a1_r, qkv_s, qkv_r, qf_s, qf_r, do_s, do_r,
    dq_s, dq_r, dkv_s, dkv_r, at_s, at_r, a2_s, a2_r, ag_s, ag_r, rz_s, rz_r, f_s, f_r,
):
    c = lax.axis_index("ctx")
    t = lax.axis_index("tab")
    x, core = lax.div(c, 2), lax.rem(c, 2)
    z, y = lax.div(t, Y), lax.rem(t, Y)

    def ctx_at(d):
        return lax.rem(c + d, CTX)

    def tab_y(d):
        return z * Y + lax.rem(y + d + Y, Y)

    def z_at(d):
        return lax.rem(z + d + Z, Z)

    def tab_z(d):
        return z_at(d) * Y + y

    def remote(src, dst, ssem, rsem, to_ctx, to_tab):
        return pltpu.make_async_remote_copy(
            src_ref=src, dst_ref=dst, send_sem=ssem, recv_sem=rsem,
            device_id=(to_ctx, to_tab), device_id_type=MESH,
        )

    def got(dst, rsem, ssem):
        remote(dst, dst, ssem, rsem, c, t).wait_recv()

    def sent(src, ssem, rsem):
        remote(src, src, ssem, rsem, c, t).wait_send()

    cp_slice = pltpu.make_async_copy(
        masters_ref.at[:, pl.ds(pl.multiple_of(c * B, B), B)], mslice, loc_s.at[0]
    )
    cp_slice.start()

    barrier = pltpu.get_barrier_semaphore()
    for d in range(LEAP, 0, -1):
        for e in (d, -d):
            pl.semaphore_signal(barrier, inc=1, device_id=(c, tab_z(e)), device_id_type=MESH)
    for e in (2, 1, 3, 0):
        for d in FAR_FIRST + ((0,) if e else ()):
            pl.semaphore_signal(
                barrier, inc=1, device_id=(ctx_at(d), tab_y(e)), device_id_type=MESH
            )

    cp_ids = []
    for i, (src, dst) in enumerate(((owner_hbm, owner_ref), (row_hbm, row_ref))):
        cp_ids.append(pltpu.make_async_copy(src, dst, loc_s.at[14 + i]))
        cp_ids[-1].start()
    cp_dout = pltpu.make_async_copy(dout_hbm, dout_ref, loc_s.at[16])
    cp_dout.start()
    cp_small = []
    for i, (src, dst) in enumerate(
        (
            (act_hbm, act_ref), (atab_hbm, atab_ref), (hist_hbm, hist_ref), (gain_hbm, gain_ref),
        )
    ):
        cp_small.append(pltpu.make_async_copy(src, dst, loc_s.at[17 + i]))
        cp_small[-1].start()
    cp_w = []
    for h in range(HEADS):
        for part in range(3):
            cp_w.append(
                pltpu.make_async_copy(
                    w_ref.at[:, pl.ds(part * HEADS * B + h * B, B)],
                    w_v.at[h, :, pl.ds(part * B, B)],
                    loc_s.at[2 + 3 * h + part],
                )
            )

    cp_slice.wait()
    tbl[0] = mslice[...].astype(BF16)
    pl.semaphore_wait(barrier, Y * CTX - 1 + 2 * LEAP)

    half_rows = (pl.ds(0, HALF), pl.ds(HALF, HALF))

    def near_send(e):
        to = SLOT_OF[-e]
        return remote(tbl.at[0], tbl.at[to], z_s.at[to], z_r.at[to], c, tab_z(e))

    def far_send(side, f):
        e = f if side == 0 else -f
        src = tbl.at[SLOT_OF[-LEAP if side == 0 else LEAP]]
        to = SLOT_OF[-LEAP - f if side == 0 else LEAP + f]
        if f < LEAP:
            return remote(src, tbl.at[to], z_s.at[to], z_r.at[to], c, tab_z(e))
        at = half_rows[side]
        return remote(
            src.at[at], tbl.at[to, at], z_s.at[15 + side], z_r.at[15 + side], c, tab_z(e)
        )

    def slot_got(to):
        if to < 15:
            got(tbl.at[to], z_r.at[to], z_s.at[to])
        else:
            for side in range(2):
                got(tbl.at[15, half_rows[side]], z_r.at[15 + side], z_s.at[15 + side])

    nearest = [e for d in range(LEAP, 0, -1) for e in (d, -d)]
    for e in nearest[:2]:
        near_send(e).start()
    for copy in cp_ids:
        copy.wait()
    owner, row = owner_ref[...], row_ref[...]
    ahead = (lax.shift_right_logical(owner, 2) + Z - z) & (Z - 1)
    slot = jnp.where(ahead > Z // 2, 2 * (Z - ahead), jnp.maximum(2 * ahead - 1, 0))
    asked = slot * ROWS + row
    owner_y = owner & (Y - 1)

    lane = lax.broadcasted_iota(I32, (B, B), 1)
    sub = lax.broadcasted_iota(I32, (B, B), 0)
    column = jnp.broadcast_to(owner_y * (Z * ROWS) + asked, (B, B)).T
    column_y = lax.shift_right_logical(column, 10)
    asked_of = (column & (Z * ROWS - 1)).astype(F32) + 1.0
    earlier = (column_y == jnp.broadcast_to(owner_y, (B, B))) & (lane < sub)
    rank = jnp.sum(jnp.where(earlier, 1.0, 0.0), axis=1, keepdims=True)
    pos = column_y * ASKED + jnp.broadcast_to(rank, (B, B)).astype(I32)
    for k in range(2):
        unpack[:, k * B : (k + 1) * B] = jnp.where(pos == lane + k * B, 1.0, 0.0).astype(BF16)
        pack[k * B : (k + 1) * B] = jnp.where(pos.T == sub + k * B, 1.0, 0.0).astype(BF16)
    number = lane - core * ASKED
    valid = (number >= 0) & (number < ASKED)
    for e in range(Y):
        mine = valid & (pos == number + ((y + Y - e) & (Y - 1)) * ASKED)
        wish = jnp.sum(jnp.where(mine, asked_of, 0.0), axis=0, keepdims=True)
        wish_out[e] = jnp.broadcast_to(wish, (8, B))

    def wish_send(e, d):
        return remote(
            wish_out.at[e], wishes.at[e, c], w_s.at[e, d], w_r.at[e, c], ctx_at(d), tab_y(-e)
        )

    for e in nearest[2:]:
        near_send(e).start()
    for e in (2, 1, 3, 0):
        for d in FAR_FIRST + ((0,) if e else ()):
            wish_send(e, d).start()
    wishes[0, c] = wish_out[0]

    def row_send(e, d):
        to = ctx_at(d)
        at = pl.ds(pl.multiple_of(lax.rem(to, 2) * ASKED, ASKED), ASKED)
        return remote(
            picked.at[e * 4 + lax.div(to, 2), at],
            x1.at[c, pl.ds(pl.multiple_of(y * ASKED, ASKED), ASKED)],
            a1_s.at[e, d], a1_r.at[e, c], to, tab_y(e),
        )

    def row_got(e, src):
        at = pl.ds(pl.multiple_of(((y + Y - e) & (Y - 1)) * ASKED, ASKED), ASKED)
        got(x1.at[src, at], a1_r.at[e, src], a1_s.at[0, 0])

    def grad_send(e, d):
        to = ctx_at(d)
        at = pl.ds(pl.multiple_of(((y + Y - e) & (Y - 1)) * ASKED, ASKED), ASKED)
        return remote(
            packed.at[to, at],
            gin.at[e * 4 + x, pl.ds(pl.multiple_of(core * ASKED, ASKED), ASKED)],
            a2_s.at[e, d], a2_r.at[e, c], to, tab_y(-e),
        )

    def grad_got(e, src):
        at = pl.ds(pl.multiple_of(lax.rem(src, 2) * ASKED, ASKED), ASKED)
        got(gin.at[e * 4 + lax.div(src, 2), at], a2_r.at[e, src], a2_s.at[0, 0])

    def gather_send(slot):
        distance = SLOTS[slot]
        copies = []
        for side in range(2) if slot == 15 else (0,) if distance > 0 else (1,):
            f = abs(distance) - LEAP
            at = half_rows[side] if slot == 15 else pl.ds(0, ROWS)
            copies.append(
                remote(
                    stage.at[slot, at], agg.at[side, f - 1, at],
                    ag_s.at[side, f - 1], ag_r.at[side, f - 1], c, tab_z(f if side == 0 else -f),
                )
            )
        return copies

    def gather_got(side, f):
        at = half_rows[side] if f == LEAP else pl.ds(0, ROWS)
        got(agg.at[side, f - 1, at], ag_r.at[side, f - 1], ag_s.at[side, f - 1])

    def target_send(slot):
        to = SLOT_OF[-SLOTS[slot]]
        return remote(
            stage.at[slot], zb.at[to - 1], rz_s.at[to - 1], rz_r.at[to - 1], c, tab_z(SLOTS[slot])
        )

    def target_got(to):
        got(zb.at[to - 1], rz_r.at[to - 1], rz_s.at[to - 1])

    holder = jnp.where(c >= SPLIT, 1, 0)

    def drain(upto=9):
        for d in range(1, CTX) if upto >= 9 else ():
            sent(fin.at[c], f_s.at[d - 1], f_r.at[d - 1])
        for e in nearest:
            near_send(e).wait_send()
        for e in range(Y):
            for d in range(CTX):
                if e or d:
                    wish_send(e, d).wait_send()
                    if upto >= 3:
                        row_send(e, d).wait_send()
                    if upto >= 7:
                        grad_send(e, d).wait_send()
        for side in range(2):
            for f in range(1, LEAP + 1):
                far_send(side, f).wait_send()
        for slot in range(1, Z) if upto >= 8 else ():
            for copy in gather_send(slot) if slot > 2 * LEAP else [target_send(slot)]:
                copy.wait_send()
        for h in range(HEADS):
            for s in range(2):
                need = (c <= SPLIT + REACH - 2) if s == 0 else (c >= SPLIT)

                @pl.when(need & (2 * h + s != c))
                def _():
                    sent(dob.at[0], do_s.at[h, s], do_r.at[0])

            if upto >= 4:
                @pl.when(2 * h + holder != c)
                def _():
                    sent(sqkv.at[h], qkv_s.at[h], qkv_r.at[0])

        for b in range(SPLIT, SPLIT + REACH - 1) if upto >= 5 else ():
            @pl.when((core == 1) & (c != b + 1))
            def _():
                sent(qf.at[b], qf_s.at[b], qf_r.at[0])

        for b in range(8) if upto >= 5 else ():
            @pl.when((c != b) & (core == (0 if b < SPLIT else 1)))
            def _():
                sent(dkvs.at[b], dkv_s.at[b], dkv_r.at[0])

            for s in range(2):
                need = b <= SPLIT + REACH - 2 if s == 0 else b >= SPLIT
                if need:
                    @pl.when((c != b) & (core == s))
                    def _():
                        sent(dqs.at[b], dq_s.at[b], dq_r.at[0, 0])
                        if upto >= 8:
                            sent(atts.at[b], at_s.at[b], at_r.at[0, 0])

    def to_heads(src_of, dst, ssem, rsem, local):
        for r in (2, 1, 3, 0):
            h = lax.rem(x + r, HEADS)
            for s in range(2):
                need = (c <= SPLIT + REACH - 2) if s == 0 else (c >= SPLIT)
                dev = 2 * h + s

                @pl.when(need & (dev != c))
                def _():
                    remote(src_of(h), dst.at[c], ssem.at[h, s], rsem.at[c], dev, t).start()

                @pl.when(need & (dev == c))
                def _():
                    local(h)

    def dout_of(h):
        return dout_ref.at[:, pl.ds(pl.multiple_of(h * B, B), B)]

    def dout_here(h):
        dob[c] = dout_ref[:, pl.ds(pl.multiple_of(h * B, B), B)]

    cp_dout.wait()
    to_heads(dout_of, dob, do_s, do_r, dout_here)
    for copy in cp_w:
        copy.start()

    slot_got(SLOT_OF[-LEAP])
    for f in range(LEAP, 0, -1):
        far_send(0, f).start()
    slot_got(SLOT_OF[LEAP])
    for f in range(LEAP, 0, -1):
        far_send(1, f).start()

    for copy in cp_small:
        copy.wait()
    actb = jnp.broadcast_to(act_ref[...], (B, B)).T
    for j in range(8):
        block = pl.ds(j * B, B)
        emb = jnp.broadcast_to(atab_ref[0:1, block], (B, B))
        for a in range(1, 8):
            emb = jnp.where(actb == a, atab_ref[a : a + 1, block], emb)
        xin[j] = emb
    h0, h1, h2, h3 = hist_ref[0, 0], hist_ref[0, 1], hist_ref[0, 2], hist_ref[0, 3]
    e0, e1, e2 = h0, h0 + h1, h0 + h1 + h2

    def spans(i, carry):
        p = lax.broadcasted_iota(I32, (B, B), 0) + i * B
        in0, in1, in2 = p < e0, p < e1, p < e2
        startb[i] = jnp.where(in0, 0, jnp.where(in1, e0, jnp.where(in2, e1, e2)))
        length = jnp.where(in0, h0, jnp.where(in1, h1, jnp.where(in2, h2, h3)))
        invb[i] = 1.0 / length.astype(F32)
        return carry

    lax.fori_loop(0, 8, spans, 0)
    for e in range(Y):
        for d in range(CTX):
            if e or d:
                src = ctx_at(CTX - d)
                got(wishes.at[e, src], w_r.at[e, src], w_s.at[0, 0])

    def spread_wish(i, carry):
        e, chip = lax.div(i, 4), lax.rem(i, 4)
        line = wishes[e, 2 * chip, 0:1, :] + wishes[e, 2 * chip + 1, 0:1, :]
        wish = jnp.broadcast_to(line, (B, B)).T.astype(I32) - 1
        at = pl.ds(8 * i, 8)
        high[at] = lax.shift_right_arithmetic(wish, 8).astype(F32).astype(BF16).reshape(8, 16, B)
        low[at] = (wish & (PLANE - 1)).astype(F32).astype(BF16).reshape(8, 16, B)
        line = jnp.broadcast_to(line, (16, B)).astype(I32) - 1
        high_row[i] = lax.shift_right_arithmetic(line, 8).astype(F32).astype(BF16)
        low_row[i] = (line & (PLANE - 1)).astype(F32).astype(BF16)
        return carry

    lax.fori_loop(0, 16, spread_wish, 0)

    one, zero, none = jnp.asarray(1, BF16), jnp.asarray(0, BF16), jnp.asarray(-1, BF16)
    lane16 = lax.broadcasted_iota(I32, (16, B), 1).astype(F32).astype(BF16)

    def pick(e, g):
        at = slice(32 * e, 32 * (e + 1))
        wanted = jnp.where(high[at] == jnp.asarray(g, BF16), low[at], none)
        hot = jnp.concatenate(
            [
                jnp.where(wanted == (lane16 + jnp.asarray(k * B, BF16))[None], one, zero)
                .reshape(4 * B, B)
                for k in range(2)
            ],
            axis=1,
        )
        rows = tbl[GROUPS * g : GROUPS * (g + 1)].reshape(PLANE, B)
        return dot(hot, rows).reshape(4, B, B)

    for g in range(GROUPS):
        for to in range(GROUPS * g, GROUPS * (g + 1)):
            if to and abs(SLOTS[to]) != LEAP:
                slot_got(to)
        for e in (2, 1, 3, 0):
            at = slice(4 * e, 4 * (e + 1))
            found = pick(e, g) if g == 0 else gacc[at] + pick(e, g)
            if g < GROUPS - 1:
                gacc[at] = found
            else:
                picked[at] = found.astype(BF16)
                for d in FAR_FIRST + ((0,) if e else ()):
                    row_send(e, d).start()
    here = pl.ds(pl.multiple_of(core * ASKED, ASKED), ASKED)
    x1[c, pl.ds(pl.multiple_of(y * ASKED, ASKED), ASKED)] = picked[x, here]
    for e in (0, 1, 3, 2):
        for d in range(CTX):
            if e or d:
                row_got(e, ctx_at(CTX - d))

    total = jnp.zeros((B, B), F32)
    for j in range(8):
        value = xin[j] + dot(unpack[...], x1[j])
        xin[j] = value
        total = total + value
    mean = jnp.sum(total, axis=1, keepdims=True) * (1.0 / MODEL)
    total = jnp.zeros((B, B), F32)
    for j in range(8):
        centre = xin[j] - mean
        total = total + centre * centre
    inv_std = lax.rsqrt(jnp.sum(total, axis=1, keepdims=True) * (1.0 / MODEL) + NORM_EPS)
    for j in range(8):
        normed = (xin[j] - mean) * inv_std
        xin[j] = normed
        hn[:, j * B : (j + 1) * B] = (normed * gain_ref[:, j * B : (j + 1) * B]).astype(BF16)
    for copy in cp_w:
        copy.wait()

    for r in (2, 1, 3, 0):
        h = lax.rem(x + r, HEADS)
        project = dot(hn[...], w_v[h])
        sig = sigmoid(project)
        pd[h] = sig * (1.0 + project * (1.0 - sig))
        active = (project * sig).astype(BF16)
        sqkv[h] = active
        dev = 2 * h + holder

        @pl.when(dev != c)
        def _():
            remote(sqkv.at[h], qkv.at[c], qkv_s.at[h], qkv_r.at[c], dev, t).start()

        @pl.when(dev == c)
        def _():
            qkv[c] = sqkv[h]

    both = (c >= SPLIT) & (c <= SPLIT + REACH - 2)

    @pl.when(both & (core == 0))
    def _():
        qf[c] = sqkv[x, :, 0:B]

    def send_back(ready, ssem, rsem, dst, block):
        @pl.when(c != block)
        def _():
            remote(ready.at[block], dst, ssem.at[block], rsem, block, t).start()

        @pl.when(c == block)
        def _():
            dst[...] = ready[block]

    def block_got(b):
        @pl.when(c != b)
        def _():
            got(qkv.at[b], qkv_r.at[b], qkv_s.at[0])
            got(dob.at[b], do_r.at[b], do_s.at[0, 0])

    def tile(kb, low_q, end_q, queries):
        n = (end_q - low_q) * B
        queries = queries.reshape(n, B)
        cotangent = dob[low_q:end_q].reshape(n, B)
        keys = qkv[kb, :, B : 2 * B]
        values = qkv[kb, :, 2 * B : 3 * B]
        raw = dot(queries, keys, NT) * SCALE
        sig = sigmoid(raw)
        inv = invb[low_q:end_q].reshape(n, B)
        k_pos = lax.broadcasted_iota(I32, (n, B), 1) + kb * B
        q_pos = lax.broadcasted_iota(I32, (n, B), 0) + low_q * B
        allowed = (k_pos >= startb[low_q:end_q].reshape(n, B)) & (k_pos <= q_pos)
        weights = jnp.where(allowed, raw * sig * inv, 0.0).astype(BF16)
        grad_w = dot(cotangent, values, NT)
        slope = sig * (1.0 + raw * (1.0 - sig))
        grad_raw = jnp.where(allowed, grad_w * slope * (inv * SCALE), 0.0).astype(BF16)
        dkv = jnp.concatenate([dot(grad_raw, queries, TN), dot(weights, cotangent, TN)], axis=1)
        return dkv, dot(grad_raw, keys), dot(weights, values)

    def keep(s, kb, low_q, end_q, dq, at):
        lowest, highest = (0, SPLIT - 1) if s == 0 else (SPLIT, 7)
        for b in range(low_q, end_q):
            rows = slice((b - low_q) * B, (b - low_q + 1) * B)
            first = kb == max(b - REACH + 1, lowest)
            dq_b = dq[rows] if first else dqacc[b] + dq[rows]
            at_b = at[rows] if first else attacc[b] + at[rows]
            if kb == min(b, highest):
                dqs[b] = dq_b.astype(BF16)
                send_back(dqs, dq_s, dq_r.at[s, x], rdq.at[s, x], b)
                atts[b] = at_b.astype(BF16)
            else:
                dqacc[b] = dq_b
                attacc[b] = at_b

    def dkv_back(kb, dkv):
        dkvs[kb] = dkv.astype(BF16)
        send_back(dkvs, dkv_s, dkv_r.at[x], rdkv.at[x], kb)

    def hand_on(b):
        return remote(
            qkv.at[b, :, pl.ds(0, B)], qf.at[b], qf_s.at[b], qf_r.at[b], 2 * x, t
        )

    shared = range(SPLIT, SPLIT + REACH - 1)

    @pl.when(core == 0)
    def _():
        for b in range(SPLIT):
            block_got(b)
        for kb in range(SPLIT):
            dkv, dq, at = tile(kb, kb, SPLIT, qkv[kb:SPLIT, :, 0:B])
            dkvacc[kb] = dkv
            keep(0, kb, kb, SPLIT, dq, at)
        for b in shared:
            @pl.when(c != b)
            def _():
                got(qf.at[b], qf_r.at[b], qf_s.at[0])
                got(dob.at[b], do_r.at[b], do_s.at[0, 0])

        for kb in range(SPLIT):
            dkv, dq, at = tile(kb, SPLIT, kb + REACH, qf[SPLIT : kb + REACH])
            dkv_back(kb, dkvacc[kb] + dkv)
            keep(0, kb, SPLIT, kb + REACH, dq, at)

    @pl.when(core == 1)
    def _():
        for b in shared:
            block_got(b)

            @pl.when(c != b + 1)
            def _():
                hand_on(b).start()

        for b in range(SPLIT + REACH - 1, 8):
            block_got(b)
        for kb in range(SPLIT, 8):
            end = min(kb + REACH, 8)
            dkv, dq, at = tile(kb, kb, end, qkv[kb:end, :, 0:B])
            dkv_back(kb, dkv)
            keep(1, kb, kb, end, dq, at)

    for r in (0, 1, 3, 2):
        h = lax.rem(x + r, HEADS)

        @pl.when(2 * h + holder != c)
        def _():
            got(rdkv.at[h], dkv_r.at[h], dkv_s.at[0])
            got(rdq.at[holder, h], dq_r.at[holder, h], dq_s.at[0])

        @pl.when(both & (2 * h != c))
        def _():
            got(rdq.at[0, h], dq_r.at[0, h], dq_s.at[0])

        dqf[...] = rdq[holder, h].astype(F32)

        @pl.when(both)
        def _():
            dqf[...] = dqf[...] + rdq[0, h].astype(F32)

        slope = pd[h]
        grad_project = jnp.concatenate(
            [
                (dqf[...] * slope[:, 0:B]).astype(BF16),
                (rdkv[h].astype(F32) * slope[:, B : 3 * B]).astype(BF16),
            ],
            axis=1,
        )
        part = dot(grad_project, w_v[h], NT)
        gh[...] = part if r == 0 else gh[...] + part

    total = jnp.zeros((B, B), F32)
    cross = jnp.zeros((B, B), F32)
    for j in range(8):
        cols = slice(j * B, (j + 1) * B)
        g = gh[:, cols] * gain_ref[:, cols]
        gh[:, cols] = g
        total = total + g
        cross = cross + g * xin[j]
    mean_g = jnp.sum(total, axis=1, keepdims=True) * (1.0 / MODEL)
    mean_c = jnp.sum(cross, axis=1, keepdims=True) * (1.0 / MODEL)
    for j in range(8):
        g = gh[:, j * B : (j + 1) * B]
        g2[j] = (inv_std * (g - mean_g - xin[j] * mean_c)).astype(BF16)

    for d in FAR_FIRST + (0,):
        to = ctx_at(d)
        packed[to] = dot(pack[...], g2[to]).astype(BF16)
        for e in (2, 1, 3, 0):
            if e or d:
                grad_send(e, d).start()
    gin[x, here] = packed[c, pl.ds(pl.multiple_of(y * ASKED, ASKED), ASKED)]
    for e in (0, 1, 3, 2):
        for d in range(CTX):
            if e or d:
                grad_got(e, ctx_at(CTX - d))

    sub16 = lax.broadcasted_iota(I32, (PLANE, B), 0).astype(F32).astype(BF16).reshape(16, 16, B)

    for g in (3, 2, 1, 0):
        wanted = jnp.where(high_row[...] == jnp.asarray(g, BF16), low_row[...], none)
        hot = jnp.concatenate(
            [jnp.where(sub16 == wanted[j][None], one, zero).reshape(PLANE, B) for j in range(16)],
            axis=1,
        )
        value = dot(hot, gin[...].reshape(16 * B, B))
        own[g] = value
        for i in range(GROUPS):
            slot = GROUPS * g + i
            if slot and abs(SLOTS[slot]) != LEAP:
                stage[slot] = value[i * ROWS : (i + 1) * ROWS].astype(BF16)
                for copy in gather_send(slot) if slot > 2 * LEAP else ():
                    copy.start()

    for s in range(2):
        @pl.when(core == s)
        def _():
            for b in range(0, SPLIT + REACH - 1) if s == 0 else range(SPLIT, 8):
                send_back(atts, at_s, at_r.at[s, x], ratt.at[s, x], b)

    for side in range(2):
        gather_got(side, 1)
    for slot in range(2 * (LEAP - 1), 0, -1):
        target_send(slot).start()
    for side in range(2):
        slot = SLOT_OF[LEAP if side == 0 else -LEAP]
        i = slot % GROUPS
        total = own[slot // GROUPS, i * ROWS : (i + 1) * ROWS, :]
        for f in range(1, LEAP):
            if f > 1:
                gather_got(side, f)
            total = total + agg[side, f - 1].astype(F32)
        gather_got(side, LEAP)
        stage[slot] = total.astype(BF16)
        at = slice(side * HALF, (side + 1) * HALF)
        stage[slot, at, :] = (total[at] + agg[side, LEAP - 1, at, :].astype(F32)).astype(BF16)
        target_send(slot).start()

    for h in range(HEADS):
        @pl.when(2 * h + holder != c)
        def _():
            got(ratt.at[holder, h], at_r.at[holder, h], at_s.at[0])

        @pl.when(both & (2 * h != c))
        def _():
            got(ratt.at[0, h], at_r.at[0, h], at_s.at[0])

        dqf[...] = ratt[holder, h].astype(F32)

        @pl.when(both)
        def _():
            dqf[...] = dqf[...] + ratt[0, h].astype(F32)

        att_out[:, h * B : (h + 1) * B] = dqf[...].astype(BF16)

    value = own[0, 0:ROWS, :]
    for to in range(1, 2 * LEAP + 1):
        target_got(to)
        value = value + zb[to - 1].astype(F32)

    fin[c] = value.astype(BF16)
    for d in FAR_FIRST:
        remote(fin.at[c], fin.at[c], f_s.at[d - 1], f_r.at[d - 1], ctx_at(d), t).start()
    for d in range(1, CTX):
        src = ctx_at(CTX - d)
        got(fin.at[src], f_r.at[d - 1], f_s.at[d - 1])

    grad_out[...] = fin[...]
    drain()


def adagrad(grad, att, rows, accum, att_out, rg_out, nm_out, na_out):
    att_out[...] = att[...]
    total = jnp.zeros((ROWS, B), F32)
    for j in range(8):
        g = grad[j].astype(F32)
        rg_out[:, j * B : (j + 1) * B] = g
        total = total + g * g
    diagonal = lax.broadcasted_iota(I32, (ROWS, ROWS), 0) == lax.broadcasted_iota(
        I32, (ROWS, ROWS), 1
    )
    before = jnp.sum(jnp.where(diagonal, accum[...], 0.0), axis=1, keepdims=True)
    after = before + jnp.sum(total, axis=1, keepdims=True) * (1.0 / MODEL)
    rate = LEARN_RATE * lax.rsqrt(after)
    for j in range(8):
        cols = slice(j * B, (j + 1) * B)
        nm_out[:, cols] = rows[:, cols] - grad[j].astype(F32) * rate
    na_out[...] = jnp.sum(jnp.where(diagonal, after, 0.0), axis=0, keepdims=True)


def per_device(
    item_owner, item_row, action_id, history_len, masters, row_accum, action_table, norm_gain,
    w_qkv, d_attended,
):
    vmem = pl.BlockSpec(memory_space=pltpu.VMEM)
    hbm = pl.BlockSpec(memory_space=pltpu.HBM)
    dma = pltpu.SemaphoreType.DMA

    def block(*lead, rows=B, cols=B, dtype=BF16):
        return pltpu.VMEM((*lead, rows, cols), dtype)

    scratch = [
        pltpu.VMEM((1, B), I32),
        pltpu.VMEM((1, B), I32),
        pltpu.VMEM((1, B), I32),
        pltpu.SMEM((1, 4), I32),
        pltpu.VMEM((8, MODEL), F32),
        pltpu.VMEM((1, MODEL), F32),
        pltpu.VMEM((B, HEADS * B), BF16),
        pltpu.VMEM((ROWS, B), F32),
        pltpu.VMEM((HEADS, MODEL, 3 * B), BF16),
        block(Z, rows=ROWS),
        block(128, rows=16),
        block(128, rows=16),
        block(16, rows=16),
        block(16, rows=16),
        block(cols=2 * B),
        block(rows=2 * B),
        block(Y, rows=8, dtype=F32),
        block(Y, CTX, rows=8, dtype=F32),
        block(16, dtype=F32),
        block(16),
        block(8, rows=Y * ASKED),
        block(8, dtype=F32),
        block(cols=MODEL),
        block(8, dtype=I32),
        block(8, dtype=F32),
        block(HEADS, cols=3 * B, dtype=F32),
        block(HEADS, cols=3 * B),
        block(8, cols=3 * B),
        block(8),
        block(8),
        block(SPLIT, cols=2 * B, dtype=F32),
        block(8, dtype=F32),
        block(8, dtype=F32),
        block(8),
        block(8, cols=2 * B),
        block(8),
        block(2, HEADS),
        block(HEADS, cols=2 * B),
        block(2, HEADS),
        block(dtype=F32),
        block(cols=MODEL, dtype=F32),
        block(8),
        block(8, rows=Y * ASKED),
        block(16),
        block(GROUPS, rows=PLANE, dtype=F32),
        block(Z, rows=ROWS),
        block(2, LEAP, rows=ROWS),
        block(2 * LEAP, rows=ROWS),
        block(8, rows=ROWS),
        dma((22,)),
        dma((Y, CTX)), dma((Y, CTX)),
        dma((Z + 1,)), dma((Z + 1,)),
        dma((Y, CTX)), dma((Y, CTX)),
        dma((HEADS,)), dma((8,)),
        dma((8,)), dma((8,)),
        dma((HEADS, 2)), dma((8,)),
        dma((8,)), dma((2, HEADS)),
        dma((8,)), dma((HEADS,)),
        dma((8,)), dma((2, HEADS)),
        dma((Y, CTX)), dma((Y, CTX)),
        dma((2, LEAP)), dma((2, LEAP)),
        dma((2 * LEAP,)), dma((2 * LEAP,)),
        dma((7,)), dma((7,)),
    ]
    attended, grads = pl.pallas_call(
        kernel,
        out_shape=(
            jax.ShapeDtypeStruct((B, HEADS * B), BF16),
            jax.ShapeDtypeStruct((8, ROWS, B), BF16),
        ),
        in_specs=[hbm] * 9,
        out_specs=(vmem, vmem),
        scratch_shapes=scratch,
        compiler_params=pltpu.CompilerParams(
            collective_id=0, has_side_effects=True, vmem_limit_bytes=VMEM_BYTES
        ),
    )(
        item_owner[:, :, 0], item_row, action_id, history_len, masters, action_table,
        norm_gain[None, :], w_qkv, d_attended[0],
    )
    attended, row_grads, new_masters, new_accum = pl.pallas_call(
        adagrad,
        out_shape=(
            jax.ShapeDtypeStruct((B, HEADS * B), BF16),
            jax.ShapeDtypeStruct((ROWS, MODEL), F32),
            jax.ShapeDtypeStruct((ROWS, MODEL), F32),
            jax.ShapeDtypeStruct((1, ROWS), F32),
        ),
        in_specs=[vmem] * 4,
        out_specs=(vmem, vmem, vmem, vmem),
        compiler_params=pltpu.CompilerParams(vmem_limit_bytes=VMEM_BYTES),
    )(grads, attended, masters, row_accum[None, :])
    return (attended[None], row_grads, new_masters, new_accum[0])


def solution(mesh):
    in_specs = (
        P("tab", "ctx", None),
        P("tab", "ctx"),
        P("tab", "ctx"),
        P("tab", None),
        P("tab", None),
        P("tab"),
        P(),
        P(),
        P(),
        P("tab", "ctx", None),
    )
    out_specs = (P("tab", "ctx", None), P("tab", None), P("tab", None), P("tab"))
    return jax.shard_map(
        per_device, mesh=mesh, in_specs=in_specs, out_specs=out_specs, check_vma=False
    )
```

```python
import math

import jax
import jax.numpy as jnp
from jax import lax
from jax.experimental import pallas as pl
from jax.experimental.pallas import tpu as pltpu
from jax.sharding import PartitionSpec as P

MESH = pl.DeviceIdType.MESH
F32 = jnp.float32
BF16 = jnp.bfloat16
I32 = jnp.int32

NORM_EPS = 1e-05
LEARN_RATE = 0.1

CTX = 8
Y = 4
B = 128
ROWS = 64
PLANE = Y * ROWS
MODEL = 1024
HEADS = 4
Z = 16
GROUPS = 4
SLOTS = (0, 1, -1, 2, -2, 3, -3, 4, -4, 5, -5, 6, -6, 7, -7, 8)
SLOT_OF = {distance: slot for slot, distance in enumerate(SLOTS)} | {-8: 15}
LEAP = 4
HALF = ROWS // 2
ASKED = 64
VMEM_BYTES = 63 * 1024 * 1024
SPLIT = 3
REACH = 5
SCALE = 1.0 / math.sqrt(B)
FAR_FIRST = (4, 3, 5, 2, 6, 1, 7)

NT = (((1,), (1,)), ((), ()))
TN = (((0,), (0,)), ((), ()))


def sigmoid(value):
    return 0.5 * jnp.tanh(0.5 * value) + 0.5


def dot(a, b, dims=(((1,), (0,)), ((), ()))):
    return lax.dot_general(a, b, dims, preferred_element_type=F32)


def kernel(
    owner_hbm, row_hbm, act_hbm, hist_hbm, masters_ref, atab_hbm, gain_hbm, w_ref,
    dout_hbm,
    att_out, grad_out,
    owner_ref, row_ref, act_ref, hist_ref, atab_ref, gain_ref, dout_ref,
    mslice, w_v, tbl, high, low, high_row, low_row, unpack, pack, wish_out, wishes,
    gacc, picked, x1, xin, hn, startb, invb,
    pd, sqkv, qkv, qf, dob, dkvacc, attacc, dqacc, dqs, dkvs, atts, rdq, rdkv, ratt, dqf, gh,
    g2, packed, gin, own, stage, agg, zb, fin,
    loc_s, w_s, w_r, z_s, z_r, a1_s, a1_r, qkv_s, qkv_r, qf_s, qf_r, do_s, do_r,
    dq_s, dq_r, dkv_s, dkv_r, at_s, at_r, a2_s, a2_r, ag_s, ag_r, rz_s, rz_r, f_s, f_r,
):
    c = lax.axis_index("ctx")
    t = lax.axis_index("tab")
    x, core = lax.div(c, 2), lax.rem(c, 2)
    z, y = lax.div(t, Y), lax.rem(t, Y)

    def ctx_at(d):
        return lax.rem(c + d, CTX)

    def tab_y(d):
        return z * Y + lax.rem(y + d + Y, Y)

    def z_at(d):
        return lax.rem(z + d + Z, Z)

    def tab_z(d):
        return z_at(d) * Y + y

    def remote(src, dst, ssem, rsem, to_ctx, to_tab):
        return pltpu.make_async_remote_copy(
            src_ref=src, dst_ref=dst, send_sem=ssem, recv_sem=rsem,
            device_id=(to_ctx, to_tab), device_id_type=MESH,
        )

    def got(dst, rsem, ssem):
        remote(dst, dst, ssem, rsem, c, t).wait_recv()

    def sent(src, ssem, rsem):
        remote(src, src, ssem, rsem, c, t).wait_send()

    cp_slice = pltpu.make_async_copy(
        masters_ref.at[:, pl.ds(pl.multiple_of(c * B, B), B)], mslice, loc_s.at[0]
    )
    cp_slice.start()

    barrier = pltpu.get_barrier_semaphore()
    for d in range(LEAP, 0, -1):
        for e in (d, -d):
            pl.semaphore_signal(barrier, inc=1, device_id=(c, tab_z(e)), device_id_type=MESH)
    for e in (2, 1, 3, 0):
        for d in FAR_FIRST + ((0,) if e else ()):
            pl.semaphore_signal(
                barrier, inc=1, device_id=(ctx_at(d), tab_y(e)), device_id_type=MESH
            )

    cp_ids = []
    for i, (src, dst) in enumerate(((owner_hbm, owner_ref), (row_hbm, row_ref))):
        cp_ids.append(pltpu.make_async_copy(src, dst, loc_s.at[14 + i]))
        cp_ids[-1].start()
    cp_dout = pltpu.make_async_copy(dout_hbm, dout_ref, loc_s.at[16])
    cp_dout.start()
    cp_small = []
    for i, (src, dst) in enumerate(
        (
            (act_hbm, act_ref), (atab_hbm, atab_ref), (hist_hbm, hist_ref), (gain_hbm, gain_ref),
        )
    ):
        cp_small.append(pltpu.make_async_copy(src, dst, loc_s.at[17 + i]))
        cp_small[-1].start()
    cp_w = []
    for h in range(HEADS):
        for part in range(3):
            cp_w.append(
                pltpu.make_async_copy(
                    w_ref.at[:, pl.ds(part * HEADS * B + h * B, B)],
                    w_v.at[h, :, pl.ds(part * B, B)],
                    loc_s.at[2 + 3 * h + part],
                )
            )

    cp_slice.wait()
    tbl[0] = mslice[...].astype(BF16)
    pl.semaphore_wait(barrier, Y * CTX - 1 + 2 * LEAP)

    half_rows = (pl.ds(0, HALF), pl.ds(HALF, HALF))

    def near_send(e):
        to = SLOT_OF[-e]
        return remote(tbl.at[0], tbl.at[to], z_s.at[to], z_r.at[to], c, tab_z(e))

    def far_send(side, f):
        e = f if side == 0 else -f
        src = tbl.at[SLOT_OF[-LEAP if side == 0 else LEAP]]
        to = SLOT_OF[-LEAP - f if side == 0 else LEAP + f]
        if f < LEAP:
            return remote(src, tbl.at[to], z_s.at[to], z_r.at[to], c, tab_z(e))
        at = half_rows[side]
        return remote(
            src.at[at], tbl.at[to, at], z_s.at[15 + side], z_r.at[15 + side], c, tab_z(e)
        )

    def slot_got(to):
        if to < 15:
            got(tbl.at[to], z_r.at[to], z_s.at[to])
        else:
            for side in range(2):
                got(tbl.at[15, half_rows[side]], z_r.at[15 + side], z_s.at[15 + side])

    nearest = [e for d in range(LEAP, 0, -1) for e in (d, -d)]
    for e in nearest[:2]:
        near_send(e).start()
    for copy in cp_ids:
        copy.wait()
    owner, row = owner_ref[...], row_ref[...]
    ahead = (lax.shift_right_logical(owner, 2) + Z - z) & (Z - 1)
    slot = jnp.where(ahead > Z // 2, 2 * (Z - ahead), jnp.maximum(2 * ahead - 1, 0))
    asked = slot * ROWS + row
    owner_y = owner & (Y - 1)

    lane = lax.broadcasted_iota(I32, (B, B), 1)
    sub = lax.broadcasted_iota(I32, (B, B), 0)
    column = jnp.broadcast_to(owner_y * (Z * ROWS) + asked, (B, B)).T
    column_y = lax.shift_right_logical(column, 10)
    asked_of = (column & (Z * ROWS - 1)).astype(F32) + 1.0
    earlier = (column_y == jnp.broadcast_to(owner_y, (B, B))) & (lane < sub)
    rank = jnp.sum(jnp.where(earlier, 1.0, 0.0), axis=1, keepdims=True)
    pos = column_y * ASKED + jnp.broadcast_to(rank, (B, B)).astype(I32)
    for k in range(2):
        unpack[:, k * B : (k + 1) * B] = jnp.where(pos == lane + k * B, 1.0, 0.0).astype(BF16)
        pack[k * B : (k + 1) * B] = jnp.where(pos.T == sub + k * B, 1.0, 0.0).astype(BF16)
    number = lane - core * ASKED
    valid = (number >= 0) & (number < ASKED)
    for e in range(Y):
        mine = valid & (pos == number + ((y + Y - e) & (Y - 1)) * ASKED)
        wish = jnp.sum(jnp.where(mine, asked_of, 0.0), axis=0, keepdims=True)
        wish_out[e] = jnp.broadcast_to(wish, (8, B))

    def wish_send(e, d):
        return remote(
            wish_out.at[e], wishes.at[e, c], w_s.at[e, d], w_r.at[e, c], ctx_at(d), tab_y(-e)
        )

    for e in nearest[2:]:
        near_send(e).start()
    for e in (2, 1, 3, 0):
        for d in FAR_FIRST + ((0,) if e else ()):
            wish_send(e, d).start()
    wishes[0, c] = wish_out[0]

    def row_send(e, d):
        to = ctx_at(d)
        at = pl.ds(pl.multiple_of(lax.rem(to, 2) * ASKED, ASKED), ASKED)
        return remote(
            picked.at[e * 4 + lax.div(to, 2), at],
            x1.at[c, pl.ds(pl.multiple_of(y * ASKED, ASKED), ASKED)],
            a1_s.at[e, d], a1_r.at[e, c], to, tab_y(e),
        )

    def row_got(e, src):
        at = pl.ds(pl.multiple_of(((y + Y - e) & (Y - 1)) * ASKED, ASKED), ASKED)
        got(x1.at[src, at], a1_r.at[e, src], a1_s.at[0, 0])

    def grad_send(e, d):
        to = ctx_at(d)
        at = pl.ds(pl.multiple_of(((y + Y - e) & (Y - 1)) * ASKED, ASKED), ASKED)
        return remote(
            packed.at[to, at],
            gin.at[e * 4 + x, pl.ds(pl.multiple_of(core * ASKED, ASKED), ASKED)],
            a2_s.at[e, d], a2_r.at[e, c], to, tab_y(-e),
        )

    def grad_got(e, src):
        at = pl.ds(pl.multiple_of(lax.rem(src, 2) * ASKED, ASKED), ASKED)
        got(gin.at[e * 4 + lax.div(src, 2), at], a2_r.at[e, src], a2_s.at[0, 0])

    def gather_send(slot):
        distance = SLOTS[slot]
        copies = []
        for side in range(2) if slot == 15 else (0,) if distance > 0 else (1,):
            f = abs(distance) - LEAP
            at = half_rows[side] if slot == 15 else pl.ds(0, ROWS)
            copies.append(
                remote(
                    stage.at[slot, at], agg.at[side, f - 1, at],
                    ag_s.at[side, f - 1], ag_r.at[side, f - 1], c, tab_z(f if side == 0 else -f),
                )
            )
        return copies

    def gather_got(side, f):
        at = half_rows[side] if f == LEAP else pl.ds(0, ROWS)
        got(agg.at[side, f - 1, at], ag_r.at[side, f - 1], ag_s.at[side, f - 1])

    def target_send(slot):
        to = SLOT_OF[-SLOTS[slot]]
        return remote(
            stage.at[slot], zb.at[to - 1], rz_s.at[to - 1], rz_r.at[to - 1], c, tab_z(SLOTS[slot])
        )

    def target_got(to):
        got(zb.at[to - 1], rz_r.at[to - 1], rz_s.at[to - 1])

    holder = jnp.where(c >= SPLIT, 1, 0)

    def drain(upto=9):
        for d in range(1, CTX) if upto >= 9 else ():
            sent(fin.at[c], f_s.at[d - 1], f_r.at[d - 1])
        for e in nearest:
            near_send(e).wait_send()
        for e in range(Y):
            for d in range(CTX):
                if e or d:
                    wish_send(e, d).wait_send()
                    if upto >= 3:
                        row_send(e, d).wait_send()
                    if upto >= 7:
                        grad_send(e, d).wait_send()
        for side in range(2):
            for f in range(1, LEAP + 1):
                far_send(side, f).wait_send()
        for slot in range(1, Z) if upto >= 8 else ():
            for copy in gather_send(slot) if slot > 2 * LEAP else [target_send(slot)]:
                copy.wait_send()
        for h in range(HEADS):
            for s in range(2):
                need = (c <= SPLIT + REACH - 2) if s == 0 else (c >= SPLIT)

                @pl.when(need & (2 * h + s != c))
                def _():
                    sent(dob.at[0], do_s.at[h, s], do_r.at[0])

            if upto >= 4:
                @pl.when(2 * h + holder != c)
                def _():
                    sent(sqkv.at[h], qkv_s.at[h], qkv_r.at[0])

        for b in range(SPLIT, SPLIT + REACH - 1) if upto >= 5 else ():
            @pl.when((core == 1) & (c != b + 1))
            def _():
                sent(qf.at[b], qf_s.at[b], qf_r.at[0])

        for b in range(8) if upto >= 5 else ():
            @pl.when((c != b) & (core == (0 if b < SPLIT else 1)))
            def _():
                sent(dkvs.at[b], dkv_s.at[b], dkv_r.at[0])

            for s in range(2):
                need = b <= SPLIT + REACH - 2 if s == 0 else b >= SPLIT
                if need:
                    @pl.when((c != b) & (core == s))
                    def _():
                        sent(dqs.at[b], dq_s.at[b], dq_r.at[0, 0])
                        if upto >= 8:
                            sent(atts.at[b], at_s.at[b], at_r.at[0, 0])

    def to_heads(src_of, dst, ssem, rsem, local):
        for r in (2, 1, 3, 0):
            h = lax.rem(x + r, HEADS)
            for s in range(2):
                need = (c <= SPLIT + REACH - 2) if s == 0 else (c >= SPLIT)
                dev = 2 * h + s

                @pl.when(need & (dev != c))
                def _():
                    remote(src_of(h), dst.at[c], ssem.at[h, s], rsem.at[c], dev, t).start()

                @pl.when(need & (dev == c))
                def _():
                    local(h)

    def dout_of(h):
        return dout_ref.at[:, pl.ds(pl.multiple_of(h * B, B), B)]

    def dout_here(h):
        dob[c] = dout_ref[:, pl.ds(pl.multiple_of(h * B, B), B)]

    cp_dout.wait()
    to_heads(dout_of, dob, do_s, do_r, dout_here)
    for copy in cp_w:
        copy.start()

    slot_got(SLOT_OF[-LEAP])
    for f in range(LEAP, 0, -1):
        far_send(0, f).start()
    slot_got(SLOT_OF[LEAP])
    for f in range(LEAP, 0, -1):
        far_send(1, f).start()

    for copy in cp_small:
        copy.wait()
    actb = jnp.broadcast_to(act_ref[...], (B, B)).T
    for j in range(8):
        block = pl.ds(j * B, B)
        emb = jnp.broadcast_to(atab_ref[0:1, block], (B, B))
        for a in range(1, 8):
            emb = jnp.where(actb == a, atab_ref[a : a + 1, block], emb)
        xin[j] = emb
    h0, h1, h2, h3 = hist_ref[0, 0], hist_ref[0, 1], hist_ref[0, 2], hist_ref[0, 3]
    e0, e1, e2 = h0, h0 + h1, h0 + h1 + h2

    def spans(i, carry):
        p = lax.broadcasted_iota(I32, (B, B), 0) + i * B
        in0, in1, in2 = p < e0, p < e1, p < e2
        startb[i] = jnp.where(in0, 0, jnp.where(in1, e0, jnp.where(in2, e1, e2)))
        length = jnp.where(in0, h0, jnp.where(in1, h1, jnp.where(in2, h2, h3)))
        invb[i] = 1.0 / length.astype(F32)
        return carry

    lax.fori_loop(0, 8, spans, 0)
    for e in range(Y):
        for d in range(CTX):
            if e or d:
                src = ctx_at(CTX - d)
                got(wishes.at[e, src], w_r.at[e, src], w_s.at[0, 0])

    def spread_wish(i, carry):
        e, chip = lax.div(i, 4), lax.rem(i, 4)
        line = wishes[e, 2 * chip, 0:1, :] + wishes[e, 2 * chip + 1, 0:1, :]
        wish = jnp.broadcast_to(line, (B, B)).T.astype(I32) - 1
        at = pl.ds(8 * i, 8)
        high[at] = lax.shift_right_arithmetic(wish, 8).astype(F32).astype(BF16).reshape(8, 16, B)
        low[at] = (wish & (PLANE - 1)).astype(F32).astype(BF16).reshape(8, 16, B)
        line = jnp.broadcast_to(line, (16, B)).astype(I32) - 1
        high_row[i] = lax.shift_right_arithmetic(line, 8).astype(F32).astype(BF16)
        low_row[i] = (line & (PLANE - 1)).astype(F32).astype(BF16)
        return carry

    lax.fori_loop(0, 16, spread_wish, 0)

    one, zero, none = jnp.asarray(1, BF16), jnp.asarray(0, BF16), jnp.asarray(-1, BF16)
    lane16 = lax.broadcasted_iota(I32, (16, B), 1).astype(F32).astype(BF16)

    def pick(e, g):
        at = slice(32 * e, 32 * (e + 1))
        wanted = jnp.where(high[at] == jnp.asarray(g, BF16), low[at], none)
        hot = jnp.concatenate(
            [
                jnp.where(wanted == (lane16 + jnp.asarray(k * B, BF16))[None], one, zero)
                .reshape(4 * B, B)
                for k in range(2)
            ],
            axis=1,
        )
        rows = tbl[GROUPS * g : GROUPS * (g + 1)].reshape(PLANE, B)
        return dot(hot, rows).reshape(4, B, B)

    for g in range(GROUPS):
        for to in range(GROUPS * g, GROUPS * (g + 1)):
            if to and abs(SLOTS[to]) != LEAP:
                slot_got(to)
        for e in (2, 1, 3, 0):
            at = slice(4 * e, 4 * (e + 1))
            found = pick(e, g) if g == 0 else gacc[at] + pick(e, g)
            if g < GROUPS - 1:
                gacc[at] = found
            else:
                picked[at] = found.astype(BF16)
                for d in FAR_FIRST + ((0,) if e else ()):
                    row_send(e, d).start()
    here = pl.ds(pl.multiple_of(core * ASKED, ASKED), ASKED)
    x1[c, pl.ds(pl.multiple_of(y * ASKED, ASKED), ASKED)] = picked[x, here]
    for e in (0, 1, 3, 2):
        for d in range(CTX):
            if e or d:
                row_got(e, ctx_at(CTX - d))

    total = jnp.zeros((B, B), F32)
    for j in range(8):
        value = xin[j] + dot(unpack[...], x1[j])
        xin[j] = value
        total = total + value
    mean = jnp.sum(total, axis=1, keepdims=True) * (1.0 / MODEL)
    total = jnp.zeros((B, B), F32)
    for j in range(8):
        centre = xin[j] - mean
        total = total + centre * centre
    inv_std = lax.rsqrt(jnp.sum(total, axis=1, keepdims=True) * (1.0 / MODEL) + NORM_EPS)
    for j in range(8):
        normed = (xin[j] - mean) * inv_std
        xin[j] = normed
        hn[:, j * B : (j + 1) * B] = (normed * gain_ref[:, j * B : (j + 1) * B]).astype(BF16)
    for copy in cp_w:
        copy.wait()

    for r in (2, 1, 3, 0):
        h = lax.rem(x + r, HEADS)
        project = dot(hn[...], w_v[h])
        sig = sigmoid(project)
        pd[h] = sig * (1.0 + project * (1.0 - sig))
        active = (project * sig).astype(BF16)
        sqkv[h] = active
        dev = 2 * h + holder

        @pl.when(dev != c)
        def _():
            remote(sqkv.at[h], qkv.at[c], qkv_s.at[h], qkv_r.at[c], dev, t).start()

        @pl.when(dev == c)
        def _():
            qkv[c] = sqkv[h]

    both = (c >= SPLIT) & (c <= SPLIT + REACH - 2)

    @pl.when(both & (core == 0))
    def _():
        qf[c] = sqkv[x, :, 0:B]

    def send_back(ready, ssem, rsem, dst, block):
        @pl.when(c != block)
        def _():
            remote(ready.at[block], dst, ssem.at[block], rsem, block, t).start()

        @pl.when(c == block)
        def _():
            dst[...] = ready[block]

    def block_got(b):
        @pl.when(c != b)
        def _():
            got(qkv.at[b], qkv_r.at[b], qkv_s.at[0])
            got(dob.at[b], do_r.at[b], do_s.at[0, 0])

    def tile(kb, low_q, end_q, queries):
        n = (end_q - low_q) * B
        queries = queries.reshape(n, B)
        cotangent = dob[low_q:end_q].reshape(n, B)
        keys = qkv[kb, :, B : 2 * B]
        values = qkv[kb, :, 2 * B : 3 * B]
        raw = dot(queries, keys, NT) * SCALE
        sig = sigmoid(raw)
        inv = invb[low_q:end_q].reshape(n, B)
        k_pos = lax.broadcasted_iota(I32, (n, B), 1) + kb * B
        q_pos = lax.broadcasted_iota(I32, (n, B), 0) + low_q * B
        allowed = (k_pos >= startb[low_q:end_q].reshape(n, B)) & (k_pos <= q_pos)
        weights = jnp.where(allowed, raw * sig * inv, 0.0).astype(BF16)
        grad_w = dot(cotangent, values, NT)
        slope = sig * (1.0 + raw * (1.0 - sig))
        grad_raw = jnp.where(allowed, grad_w * slope * (inv * SCALE), 0.0).astype(BF16)
        dkv = jnp.concatenate([dot(grad_raw, queries, TN), dot(weights, cotangent, TN)], axis=1)
        return dkv, dot(grad_raw, keys), dot(weights, values)

    def keep(s, kb, low_q, end_q, dq, at):
        lowest, highest = (0, SPLIT - 1) if s == 0 else (SPLIT, 7)
        for b in range(low_q, end_q):
            rows = slice((b - low_q) * B, (b - low_q + 1) * B)
            first = kb == max(b - REACH + 1, lowest)
            dq_b = dq[rows] if first else dqacc[b] + dq[rows]
            at_b = at[rows] if first else attacc[b] + at[rows]
            if kb == min(b, highest):
                dqs[b] = dq_b.astype(BF16)
                send_back(dqs, dq_s, dq_r.at[s, x], rdq.at[s, x], b)
                atts[b] = at_b.astype(BF16)
            else:
                dqacc[b] = dq_b
                attacc[b] = at_b

    def dkv_back(kb, dkv):
        dkvs[kb] = dkv.astype(BF16)
        send_back(dkvs, dkv_s, dkv_r.at[x], rdkv.at[x], kb)

    def hand_on(b):
        return remote(
            qkv.at[b, :, pl.ds(0, B)], qf.at[b], qf_s.at[b], qf_r.at[b], 2 * x, t
        )

    shared = range(SPLIT, SPLIT + REACH - 1)

    @pl.when(core == 0)
    def _():
        for b in range(SPLIT):
            block_got(b)
        for kb in range(SPLIT):
            dkv, dq, at = tile(kb, kb, SPLIT, qkv[kb:SPLIT, :, 0:B])
            dkvacc[kb] = dkv
            keep(0, kb, kb, SPLIT, dq, at)
        for b in shared:
            @pl.when(c != b)
            def _():
                got(qf.at[b], qf_r.at[b], qf_s.at[0])
                got(dob.at[b], do_r.at[b], do_s.at[0, 0])

        for kb in range(SPLIT):
            dkv, dq, at = tile(kb, SPLIT, kb + REACH, qf[SPLIT : kb + REACH])
            dkv_back(kb, dkvacc[kb] + dkv)
            keep(0, kb, SPLIT, kb + REACH, dq, at)

    @pl.when(core == 1)
    def _():
        for b in shared:
            block_got(b)

            @pl.when(c != b + 1)
            def _():
                hand_on(b).start()

        for b in range(SPLIT + REACH - 1, 8):
            block_got(b)
        for kb in range(SPLIT, 8):
            end = min(kb + REACH, 8)
            dkv, dq, at = tile(kb, kb, end, qkv[kb:end, :, 0:B])
            dkv_back(kb, dkv)
            keep(1, kb, kb, end, dq, at)

    for r in (0, 1, 3, 2):
        h = lax.rem(x + r, HEADS)

        @pl.when(2 * h + holder != c)
        def _():
            got(rdkv.at[h], dkv_r.at[h], dkv_s.at[0])
            got(rdq.at[holder, h], dq_r.at[holder, h], dq_s.at[0])

        @pl.when(both & (2 * h != c))
        def _():
            got(rdq.at[0, h], dq_r.at[0, h], dq_s.at[0])

        dqf[...] = rdq[holder, h].astype(F32)

        @pl.when(both)
        def _():
            dqf[...] = dqf[...] + rdq[0, h].astype(F32)

        slope = pd[h]
        grad_project = jnp.concatenate(
            [
                (dqf[...] * slope[:, 0:B]).astype(BF16),
                (rdkv[h].astype(F32) * slope[:, B : 3 * B]).astype(BF16),
            ],
            axis=1,
        )
        part = dot(grad_project, w_v[h], NT)
        gh[...] = part if r == 0 else gh[...] + part

    total = jnp.zeros((B, B), F32)
    cross = jnp.zeros((B, B), F32)
    for j in range(8):
        cols = slice(j * B, (j + 1) * B)
        g = gh[:, cols] * gain_ref[:, cols]
        gh[:, cols] = g
        total = total + g
        cross = cross + g * xin[j]
    mean_g = jnp.sum(total, axis=1, keepdims=True) * (1.0 / MODEL)
    mean_c = jnp.sum(cross, axis=1, keepdims=True) * (1.0 / MODEL)
    for j in range(8):
        g = gh[:, j * B : (j + 1) * B]
        g2[j] = (inv_std * (g - mean_g - xin[j] * mean_c)).astype(BF16)

    for d in FAR_FIRST + (0,):
        to = ctx_at(d)
        packed[to] = dot(pack[...], g2[to]).astype(BF16)
        for e in (2, 1, 3, 0):
            if e or d:
                grad_send(e, d).start()
    gin[x, here] = packed[c, pl.ds(pl.multiple_of(y * ASKED, ASKED), ASKED)]
    for e in (0, 1, 3, 2):
        for d in range(CTX):
            if e or d:
                grad_got(e, ctx_at(CTX - d))

    sub16 = lax.broadcasted_iota(I32, (PLANE, B), 0).astype(F32).astype(BF16).reshape(16, 16, B)

    for g in (3, 2, 1, 0):
        wanted = jnp.where(high_row[...] == jnp.asarray(g, BF16), low_row[...], none)
        hot = jnp.concatenate(
            [jnp.where(sub16 == wanted[j][None], one, zero).reshape(PLANE, B) for j in range(16)],
            axis=1,
        )
        value = dot(hot, gin[...].reshape(16 * B, B))
        own[g] = value
        for i in range(GROUPS):
            slot = GROUPS * g + i
            if slot and abs(SLOTS[slot]) != LEAP:
                stage[slot] = value[i * ROWS : (i + 1) * ROWS].astype(BF16)
                for copy in gather_send(slot) if slot > 2 * LEAP else [target_send(slot)]:
                    copy.start()

    for side in range(2):
        slot = SLOT_OF[LEAP if side == 0 else -LEAP]
        i = slot % GROUPS
        total = own[slot // GROUPS, i * ROWS : (i + 1) * ROWS, :]
        for f in range(1, LEAP):
            gather_got(side, f)
            total = total + agg[side, f - 1].astype(F32)
        gather_got(side, LEAP)
        stage[slot] = total.astype(BF16)
        at = slice(side * HALF, (side + 1) * HALF)
        stage[slot, at, :] = (total[at] + agg[side, LEAP - 1, at, :].astype(F32)).astype(BF16)
        target_send(slot).start()

    for s in range(2):
        @pl.when(core == s)
        def _():
            for b in range(0, SPLIT + REACH - 1) if s == 0 else range(SPLIT, 8):
                send_back(atts, at_s, at_r.at[s, x], ratt.at[s, x], b)

    for h in range(HEADS):
        @pl.when(2 * h + holder != c)
        def _():
            got(ratt.at[holder, h], at_r.at[holder, h], at_s.at[0])

        @pl.when(both & (2 * h != c))
        def _():
            got(ratt.at[0, h], at_r.at[0, h], at_s.at[0])

        dqf[...] = ratt[holder, h].astype(F32)

        @pl.when(both)
        def _():
            dqf[...] = dqf[...] + ratt[0, h].astype(F32)

        att_out[:, h * B : (h + 1) * B] = dqf[...].astype(BF16)

    value = own[0, 0:ROWS, :]
    for to in range(1, 2 * LEAP + 1):
        target_got(to)
        value = value + zb[to - 1].astype(F32)

    fin[c] = value.astype(BF16)
    for d in FAR_FIRST:
        remote(fin.at[c], fin.at[c], f_s.at[d - 1], f_r.at[d - 1], ctx_at(d), t).start()
    for d in range(1, CTX):
        src = ctx_at(CTX - d)
        got(fin.at[src], f_r.at[d - 1], f_s.at[d - 1])

    grad_out[...] = fin[...]
    drain()


def adagrad(grad, att, rows, accum, att_out, rg_out, nm_out, na_out):
    att_out[...] = att[...]
    total = jnp.zeros((ROWS, B), F32)
    for j in range(8):
        g = grad[j].astype(F32)
        rg_out[:, j * B : (j + 1) * B] = g
        total = total + g * g
    diagonal = lax.broadcasted_iota(I32, (ROWS, ROWS), 0) == lax.broadcasted_iota(
        I32, (ROWS, ROWS), 1
    )
    before = jnp.sum(jnp.where(diagonal, accum[...], 0.0), axis=1, keepdims=True)
    after = before + jnp.sum(total, axis=1, keepdims=True) * (1.0 / MODEL)
    rate = LEARN_RATE * lax.rsqrt(after)
    for j in range(8):
        cols = slice(j * B, (j + 1) * B)
        nm_out[:, cols] = rows[:, cols] - grad[j].astype(F32) * rate
    na_out[...] = jnp.sum(jnp.where(diagonal, after, 0.0), axis=0, keepdims=True)


def per_device(
    item_owner, item_row, action_id, history_len, masters, row_accum, action_table, norm_gain,
    w_qkv, d_attended,
):
    vmem = pl.BlockSpec(memory_space=pltpu.VMEM)
    hbm = pl.BlockSpec(memory_space=pltpu.HBM)
    dma = pltpu.SemaphoreType.DMA

    def block(*lead, rows=B, cols=B, dtype=BF16):
        return pltpu.VMEM((*lead, rows, cols), dtype)

    scratch = [
        pltpu.VMEM((1, B), I32),
        pltpu.VMEM((1, B), I32),
        pltpu.VMEM((1, B), I32),
        pltpu.SMEM((1, 4), I32),
        pltpu.VMEM((8, MODEL), F32),
        pltpu.VMEM((1, MODEL), F32),
        pltpu.VMEM((B, HEADS * B), BF16),
        pltpu.VMEM((ROWS, B), F32),
        pltpu.VMEM((HEADS, MODEL, 3 * B), BF16),
        block(Z, rows=ROWS),
        block(128, rows=16),
        block(128, rows=16),
        block(16, rows=16),
        block(16, rows=16),
        block(cols=2 * B),
        block(rows=2 * B),
        block(Y, rows=8, dtype=F32),
        block(Y, CTX, rows=8, dtype=F32),
        block(16, dtype=F32),
        block(16),
        block(8, rows=Y * ASKED),
        block(8, dtype=F32),
        block(cols=MODEL),
        block(8, dtype=I32),
        block(8, dtype=F32),
        block(HEADS, cols=3 * B, dtype=F32),
        block(HEADS, cols=3 * B),
        block(8, cols=3 * B),
        block(8),
        block(8),
        block(SPLIT, cols=2 * B, dtype=F32),
        block(8, dtype=F32),
        block(8, dtype=F32),
        block(8),
        block(8, cols=2 * B),
        block(8),
        block(2, HEADS),
        block(HEADS, cols=2 * B),
        block(2, HEADS),
        block(dtype=F32),
        block(cols=MODEL, dtype=F32),
        block(8),
        block(8, rows=Y * ASKED),
        block(16),
        block(GROUPS, rows=PLANE, dtype=F32),
        block(Z, rows=ROWS),
        block(2, LEAP, rows=ROWS),
        block(2 * LEAP, rows=ROWS),
        block(8, rows=ROWS),
        dma((22,)),
        dma((Y, CTX)), dma((Y, CTX)),
        dma((Z + 1,)), dma((Z + 1,)),
        dma((Y, CTX)), dma((Y, CTX)),
        dma((HEADS,)), dma((8,)),
        dma((8,)), dma((8,)),
        dma((HEADS, 2)), dma((8,)),
        dma((8,)), dma((2, HEADS)),
        dma((8,)), dma((HEADS,)),
        dma((8,)), dma((2, HEADS)),
        dma((Y, CTX)), dma((Y, CTX)),
        dma((2, LEAP)), dma((2, LEAP)),
        dma((2 * LEAP,)), dma((2 * LEAP,)),
        dma((7,)), dma((7,)),
    ]
    attended, grads = pl.pallas_call(
        kernel,
        out_shape=(
            jax.ShapeDtypeStruct((B, HEADS * B), BF16),
            jax.ShapeDtypeStruct((8, ROWS, B), BF16),
        ),
        in_specs=[hbm] * 9,
        out_specs=(vmem, vmem),
        scratch_shapes=scratch,
        compiler_params=pltpu.CompilerParams(
            collective_id=0, has_side_effects=True, vmem_limit_bytes=VMEM_BYTES
        ),
    )(
        item_owner[:, :, 0], item_row, action_id, history_len, masters, action_table,
        norm_gain[None, :], w_qkv, d_attended[0],
    )
    attended, row_grads, new_masters, new_accum = pl.pallas_call(
        adagrad,
        out_shape=(
            jax.ShapeDtypeStruct((B, HEADS * B), BF16),
            jax.ShapeDtypeStruct((ROWS, MODEL), F32),
            jax.ShapeDtypeStruct((ROWS, MODEL), F32),
            jax.ShapeDtypeStruct((1, ROWS), F32),
        ),
        in_specs=[vmem] * 4,
        out_specs=(vmem, vmem, vmem, vmem),
        compiler_params=pltpu.CompilerParams(vmem_limit_bytes=VMEM_BYTES),
    )(grads, attended, masters, row_accum[None, :])
    return (attended[None], row_grads, new_masters, new_accum[0])


def solution(mesh):
    in_specs = (
        P("tab", "ctx", None),
        P("tab", "ctx"),
        P("tab", "ctx"),
        P("tab", None),
        P("tab", None),
        P("tab"),
        P(),
        P(),
        P(),
        P("tab", "ctx", None),
    )
    out_specs = (P("tab", "ctx", None), P("tab", None), P("tab", None), P("tab"))
    return jax.shard_map(
        per_device, mesh=mesh, in_specs=in_specs, out_specs=out_specs, check_vma=False
    )
```
